32 devices in a mesh: dp: 8 (over z, x), mp: 4 (over y, core).
Axes of the slice: x: 2, y: 2, z: 4, core: 2. Of those that a mesh axis runs over, the one named last changes fastest.
Arguments:
- rows: bfloat16 [16384, 768], P(('dp', 'mp')), may hold values from -6 to 6
- cotangent: bfloat16 [16384, 768], P(('dp', 'mp')), may hold values from -6 to 6
- group_ids: int32 [64], P(('dp', 'mp')), may hold values from 0 to 7, as said below
- qkv_weight: bfloat16 [3, 768, 768], P(None, None, 'mp'), may hold values from -0.21875 to 0.21875
- out_weight: bfloat16 [768, 768], P('mp'), may hold values from -1.25 to 1.25
- in_weight: bfloat16 [768, 3072], P(None, 'mp'), may hold values from -0.21875 to 0.21875
- down_weight: bfloat16 [3072, 768], P('mp'), may hold values from -0.109375 to 0.109375
- vectors: float32 [6, 768], replicated
- qkv_master: float32 [3, 768, 768], P(None, 'dp', 'mp')
- qkv_first: float32 [3, 768, 768], P(None, 'dp', 'mp'), may hold values from -384 to 384
- qkv_second: float32 [3, 768, 768], P(None, 'dp', 'mp'), may hold values from 4096 to 16384
- out_master: float32 [768, 768], P('mp', 'dp')
- out_first: float32 [768, 768], P('mp', 'dp'), may hold values from -112 to 112
- out_second: float32 [768, 768], P('mp', 'dp'), may hold values from 368.64 to 1474.56
- in_master: float32 [768, 3072], P('dp', 'mp')
- in_first: float32 [768, 3072], P('dp', 'mp'), may hold values from -224 to 224
- in_second: float32 [768, 3072], P('dp', 'mp'), may hold values from 1474.56 to 5898.24
- down_master: float32 [3072, 768], P('mp', 'dp')
- down_first: float32 [3072, 768], P('mp', 'dp'), may hold values from -448 to 448
- down_second: float32 [3072, 768], P('mp', 'dp'), may hold values from 5898.24 to 23592.96
- vec_first: float32 [6, 768], replicated, may hold values from -768 to 768
- vec_second: float32 [6, 768], replicated, may hold values from 16384 to 65536
Outputs:
- out_rows: bfloat16 [16384, 768], P(('dp', 'mp'))
- input_grad: float32 [16384, 768], P(('dp', 'mp'))
- qkv_grad: float32 [3, 768, 768], P(None, 'dp', 'mp')
- out_grad: float32 [768, 768], P('mp', 'dp')
- in_grad: float32 [768, 3072], P('dp', 'mp')
- down_grad: float32 [3072, 768], P('mp', 'dp')
- qkv_first_new: float32 [3, 768, 768], P(None, 'dp', 'mp')
- qkv_second_new: float32 [3, 768, 768], P(None, 'dp', 'mp')
- qkv_new: float32 [3, 768, 768], P(None, 'dp', 'mp')
- out_first_new: float32 [768, 768], P('mp', 'dp')
- out_second_new: float32 [768, 768], P('mp', 'dp')
- out_new: float32 [768, 768], P('mp', 'dp')
- in_first_new: float32 [768, 3072], P('dp', 'mp')
- in_second_new: float32 [768, 3072], P('dp', 'mp')
- in_new: float32 [768, 3072], P('dp', 'mp')
- down_first_new: float32 [3072, 768], P('mp', 'dp')
- down_second_new: float32 [3072, 768], P('mp', 'dp')
- down_new: float32 [3072, 768], P('mp', 'dp')
- vec_grad: float32 [6, 768], replicated
- vec_first_new: float32 [6, 768], replicated
- vec_second_new: float32 [6, 768], replicated
- vec_new: float32 [6, 768], replicated
- matrix_norms: float32 [3, 4], replicated
The draws below stay inside these ranges and needn't reach their ends.
Inputs may be any that keep to these rules, and one draw needn't show every extreme that they name: group_ids never fall from one image to the next; every group holds at least max(1, 1) images.
All inputs are finite; a program needn't handle non-finite values.
Results may differ from the reference program's by a relative error of at most 0.014.
Values may be sent and summed in bfloat16 or wider, within the bound.
No kernel may reach another device: no remote copies, remote signals or barrier semaphores. Data moves between devices by JAX's collectives and lax.ppermute only.
A program may use at most 128 MiB of HBM per device.

```python
import math
import jax
import jax.numpy as jnp
from jax import lax

D = 768
HEADS = 12
HEAD_DIM = 64
FF = 3072
PATCHES = 256
IMG_BLOCK = 4
GROUPS = 8
STEP = 5
IMAGES = 64
ROWS = 16384


def draw_group_ids(key, part):
    floor_count = max(1, IMAGES // (8 * GROUPS))
    fixed_part = jnp.arange(GROUPS * floor_count, dtype=jnp.int32) // floor_count
    extra_count = IMAGES - GROUPS * floor_count
    picks = jax.random.randint(key, (extra_count,), 0, 100)
    cutoffs = jnp.array([35, 60, 72, 80, 87, 93, 97], dtype=jnp.int32)
    extra_ids = jnp.sum((picks[:, None] >= cutoffs[None, :]).astype(jnp.int32), axis=1).astype(jnp.int32)
    return jnp.sort(jnp.concatenate([fixed_part, extra_ids])).astype(jnp.int32)


def draw_vectors(key, part):
    gain_key, shift_key = jax.random.split(key)
    gains = jax.random.uniform(gain_key, (2, D), jnp.float32, 0.5, 1.5)
    shifts = 0.3 * jax.random.normal(shift_key, (4, D), jnp.float32)
    return jnp.stack([gains[0], shifts[0], gains[1], shifts[1], shifts[2], shifts[3]])


def rising(key, shape, sigma):
    base = jax.random.normal(key, shape, jnp.float32)
    lead = jnp.arange(shape[-2], dtype=jnp.float32) / max(shape[-2] - 1, 1)
    trail = jnp.arange(shape[-1], dtype=jnp.float32) / max(shape[-1] - 1, 1)
    factor = jnp.sqrt((1.0 + 2.0 * lead)[:, None] * (1.0 + 2.0 * trail)[None, :])
    return base * sigma * factor


def draw_qkv_master(key, part):
    return rising(key, (3, D, D), D ** (-0.5))


def draw_out_master(key, part):
    return rising(key, (D, D), (D // 32) ** (-0.5))


def draw_in_master(key, part):
    return rising(key, (D, FF), D ** (-0.5))


def draw_down_master(key, part):
    return rising(key, (FF, D), FF ** (-0.5))


def block_scale(stream_key, dims, shards, low, high):
    level, own = 1.0, jax.random.fold_in(stream_key, 6)
    for position, blocks in shards:
        steps = jnp.exp(jax.random.uniform(jax.random.fold_in(own, position), (blocks,), jnp.float32, low / len(shards), high / len(shards)))
        level = level * jnp.repeat(steps, dims[position] // blocks).reshape([-1 if axis == position else 1 for axis in range(len(dims))])
    return level


def normal_values(key, extent, spread, limit, cuts=(), kind=jnp.bfloat16):
    factor_of = block_scale(key, extent, cuts, -0.22, 0.18) if cuts else 1.0
    result = jax.random.normal(key, extent, jnp.float32) * spread * factor_of
    return jnp.minimum(jnp.maximum(result, -limit), limit).astype(kind)


def setup_inputs(seed: int = 0) -> dict:
    seeds = jax.random.split(jax.random.key(seed), 23)
    rows = normal_values(seeds[0], (ROWS, D), 1.0, 6.0, ((0, 32),))
    cotangent = normal_values(seeds[1], (ROWS, D), 1.0, 6.0, ((0, 32),))
    group_ids = draw_group_ids(jax.random.fold_in(seeds[22], 71), 0)
    qkv_weight = normal_values(seeds[3], (3, D, D), D ** -0.5, 0.21875, ((2, 4),))
    out_weight = normal_values(seeds[4], (D, D), (D // 32) ** -0.5, 1.25, ((0, 4),))
    in_weight = normal_values(seeds[5], (D, FF), D ** -0.5, 0.21875, ((1, 4),))
    down_weight = normal_values(seeds[6], (FF, D), FF ** -0.5, 0.109375, ((0, 4),))
    vectors = draw_vectors(jax.random.fold_in(seeds[22], 71), 0)
    qkv_master = draw_qkv_master(jax.random.fold_in(seeds[22], 71), 0)
    qkv_first = normal_values(seeds[9], (3, D, D), (0.5 * ROWS ** 0.5), 384.0, ((1, 8), (2, 4)), jnp.float32)
    qkv_second = jnp.clip(jnp.exp(math.log(16384.0) - 1.3862944 * jax.random.uniform(seeds[10], (3, D, D), jnp.float32) ** block_scale(seeds[10], (3, D, D), ((1, 8), (2, 4)), -0.2, 0.2)), 4096.0, 16384.0)
    out_master = draw_out_master(jax.random.fold_in(seeds[22], 71), 0)
    out_first = normal_values(seeds[12], (D, D), (0.15 * ROWS ** 0.5), 112.0, ((0, 4), (1, 8)), jnp.float32)
    out_second = jnp.clip(jnp.exp(math.log(1474.56) - 1.3862944 * jax.random.uniform(seeds[13], (D, D), jnp.float32) ** block_scale(seeds[13], (D, D), ((0, 4), (1, 8)), -0.2, 0.2)), 368.64, 1474.56)
    in_master = draw_in_master(jax.random.fold_in(seeds[22], 71), 0)
    in_first = normal_values(seeds[15], (D, FF), (0.3 * ROWS ** 0.5), 224.0, ((0, 8), (1, 4)), jnp.float32)
    in_second = jnp.clip(jnp.exp(math.log(5898.24) - 1.3862944 * jax.random.uniform(seeds[16], (D, FF), jnp.float32) ** block_scale(seeds[16], (D, FF), ((0, 8), (1, 4)), -0.2, 0.2)), 1474.56, 5898.24)
    down_master = draw_down_master(jax.random.fold_in(seeds[22], 71), 0)
    down_first = normal_values(seeds[18], (FF, D), (0.6 * ROWS ** 0.5), 448.0, ((0, 4), (1, 8)), jnp.float32)
    down_second = jnp.clip(jnp.exp(math.log(23592.96) - 1.3862944 * jax.random.uniform(seeds[19], (FF, D), jnp.float32) ** block_scale(seeds[19], (FF, D), ((0, 4), (1, 8)), -0.2, 0.2)), 5898.24, 23592.96)
    vec_first = normal_values(seeds[20], (6, D), (ROWS ** 0.5), 768.0, (), jnp.float32)
    vec_second = jnp.clip(jnp.exp(jax.random.uniform(seeds[21], (6, D), jnp.float32, math.log(16384.0), math.log(65536.0))), 16384.0, 65536.0)
    return {"rows": rows, "cotangent": cotangent, "group_ids": group_ids, "qkv_weight": qkv_weight, "out_weight": out_weight, "in_weight": in_weight, "down_weight": down_weight, "vectors": vectors, "qkv_master": qkv_master, "qkv_first": qkv_first, "qkv_second": qkv_second, "out_master": out_master, "out_first": out_first, "out_second": out_second, "in_master": in_master, "in_first": in_first, "in_second": in_second, "down_master": down_master, "down_first": down_first, "down_second": down_second, "vec_first": vec_first, "vec_second": vec_second}


NORM_EPS = 1e-06
ADAM_EPS = 1e-06
MOMENT_DECAY = 0.5
LEARN_RATE = 0.5
WEIGHT_DECAY = 0.01

@jax.custom_vjp
def low(v):
    return lax.optimization_barrier(v.astype(jnp.bfloat16)).astype(jnp.float32)

@jax.custom_vjp
def low_back(v):
    return v

def low_keep(v):
    return (low(v), None)

def low_pass(kept, grad):
    return (grad,)

def back_keep(v):
    return (v, None)

def back_low(kept, grad):
    return (low(grad),)
low.defvjp(low_keep, low_pass)
low_back.defvjp(back_keep, back_low)

def matmul(left, right):
    return jnp.dot(left, right, precision=lax.Precision.HIGHEST, preferred_element_type=jnp.float32)

def layer_norm(values, gain, shift):
    center = values - lax.optimization_barrier(jnp.mean(values, axis=-1, keepdims=True))
    variance = lax.optimization_barrier(jnp.mean(center * center, axis=-1, keepdims=True))
    return center * lax.rsqrt(variance + NORM_EPS) * gain + shift

def block(inputs, params):
    qkv_w, out_w, in_w, down_w, vecs = params
    normed_in = low(layer_norm(inputs, vecs[0], vecs[1]))
    shape = (IMG_BLOCK, PATCHES, HEADS, HEAD_DIM)
    queries = low(low_back(matmul(normed_in, qkv_w[0]))).reshape(shape)
    keys = low(low_back(matmul(normed_in, qkv_w[1]))).reshape(shape)
    values = low(low_back(matmul(normed_in, qkv_w[2]))).reshape(shape)
    scores = low_back(jnp.einsum('bqhd,bkhd->bhqk', queries, keys, precision=lax.Precision.HIGHEST)) * HEAD_DIM ** (-0.5)
    peak = lax.optimization_barrier(jnp.max(scores, axis=-1, keepdims=True))
    expo = jnp.exp(scores - peak)
    probs = low(expo / lax.optimization_barrier(jnp.sum(expo, axis=-1, keepdims=True)))
    mixed = jnp.einsum('bhqk,bkhd->bqhd', probs, values, precision=lax.Precision.HIGHEST).reshape(-1, D)
    mixed = low(low_back(mixed))
    first = inputs + low_back(matmul(mixed, out_w)) + vecs[4]
    normed_mid = low(layer_norm(first, vecs[2], vecs[3]))
    activ = low(jax.nn.gelu(low_back(matmul(normed_mid, in_w)), approximate=False))
    return first + low_back(matmul(activ, down_w)) + vecs[5]

def forward(stacked, params):

    def step(carry, piece):
        return (carry, jax.checkpoint(block)(piece, params))
    unused, outputs = lax.scan(step, jnp.zeros((), jnp.float32), stacked)
    return outputs

def lamb(grad, master, first, second, correction):
    first_new = MOMENT_DECAY * first + (1.0 - MOMENT_DECAY) * grad
    second_new = MOMENT_DECAY * second + (1.0 - MOMENT_DECAY) * grad * grad
    update = first_new / correction / (jnp.sqrt(second_new / correction) + ADAM_EPS) + WEIGHT_DECAY * master
    weight_norm = jnp.sqrt(jnp.sum(master * master))
    update_norm = jnp.sqrt(jnp.sum(update * update))
    trust = weight_norm / (update_norm + ADAM_EPS)
    return (first_new, second_new, master - LEARN_RATE * trust * update, weight_norm, update_norm, trust)

def reference(rows, cotangent, group_ids, qkv_weight, out_weight, in_weight, down_weight, vectors, qkv_master, qkv_first, qkv_second, out_master, out_first, out_second, in_master, in_first, in_second, down_master, down_first, down_second, vec_first, vec_second):
    onehot = (group_ids[:, None] == jnp.arange(GROUPS, dtype=jnp.int32)[None, :]).astype(jnp.float32)
    counts = lax.optimization_barrier(jnp.sum(onehot, axis=0))
    image_weight = jnp.sqrt(IMAGES / (GROUPS * jnp.dot(onehot, counts, precision=lax.Precision.HIGHEST)))
    blocks = IMAGES // IMG_BLOCK
    weighted = cotangent.astype(jnp.float32).reshape(IMAGES, PATCHES, D) * image_weight[:, None, None]
    weighted = weighted.reshape(blocks, IMG_BLOCK * PATCHES, D)
    stacked = rows.astype(jnp.float32).reshape(blocks, IMG_BLOCK * PATCHES, D)
    params = (qkv_weight.astype(jnp.float32), out_weight.astype(jnp.float32), in_weight.astype(jnp.float32), down_weight.astype(jnp.float32), vectors)
    outputs, pullback = jax.vjp(forward, stacked, params)
    grad_rows, grads = pullback(weighted)
    out_rows = outputs.reshape(ROWS, D).astype(jnp.bfloat16)
    input_grad = grad_rows.reshape(ROWS, D)
    qkv_grad, out_grad, in_grad, down_grad, vec_grad = grads
    correction = 1.0 - MOMENT_DECAY ** STEP
    qkv_res = lamb(qkv_grad, qkv_master, qkv_first, qkv_second, correction)
    out_res = lamb(out_grad, out_master, out_first, out_second, correction)
    in_res = lamb(in_grad, in_master, in_first, in_second, correction)
    down_res = lamb(down_grad, down_master, down_first, down_second, correction)
    every = (qkv_res, out_res, in_res, down_res)
    matrix_norms = jnp.stack([jnp.stack([entry[3] for entry in every]), jnp.stack([entry[4] for entry in every]), jnp.stack([entry[5] for entry in every])])
    vec_first_new = MOMENT_DECAY * vec_first + (1.0 - MOMENT_DECAY) * vec_grad
    vec_second_new = MOMENT_DECAY * vec_second + (1.0 - MOMENT_DECAY) * vec_grad * vec_grad
    vec_new = vectors - LEARN_RATE * (vec_first_new / correction) / (jnp.sqrt(vec_second_new / correction) + ADAM_EPS)
    return (out_rows, input_grad, qkv_grad, out_grad, in_grad, down_grad, qkv_res[0], qkv_res[1], qkv_res[2], out_res[0], out_res[1], out_res[2], in_res[0], in_res[1], in_res[2], down_res[0], down_res[1], down_res[2], vec_grad, vec_first_new, vec_second_new, vec_new, matrix_norms)
```

```python
import math

import jax
import jax.numpy as jnp
from jax import lax
from jax.experimental import pallas as pl
from jax.experimental.pallas import tpu as pltpu
from jax.sharding import PartitionSpec as P

HEAD_DIM = 64
PATCHES = 256
GROUPS = 8
STEP = 5

NORM_EPS = 1e-06
ADAM_EPS = 1e-06
MOMENT_DECAY = 0.5
LEARN_RATE = 0.5
WEIGHT_DECAY = 0.01
SCALE = HEAD_DIM ** (-0.5)

F32 = jnp.float32
BF16 = jnp.bfloat16
MB = 1024 * 1024


def mm(left, right):
    return jnp.dot(left, right, preferred_element_type=F32)


def mm_nt(left, right):
    return lax.dot_general(left, right, (((1,), (1,)), ((), ())), preferred_element_type=F32)


def mm_tn(left, right):
    return lax.dot_general(left, right, (((0,), (0,)), ((), ())), preferred_element_type=F32)


def layer_stats(values):
    center = values - jnp.mean(values, axis=-1, keepdims=True)
    inverse = lax.rsqrt(jnp.mean(center * center, axis=-1, keepdims=True) + NORM_EPS)
    return center * inverse, inverse


def norm_back(grad_normed, normed, inverse):
    return inverse * (
        grad_normed
        - jnp.mean(grad_normed, axis=-1, keepdims=True)
        - normed * jnp.mean(grad_normed * normed, axis=-1, keepdims=True)
    )


def gelu_pair(t):
    size = jnp.abs(t) * (2.0**-0.5)
    k = 1.0 / (1.0 + 0.3275911 * size)
    bell = jnp.exp(-size * size)
    poly = k * (
        0.254829592
        + k * (-0.284496736 + k * (1.421413741 + k * (-1.453152027 + k * 1.061405429)))
    )
    tail = 0.5 * poly * bell
    cdf = jnp.where(t < 0, tail, 1.0 - tail)
    return t * cdf, cdf + t * bell * (1.0 / math.sqrt(2.0 * math.pi))


def put_turned(out_ref, value, pos_ref, count, start):
    turned = value.T
    part = turned.shape[0] // count
    width = turned.shape[1]
    if len(out_ref.shape) == 2:
        out_ref[:, start : start + width] = turned
        return
    for j in range(count):
        out_ref[pos_ref[j], :, start : start + width] = turned[j * part : (j + 1) * part]


def turned_shape(width, rows, count):
    part = width // count
    if part % 16 == 0:
        return (count, part, rows)
    return (width, rows)


def turned_order(turned, pos, count):
    width = turned.shape[0] if turned.ndim == 2 else turned.shape[0] * turned.shape[1]
    rows = turned.shape[-1]
    if turned.ndim == 2:
        shaped = turned.reshape(count, width // count, rows)
        turned = jnp.zeros_like(shaped).at[pos].set(shaped)
    return turned.reshape(width, rows)


def params(limit, **more):
    return pltpu.CompilerParams(vmem_limit_bytes=limit * MB, **more)


def full(shape):
    return pl.BlockSpec(shape, lambda *_: (0,) * len(shape))


SMEM = pl.BlockSpec(memory_space=pltpu.SMEM)


def start_kernel(pos_ref, rows_ref, vec_ref, x_ref, xt_ref, *, count):
    width, rows = rows_ref.shape[1], rows_ref.shape[0]
    for start in range(0, rows, PATCHES):
        normed, _ = layer_stats(rows_ref[start : start + PATCHES].astype(F32))
        low = (normed * vec_ref[0:1] + vec_ref[1:2]).astype(BF16)
        x_ref[start : start + PATCHES] = low
        put_turned(xt_ref, low, pos_ref, count, start)


def run_start(pos, rows, vectors, count):
    r, d = rows.shape
    return pl.pallas_call(
        lambda *refs: start_kernel(*refs, count=count),
        out_shape=(
            jax.ShapeDtypeStruct((r, d), BF16),
            jax.ShapeDtypeStruct(turned_shape(d, r, count), BF16),
        ),
        in_specs=[SMEM, pl.BlockSpec(memory_space=pltpu.VMEM), pl.BlockSpec(memory_space=pltpu.VMEM)],
        compiler_params=params(32),
    )(pos, rows, vectors)


def gout_kernel(pos_ref, weight_ref, cot_ref, g_ref, gt_ref, *, count):
    rows = cot_ref.shape[0]
    for index in range(rows // PATCHES):
        start = index * PATCHES
        low = (cot_ref[start : start + PATCHES].astype(F32) * weight_ref[index]).astype(BF16)
        g_ref[start : start + PATCHES] = low
        put_turned(gt_ref, low, pos_ref, count, start)


def run_gout(pos, weight, cot, count):
    r, d = cot.shape
    return pl.pallas_call(
        lambda *refs: gout_kernel(*refs, count=count),
        out_shape=(
            jax.ShapeDtypeStruct((r, d), BF16),
            jax.ShapeDtypeStruct(turned_shape(d, r, count), BF16),
        ),
        in_specs=[SMEM, SMEM, pl.BlockSpec(memory_space=pltpu.VMEM)],
        compiler_params=params(32),
    )(pos, weight, cot)


def attend_shard(x, w_ref, saved_ref, probs_ref):
    cols = w_ref.shape[1] // 4
    qkv = mm(x, w_ref[:, : 3 * cols]).astype(BF16)
    saved_ref[:, : 3 * cols] = qkv
    mixed = []
    for h in range(cols // HEAD_DIM):
        at = h * HEAD_DIM
        q = qkv[:, at : at + HEAD_DIM] * SCALE
        k = qkv[:, cols + at : cols + at + HEAD_DIM]
        v = qkv[:, 2 * cols + at : 2 * cols + at + HEAD_DIM]
        scores = mm_nt(q, k)
        expo = jnp.exp(scores - jnp.max(scores, axis=-1, keepdims=True))
        probs = (expo * (1.0 / jnp.sum(expo, axis=-1, keepdims=True))).astype(BF16)
        probs_ref[h] = probs
        mixed.append(mm(probs, v).astype(BF16))
    mixed = jnp.concatenate(mixed, axis=1)
    saved_ref[:, 3 * cols :] = mixed
    return mm_nt(mixed, w_ref[:, 3 * cols :])


def attn_one_kernel(x_ref, rows_ref, vec_ref, wa_ref, wb_ref, acc_ref, sa_ref, pa_ref, sb_ref, pb_ref):
    x = x_ref[...]
    term = attend_shard(x, wa_ref, sa_ref, pa_ref)
    term += attend_shard(x, wb_ref, sb_ref, pb_ref)
    acc_ref[...] = rows_ref[...].astype(F32) + term + vec_ref[4:5]


def attn_two_kernel(
    pos_ref, x_ref, acc_ref, vec_ref, wa_ref, wb_ref,
    first_ref, mid_ref, midt_ref, sa_ref, pa_ref, sb_ref, pb_ref, *, count,
):
    x = x_ref[...]
    term = attend_shard(x, wa_ref, sa_ref, pa_ref)
    term += attend_shard(x, wb_ref, sb_ref, pb_ref)
    first = acc_ref[...] + term
    first_ref[...] = first
    normed, _ = layer_stats(first)
    low = (normed * vec_ref[2:3] + vec_ref[3:4]).astype(BF16)
    mid_ref[...] = low
    put_turned(midt_ref, low, pos_ref, count, 0)


def image_block(d):
    return pl.BlockSpec((PATCHES, d), lambda i: (i, 0))


def saved_outputs(r, d, heads):
    images = r // PATCHES
    shapes = (
        jax.ShapeDtypeStruct((r, d), BF16),
        jax.ShapeDtypeStruct((images * heads, PATCHES, PATCHES), BF16),
    )
    specs = [image_block(d), pl.BlockSpec((heads, PATCHES, PATCHES), lambda i: (i, 0, 0))]
    return shapes, specs


def attn_cost(r, d):
    return pl.CostEstimate(flops=2 * 2 * r * d * d + 8 * r * PATCHES * d // 2, bytes_accessed=10 * MB, transcendentals=r * PATCHES * 6)


def run_attn_one(x, rows, vectors, wa, wb):
    r, d = x.shape
    heads = d // 4 // HEAD_DIM
    shapes, specs = saved_outputs(r, d, heads)
    return pl.pallas_call(
        attn_one_kernel,
        grid=(r // PATCHES,),
        out_shape=(jax.ShapeDtypeStruct((r, d), F32),) + shapes * 2,
        in_specs=[image_block(d), image_block(d), full(vectors.shape), full((d, d)), full((d, d))],
        out_specs=[image_block(d)] + specs * 2,
        compiler_params=params(32),
        cost_estimate=attn_cost(r, d),
    )(x, rows, vectors, wa, wb)


def run_attn_two(pos, x, acc, vectors, wa, wb, count):
    r, d = x.shape
    heads = d // 4 // HEAD_DIM
    shapes, specs = saved_outputs(r, d, heads)
    tshape = turned_shape(d, r, count)
    tspec = pl.BlockSpec(
        tshape[:-1] + (PATCHES,), lambda i: (0,) * (len(tshape) - 1) + (i,)
    )
    return pl.pallas_call(
        lambda *refs: attn_two_kernel(*refs, count=count),
        grid=(r // PATCHES,),
        out_shape=(
            jax.ShapeDtypeStruct((r, d), F32),
            jax.ShapeDtypeStruct((r, d), BF16),
            jax.ShapeDtypeStruct(tshape, BF16),
        )
        + shapes * 2,
        in_specs=[SMEM, image_block(d), image_block(d), full(vectors.shape), full((d, d)), full((d, d))],
        out_specs=[image_block(d), image_block(d), tspec] + specs * 2,
        compiler_params=params(32),
        cost_estimate=attn_cost(r, d),
    )(pos, x, acc, vectors, wa, wb)


TILES = 3


def ffn_tile(mid_ref, midt_ref, g_ref, gt_ref, in_ref, down_ref, gi_ref, gd_ref, y_ref, dm_ref):
    w_in = in_ref[...]
    w_down = down_ref[...]
    pre = mm(mid_ref[...], w_in)
    dact = mm_nt(g_ref[...], w_down)
    activ, slope = gelu_pair(pre)
    activ = activ.astype(BF16)
    dpre = (dact * slope).astype(BF16)
    y_ref[...] += mm(activ, w_down)
    dm_ref[...] += mm_nt(dpre, w_in)
    gd_ref[...] = mm(gt_ref[...], activ).astype(BF16)
    gi_ref[...] = mm(midt_ref[...], dpre).astype(BF16)


def ffn_pair(mid_ref, midt_ref, g_ref, gt_ref, wa, wb, ga, gb, y_ref, dm_ref):
    step = pl.program_id(0)

    @pl.when(step < TILES)
    def _():
        ffn_tile(mid_ref, midt_ref, g_ref, gt_ref, *wa, *ga, y_ref, dm_ref)

    @pl.when(step >= TILES)
    def _():
        ffn_tile(mid_ref, midt_ref, g_ref, gt_ref, *wb, *gb, y_ref, dm_ref)


def ffn_one_kernel(
    mid_ref, midt_ref, g_ref, gt_ref, ia_ref, da_ref, ib_ref, db_ref,
    y_ref, dm_ref, gia_ref, gda_ref, gib_ref, gdb_ref,
):
    @pl.when(pl.program_id(0) == 0)
    def _():
        y_ref[...] = jnp.zeros_like(y_ref)
        dm_ref[...] = jnp.zeros_like(dm_ref)

    ffn_pair(
        mid_ref, midt_ref, g_ref, gt_ref, (ia_ref, da_ref), (ib_ref, db_ref),
        (gia_ref, gda_ref), (gib_ref, gdb_ref), y_ref, dm_ref,
    )


def ffn_two_kernel(
    pos_ref, weight_ref, mid_ref, midt_ref, g_ref, gt_ref, ia_ref, da_ref, ib_ref, db_ref,
    y_in_ref, dm_in_ref, first_ref, cot_ref, vec_ref,
    out_ref, gf_ref, gfl_ref, gft_ref, sums_ref, gia_ref, gda_ref, gib_ref, gdb_ref,
    y_ref, dm_ref, *, count,
):
    @pl.when(pl.program_id(0) == 0)
    def _():
        y_ref[...] = y_in_ref[...]
        dm_ref[...] = dm_in_ref[...]

    ffn_pair(
        mid_ref, midt_ref, g_ref, gt_ref, (ia_ref, da_ref), (ib_ref, db_ref),
        (gia_ref, gda_ref), (gib_ref, gdb_ref), y_ref, dm_ref,
    )

    @pl.when(pl.program_id(0) == pl.num_programs(0) - 1)
    def _():
        rows = first_ref.shape[0]
        sums = [0.0, 0.0, 0.0, 0.0]
        chunk = 128
        for start in range(0, rows, chunk):
            here = slice(start, start + chunk)
            first = first_ref[here]
            normed, inverse = layer_stats(first)
            out_ref[here] = (first + y_ref[here] + vec_ref[5:6]).astype(BF16)
            dmid = dm_ref[here]
            gout = cot_ref[here].astype(F32) * weight_ref[start // PATCHES]
            gfirst = gout + norm_back(dmid * vec_ref[2:3], normed, inverse)
            gf_ref[here] = gfirst
            low = gfirst.astype(BF16)
            gfl_ref[here] = low
            put_turned(gft_ref, low, pos_ref, count, start)
            for index, term in enumerate((dmid * normed, dmid, gfirst, gout)):
                sums[index] += jnp.sum(term, axis=0, keepdims=True)
        sums_ref[...] = jnp.concatenate(sums + sums, axis=0)


def ffn_specs(d):
    tile = d // TILES
    cols = lambda f: pl.BlockSpec((d, tile), lambda i: (0, f(i)))
    rows = lambda f: pl.BlockSpec((tile, d), lambda i: (f(i), 0))
    fa = lambda i: jnp.minimum(i, TILES - 1)
    fb = lambda i: jnp.maximum(i - TILES, 0)
    return [cols(fa), rows(fa), cols(fb), rows(fb)], [cols(fa), cols(fa), cols(fb), cols(fb)]


def ffn_cost(r, d):
    return pl.CostEstimate(flops=2 * 7 * 2 * r * d * d, bytes_accessed=16 * MB, transcendentals=4 * r * d)


def run_ffn_one(mid, midt, g, gt, wa, wb):
    r, d = mid.shape
    w_specs, g_specs = ffn_specs(d)
    grad = jax.ShapeDtypeStruct((d, d), BF16)
    return pl.pallas_call(
        ffn_one_kernel,
        grid=(2 * TILES,),
        out_shape=(jax.ShapeDtypeStruct((r, d), F32),) * 2 + (grad,) * 4,
        in_specs=[full((r, d)), full((d, r)), full((r, d)), full((d, r))] + w_specs,
        out_specs=[full((r, d)), full((r, d))] + g_specs,
        compiler_params=params(40),
        cost_estimate=ffn_cost(r, d),
    )(mid, midt, g, gt, *wa, *wb)


def run_ffn_two(pos, weight, mid, midt, g, gt, wa, wb, y, dm, first, cot, vectors, count):
    r, d = mid.shape
    w_specs, g_specs = ffn_specs(d)
    grad = jax.ShapeDtypeStruct((d, d), BF16)
    tshape = turned_shape(d, r, count)
    return pl.pallas_call(
        lambda *refs: ffn_two_kernel(*refs, count=count),
        grid=(2 * TILES,),
        out_shape=(
            jax.ShapeDtypeStruct((r, d), BF16),
            jax.ShapeDtypeStruct((r, d), F32),
            jax.ShapeDtypeStruct((r, d), BF16),
            jax.ShapeDtypeStruct(tshape, BF16),
            jax.ShapeDtypeStruct((8, d), F32),
        )
        + (grad,) * 4,
        in_specs=[SMEM, SMEM, full((r, d)), full((d, r)), full((r, d)), full((d, r))]
        + w_specs
        + [full((r, d))] * 4
        + [full(vectors.shape)],
        out_specs=[full((r, d)), full((r, d)), full((r, d)), full(tshape), full((8, d))] + g_specs,
        scratch_shapes=[pltpu.VMEM((r, d), F32), pltpu.VMEM((r, d), F32)],
        compiler_params=params(52),
        cost_estimate=ffn_cost(r, d),
    )(pos, weight, mid, midt, g, gt, *wa, *wb, y, dm, first, cot, vectors)


def attend_back_shard(gf, w_ref, saved_ref, probs_ref, keep_ref):
    cols = w_ref.shape[1] // 4
    start = pl.multiple_of(pl.program_id(0) * PATCHES, PATCHES)
    dmix = mm(gf, w_ref[:, 3 * cols :]).astype(BF16)
    dq, dk, dv = [], [], []
    for h in range(cols // HEAD_DIM):
        at = h * HEAD_DIM
        q = saved_ref[:, at : at + HEAD_DIM]
        k = saved_ref[:, cols + at : cols + at + HEAD_DIM]
        v = saved_ref[:, 2 * cols + at : 2 * cols + at + HEAD_DIM]
        do = dmix[:, at : at + HEAD_DIM]
        probs = probs_ref[h]
        dv.append(mm_tn(probs, do).astype(BF16))
        dp = mm_nt(do, v)
        wide = probs.astype(F32)
        ds = (SCALE * wide * (dp - jnp.sum(wide * dp, axis=-1, keepdims=True))).astype(BF16)
        dq.append(mm(ds, k).astype(BF16))
        dk.append(mm_tn(ds, q).astype(BF16))
    dqkv = jnp.concatenate(dq + dk + dv, axis=1)
    keep_ref[pl.ds(start, PATCHES), : 3 * cols] = dqkv
    keep_ref[pl.ds(start, PATCHES), 3 * cols :] = saved_ref[:, 3 * cols :]
    return mm_nt(dqkv, w_ref[:, : 3 * cols])


def attn_grad(xt_ref, gft_ref, keep_ref, g_ref):
    cols = keep_ref.shape[1] // 4
    g_ref[:, : 3 * cols] = mm(xt_ref[...], keep_ref[:, : 3 * cols]).astype(BF16)
    g_ref[:, 3 * cols :] = mm(gft_ref[...], keep_ref[:, 3 * cols :]).astype(BF16)


def back_one_kernel(
    gf_ref, xt_ref, gft_ref, wa_ref, wb_ref, sa_ref, pa_ref, sb_ref, pb_ref,
    acc_ref, ga_ref, gb_ref, ka_ref, kb_ref,
):
    gf = gf_ref[...]
    term = attend_back_shard(gf, wa_ref, sa_ref, pa_ref, ka_ref)
    term += attend_back_shard(gf, wb_ref, sb_ref, pb_ref, kb_ref)
    acc_ref[...] = term

    @pl.when(pl.program_id(0) == pl.num_programs(0) - 1)
    def _():
        attn_grad(xt_ref, gft_ref, ka_ref, ga_ref)
        attn_grad(xt_ref, gft_ref, kb_ref, gb_ref)


def back_two_kernel(
    gf_ref, xt_ref, gft_ref, wa_ref, wb_ref, sa_ref, pa_ref, sb_ref, pb_ref,
    acc_ref, rows_ref, gfirst_ref, vec_ref,
    ig_ref, sums_ref, ga_ref, gb_ref, ka_ref, kb_ref,
):
    gf = gf_ref[...]
    term = attend_back_shard(gf, wa_ref, sa_ref, pa_ref, ka_ref)
    term += attend_back_shard(gf, wb_ref, sb_ref, pb_ref, kb_ref)
    grad_in = acc_ref[...] + term
    normed, inverse = layer_stats(rows_ref[...].astype(F32))
    ig_ref[...] = gfirst_ref[...] + norm_back(grad_in * vec_ref[0:1], normed, inverse)
    one = jnp.sum(grad_in * normed, axis=0, keepdims=True)
    two = jnp.sum(grad_in, axis=0, keepdims=True)
    sums = jnp.concatenate([one, two] * 4, axis=0)

    @pl.when(pl.program_id(0) == 0)
    def _():
        sums_ref[...] = sums

    @pl.when(pl.program_id(0) > 0)
    def _():
        sums_ref[...] += sums

    @pl.when(pl.program_id(0) == pl.num_programs(0) - 1)
    def _():
        attn_grad(xt_ref, gft_ref, ka_ref, ga_ref)
        attn_grad(xt_ref, gft_ref, kb_ref, gb_ref)


def back_cost(r, d):
    return pl.CostEstimate(flops=2 * 2 * 2 * r * d * d + 20 * r * PATCHES * d // 2, bytes_accessed=12 * MB, transcendentals=0)


def run_back(gfl, xt, gft, wa, wb, saved_a, saved_b, tail=None):
    r, d = gfl.shape
    heads = d // 4 // HEAD_DIM
    _, specs = saved_outputs(r, d, heads)
    grad = jax.ShapeDtypeStruct((d, d), BF16)
    wide = jax.ShapeDtypeStruct((r, d), F32)
    in_specs = [image_block(d), full((d, r)), full((d, r)), full((d, d)), full((d, d))] + specs * 2
    scratch = [pltpu.VMEM((r, d), BF16)] * 2
    if tail is None:
        return pl.pallas_call(
            back_one_kernel,
            grid=(r // PATCHES,),
            out_shape=(wide, grad, grad),
            in_specs=in_specs,
            out_specs=[image_block(d), full((d, d)), full((d, d))],
            scratch_shapes=scratch,
            compiler_params=params(40),
            cost_estimate=back_cost(r, d),
        )(gfl, xt, gft, wa, wb, *saved_a, *saved_b)
    return pl.pallas_call(
        back_two_kernel,
        grid=(r // PATCHES,),
        out_shape=(wide, jax.ShapeDtypeStruct((8, d), F32), grad, grad),
        in_specs=in_specs + [image_block(d)] * 3 + [full(tail[3].shape)],
        out_specs=[image_block(d), full((8, d)), full((d, d)), full((d, d))],
        scratch_shapes=scratch,
        compiler_params=params(40),
        cost_estimate=back_cost(r, d),
    )(gfl, xt, gft, wa, wb, *saved_a, *saved_b, *tail)


def swap(value, axis, bit):
    size = lax.axis_size(axis)
    return lax.ppermute(value, axis, [(i, i ^ bit) for i in range(size)])


def all_sum(value):
    for axis in ("mp", "dp"):
        bit = 1
        while bit < lax.axis_size(axis):
            value = value + swap(value, axis, bit)
            bit *= 2
    return value


def reduce_parts(g0, g1, g2, g3, bits):
    c1 = swap(g1, "mp", 1)
    c3 = swap(g3, "mp", 1)
    s2 = (g2.astype(F32) + c3.astype(F32)).astype(BF16)
    y2 = swap(s2, "mp", 2)
    total = g0.astype(F32) + c1.astype(F32) + y2.astype(F32)
    for bit in bits:
        half = total.shape[0] // 2
        total = total[:half] + swap(total[half:].astype(BF16), "dp", 1 << bit).astype(F32)
    return total


def lamb_parts(grad, master, first, second, correction):
    first_new = MOMENT_DECAY * first + (1.0 - MOMENT_DECAY) * grad
    second_new = MOMENT_DECAY * second + (1.0 - MOMENT_DECAY) * grad * grad
    update = (
        first_new / correction / (jnp.sqrt(second_new / correction) + ADAM_EPS)
        + WEIGHT_DECAY * master
    )
    return (first_new, second_new, update)


def shards(
    rows,
    cotangent,
    group_ids,
    qkv_weight,
    out_weight,
    in_weight,
    down_weight,
    vectors,
    qkv_master,
    qkv_first,
    qkv_second,
    out_master,
    out_first,
    out_second,
    in_master,
    in_first,
    in_second,
    down_master,
    down_first,
    down_second,
    vec_first,
    vec_second,
):
    count = lax.axis_size("dp")
    width = rows.shape[1]
    cols = qkv_weight.shape[2]
    nbits = count.bit_length() - 1
    bits = tuple(range(nbits))
    rel = jnp.arange(count, dtype=jnp.int32) ^ lax.axis_index("dp").astype(jnp.int32)
    pos = sum(((rel >> bit) & 1) << (nbits - 1 - place) for place, bit in enumerate(bits))

    attn_w = [
        jnp.concatenate([qkv_weight[0], qkv_weight[1], qkv_weight[2], out_weight.T], axis=1)
    ]
    in_w = [in_weight]
    down_w = [down_weight]
    for group in (attn_w, in_w, down_w):
        near = swap(group[0], "mp", 1)
        far = swap(group[0], "mp", 2)
        group += [near, far, swap(far, "mp", 1)]

    onehot = (group_ids[:, None] == jnp.arange(GROUPS, dtype=jnp.int32)[None, :]).astype(F32)
    counts = all_sum(jnp.sum(onehot, axis=0))
    image_weight = jnp.sqrt(jnp.sum(counts) / (GROUPS * jnp.sum(onehot * counts, axis=1)))

    x, xt = run_start(pos, rows, vectors, count)
    xt = turned_order(xt, pos, count)
    gout, goutt = run_gout(pos, image_weight, cotangent, count)
    goutt = turned_order(goutt, pos, count)
    acc, s1, p1, s0, p0 = run_attn_one(x, rows, vectors, attn_w[1], attn_w[0])
    first, mid, midt, s3, p3, s2, p2 = run_attn_two(pos, x, acc, vectors, attn_w[3], attn_w[2], count)
    midt = turned_order(midt, pos, count)
    y, dm, gi1, gd1, gi0, gd0 = run_ffn_one(
        mid, midt, gout, goutt, (in_w[1], down_w[1]), (in_w[0], down_w[0])
    )
    out_rows, gfirst, gfl, gft, sums_b, gi3, gd3, gi2, gd2 = run_ffn_two(
        pos, image_weight, mid, midt, gout, goutt, (in_w[3], down_w[3]), (in_w[2], down_w[2]),
        y, dm, first, cotangent, vectors, count,
    )
    gft = turned_order(gft, pos, count)
    gin, ga3, ga2 = run_back(gfl, xt, gft, attn_w[3], attn_w[2], (s3, p3), (s2, p2))
    input_grad, sums_a, ga1, ga0 = run_back(
        gfl, xt, gft, attn_w[1], attn_w[0], (s1, p1), (s0, p0), (gin, rows, gfirst, vectors)
    )
    down_sum = reduce_parts(gd0, gd1, gd2, gd3, bits)
    in_sum = reduce_parts(gi0, gi1, gi2, gi3, bits)
    attn_sum = reduce_parts(ga0, ga1, ga2, ga3, bits)

    part = width // count
    qkv_grad = jnp.moveaxis(attn_sum[:, : 3 * cols].reshape(part, 3, cols), 1, 0)
    out_grad = attn_sum[:, 3 * cols :].T
    in_grad = in_sum
    down_grad = down_sum.T

    correction = 1.0 - MOMENT_DECAY**STEP
    qkv_res = lamb_parts(qkv_grad, qkv_master, qkv_first, qkv_second, correction)
    out_res = lamb_parts(out_grad, out_master, out_first, out_second, correction)
    in_res = lamb_parts(in_grad, in_master, in_first, in_second, correction)
    down_res = lamb_parts(down_grad, down_master, down_first, down_second, correction)
    every = (qkv_res, out_res, in_res, down_res)
    masters = (qkv_master, out_master, in_master, down_master)
    squares = jnp.stack(
        [jnp.sum(master * master) for master in masters]
        + [jnp.sum(entry[2] * entry[2]) for entry in every]
    )
    squares = jnp.pad(squares[None], ((0, 1), (0, width - 8)))
    small = all_sum(jnp.concatenate([sums_a[:2], sums_b[:4], squares], axis=0))
    vec_grad = small[:6]
    weight_norms = jnp.sqrt(small[6, :4])
    update_norms = jnp.sqrt(small[6, 4:8])
    trusts = weight_norms / (update_norms + ADAM_EPS)
    new_masters = [
        masters[index] - LEARN_RATE * trusts[index] * every[index][2] for index in range(4)
    ]
    matrix_norms = jnp.stack([weight_norms, update_norms, trusts])
    vec_first_new = MOMENT_DECAY * vec_first + (1.0 - MOMENT_DECAY) * vec_grad
    vec_second_new = MOMENT_DECAY * vec_second + (1.0 - MOMENT_DECAY) * vec_grad * vec_grad
    vec_new = vectors - LEARN_RATE * (vec_first_new / correction) / (
        jnp.sqrt(vec_second_new / correction) + ADAM_EPS
    )
    return (
        out_rows,
        input_grad,
        qkv_grad,
        out_grad,
        in_grad,
        down_grad,
        qkv_res[0],
        qkv_res[1],
        new_masters[0],
        out_res[0],
        out_res[1],
        new_masters[1],
        in_res[0],
        in_res[1],
        new_masters[2],
        down_res[0],
        down_res[1],
        new_masters[3],
        vec_grad,
        vec_first_new,
        vec_second_new,
        vec_new,
        matrix_norms,
    )


def solution(mesh):
    rows = P(("dp", "mp"), None)
    qkv_state = P(None, "dp", "mp")
    out_state = P("mp", "dp")
    in_state = P("dp", "mp")
    in_specs = (
        (rows, rows, P(("dp", "mp")), P(None, None, "mp"), P("mp", None), P(None, "mp"), P("mp", None), P())
        + (qkv_state,) * 3
        + (out_state,) * 3
        + (in_state,) * 3
        + (out_state,) * 3
        + (P(), P())
    )
    out_specs = (
        (rows, rows, qkv_state, out_state, in_state, out_state)
        + (qkv_state,) * 3
        + (out_state,) * 3
        + (in_state,) * 3
        + (out_state,) * 3
        + (P(),) * 5
    )
    return jax.shard_map(shards, mesh=mesh, in_specs=in_specs, out_specs=out_specs, check_vma=False)
```

```python
import math

import jax
import jax.numpy as jnp
from jax import lax
from jax.experimental import pallas as pl
from jax.experimental.pallas import tpu as pltpu
from jax.sharding import PartitionSpec as P

HEAD_DIM = 64
PATCHES = 256
GROUPS = 8
STEP = 5

NORM_EPS = 1e-06
ADAM_EPS = 1e-06
MOMENT_DECAY = 0.5
LEARN_RATE = 0.5
WEIGHT_DECAY = 0.01
SCALE = HEAD_DIM ** (-0.5)

F32 = jnp.float32
BF16 = jnp.bfloat16
MB = 1024 * 1024
BIG = 16


def mm(left, right):
    return jnp.dot(left, right, preferred_element_type=F32)


def mm_nt(left, right):
    return lax.dot_general(left, right, (((1,), (1,)), ((), ())), preferred_element_type=F32)


def mm_tn(left, right):
    return lax.dot_general(left, right, (((0,), (0,)), ((), ())), preferred_element_type=F32)


def layer_stats(values):
    center = values - jnp.mean(values, axis=-1, keepdims=True)
    inverse = lax.rsqrt(jnp.mean(center * center, axis=-1, keepdims=True) + NORM_EPS)
    return center * inverse, inverse


def norm_back(grad_normed, normed, inverse):
    return inverse * (
        grad_normed
        - jnp.mean(grad_normed, axis=-1, keepdims=True)
        - normed * jnp.mean(grad_normed * normed, axis=-1, keepdims=True)
    )


def gelu_pair(t):
    size = jnp.abs(t) * (2.0**-0.5)
    k = 1.0 / (1.0 + 0.3275911 * size)
    bell = jnp.exp(-size * size)
    poly = k * (
        0.254829592
        + k * (-0.284496736 + k * (1.421413741 + k * (-1.453152027 + k * 1.061405429)))
    )
    tail = 0.5 * poly * bell
    cdf = jnp.where(t < 0, tail, 1.0 - tail)
    return t * cdf, cdf + t * bell * (1.0 / math.sqrt(2.0 * math.pi))


def put_turned(out_ref, value, pos_ref, count, start):
    turned = value.T
    part = turned.shape[0] // count
    width = turned.shape[1]
    if len(out_ref.shape) == 2:
        out_ref[:, start : start + width] = turned
        return
    for j in range(count):
        out_ref[pos_ref[j], :, start : start + width] = turned[j * part : (j + 1) * part]


def turned_shape(width, rows, count):
    part = width // count
    if part % 16 == 0:
        return (count, part, rows)
    return (width, rows)


def turned_order(turned, pos, count):
    width = turned.shape[0] if turned.ndim == 2 else turned.shape[0] * turned.shape[1]
    rows = turned.shape[-1]
    if turned.ndim == 2:
        shaped = turned.reshape(count, width // count, rows)
        turned = jnp.zeros_like(shaped).at[pos].set(shaped)
    return turned.reshape(width, rows)


def params(limit, **more):
    return pltpu.CompilerParams(vmem_limit_bytes=limit * MB, **more)


def full(shape):
    return pl.BlockSpec(shape, lambda *_: (0,) * len(shape), pipeline_mode=pl.Buffered(1))


SMEM = pl.BlockSpec(memory_space=pltpu.SMEM)


def start_kernel(pos_ref, pos2_ref, rows_ref, vec_ref, x_ref, xt_ref, xt2_ref, *, count):
    width, rows = rows_ref.shape[1], rows_ref.shape[0]
    for start in range(0, rows, PATCHES):
        normed, _ = layer_stats(rows_ref[start : start + PATCHES].astype(F32))
        low = (normed * vec_ref[0:1] + vec_ref[1:2]).astype(BF16)
        x_ref[start : start + PATCHES] = low
        put_turned(xt_ref, low, pos_ref, count, start)
        put_turned(xt2_ref, low, pos2_ref, count, start)


def run_start(pos, pos2, rows, vectors, count):
    r, d = rows.shape
    return pl.pallas_call(
        lambda *refs: start_kernel(*refs, count=count),
        out_shape=(
            jax.ShapeDtypeStruct((r, d), BF16),
            jax.ShapeDtypeStruct(turned_shape(d, r, count), BF16),
            jax.ShapeDtypeStruct(turned_shape(d, r, count), BF16),
        ),
        in_specs=[SMEM, SMEM, pl.BlockSpec(memory_space=pltpu.VMEM), pl.BlockSpec(memory_space=pltpu.VMEM)],
        compiler_params=params(BIG),
    )(pos, pos2, rows, vectors)


def gout_kernel(pos_ref, weight_ref, cot_ref, g_ref, gt_ref, *, count):
    rows = cot_ref.shape[0]
    for index in range(rows // PATCHES):
        start = index * PATCHES
        low = (cot_ref[start : start + PATCHES].astype(F32) * weight_ref[index]).astype(BF16)
        g_ref[start : start + PATCHES] = low
        put_turned(gt_ref, low, pos_ref, count, start)


def run_gout(pos, weight, cot, count):
    r, d = cot.shape
    return pl.pallas_call(
        lambda *refs: gout_kernel(*refs, count=count),
        out_shape=(
            jax.ShapeDtypeStruct((r, d), BF16),
            jax.ShapeDtypeStruct(turned_shape(d, r, count), BF16),
        ),
        in_specs=[SMEM, SMEM, pl.BlockSpec(memory_space=pltpu.VMEM)],
        compiler_params=params(BIG),
    )(pos, weight, cot)


def attend_shard(x, w_ref, saved_ref, probs_ref):
    cols = w_ref.shape[0] // 4
    qkv = mm_nt(x, w_ref[: 3 * cols]).astype(BF16)
    saved_ref[:, : 3 * cols] = qkv
    mixed = []
    for h in range(cols // HEAD_DIM):
        at = h * HEAD_DIM
        q = qkv[:, at : at + HEAD_DIM] * SCALE
        k = qkv[:, cols + at : cols + at + HEAD_DIM]
        v = qkv[:, 2 * cols + at : 2 * cols + at + HEAD_DIM]
        scores = mm_nt(q, k)
        expo = jnp.exp(scores - jnp.max(scores, axis=-1, keepdims=True))
        probs = (expo * (1.0 / jnp.sum(expo, axis=-1, keepdims=True))).astype(BF16)
        probs_ref[h] = probs
        mixed.append(mm(probs, v).astype(BF16))
    mixed = jnp.concatenate(mixed, axis=1)
    saved_ref[:, 3 * cols :] = mixed
    return mm(mixed, w_ref[3 * cols :])


def attn_one_kernel(x_ref, rows_ref, vec_ref, wa_ref, wb_ref, acc_ref, sa_ref, pa_ref, sb_ref, pb_ref):
    x = x_ref[...]
    term = attend_shard(x, wa_ref, sa_ref, pa_ref)
    term += attend_shard(x, wb_ref, sb_ref, pb_ref)
    acc_ref[...] = rows_ref[...].astype(F32) + term + vec_ref[4:5]


def join_halves(low_ref, own_ref, other_ref, whole_ref):
    half = own_ref.shape[0]

    @pl.when(low_ref[0] == 0)
    def _():
        whole_ref[:half] = own_ref[...]
        whole_ref[half:] = other_ref[...]

    @pl.when(low_ref[0] != 0)
    def _():
        whole_ref[:half] = other_ref[...]
        whole_ref[half:] = own_ref[...]


def join_pair(low_ref, halves, wholes):
    @pl.when(pl.program_id(0) == 0)
    def _():
        for (own, other), whole in zip(halves, wholes):
            join_halves(low_ref, own, other, whole)


def attn_two_kernel(
    pos_ref, low_ref, x_ref, acc_ref, vec_ref, ha_ref, ia_ref, hb_ref, ib_ref,
    first_ref, mid_ref, midt_ref, sa_ref, pa_ref, sb_ref, pb_ref, wa_ref, wb_ref, *, count,
):
    join_pair(low_ref, ((ha_ref, ia_ref), (hb_ref, ib_ref)), (wa_ref, wb_ref))
    x = x_ref[...]
    term = attend_shard(x, wa_ref, sa_ref, pa_ref)
    term += attend_shard(x, wb_ref, sb_ref, pb_ref)
    first = acc_ref[...] + term
    first_ref[...] = first
    normed, _ = layer_stats(first)
    low = (normed * vec_ref[2:3] + vec_ref[3:4]).astype(BF16)
    mid_ref[...] = low
    put_turned(midt_ref, low, pos_ref, count, 0)


def image_block(d):
    return pl.BlockSpec((PATCHES, d), lambda i: (i, 0))


def saved_outputs(r, d, heads):
    images = r // PATCHES
    shapes = (
        jax.ShapeDtypeStruct((r, d), BF16),
        jax.ShapeDtypeStruct((images * heads, PATCHES, PATCHES), BF16),
    )
    specs = [image_block(d), pl.BlockSpec((heads, PATCHES, PATCHES), lambda i: (i, 0, 0))]
    return shapes, specs


def cost(micros):
    return pl.CostEstimate(flops=int(micros * 1e9), bytes_accessed=int(micros * 3e6), transcendentals=0)


def run_attn_one(x, rows, vectors, wa, wb):
    r, d = x.shape
    heads = d // 4 // HEAD_DIM
    shapes, specs = saved_outputs(r, d, heads)
    return pl.pallas_call(
        attn_one_kernel,
        grid=(r // PATCHES,),
        out_shape=(jax.ShapeDtypeStruct((r, d), F32),) + shapes * 2,
        in_specs=[image_block(d), image_block(d), full(vectors.shape), full((d, d)), full((d, d))],
        out_specs=[image_block(d)] + specs * 2,
        compiler_params=params(BIG),
        cost_estimate=cost(7),
    )(x, rows, vectors, wa, wb)


def run_attn_two(pos, low, x, acc, vectors, wa, wb, count):
    r, d = x.shape
    heads = d // 4 // HEAD_DIM
    shapes, specs = saved_outputs(r, d, heads)
    tshape = turned_shape(d, r, count)
    tspec = pl.BlockSpec(
        tshape[:-1] + (PATCHES,), lambda i: (0,) * (len(tshape) - 1) + (i,)
    )
    return pl.pallas_call(
        lambda *refs: attn_two_kernel(*refs, count=count),
        grid=(r // PATCHES,),
        out_shape=(
            jax.ShapeDtypeStruct((r, d), F32),
            jax.ShapeDtypeStruct((r, d), BF16),
            jax.ShapeDtypeStruct(tshape, BF16),
        )
        + shapes * 2,
        in_specs=[SMEM, SMEM, image_block(d), image_block(d), full(vectors.shape)]
        + [full((d // 2, d))] * 4,
        out_specs=[image_block(d), image_block(d), tspec] + specs * 2,
        scratch_shapes=[pltpu.VMEM((d, d), BF16)] * 2,
        compiler_params=params(BIG),
        cost_estimate=cost(7),
    )(pos, low, x, acc, vectors, *wa, *wb)


TILES = 3


def ffn_tile(mid_ref, midt_ref, g_ref, gt_ref, w_in, w_down, gi_ref, gd_ref, y_ref, dm_ref):
    pre = mm(mid_ref[...], w_in)
    dact = mm_nt(g_ref[...], w_down)
    activ, slope = gelu_pair(pre)
    activ = activ.astype(BF16)
    dpre = (dact * slope).astype(BF16)
    y_ref[...] += mm(activ, w_down)
    dm_ref[...] += mm_nt(dpre, w_in)
    gd_ref[...] = mm(gt_ref[...], activ).astype(BF16)
    gi_ref[...] = mm(midt_ref[...], dpre).astype(BF16)


def ffn_one_kernel(
    mid_ref, midt_ref, g_ref, gt_ref, ia_ref, da_ref, ib_ref, db_ref,
    y_ref, dm_ref, gia_ref, gda_ref, gib_ref, gdb_ref,
):
    step = pl.program_id(0)

    @pl.when(step == 0)
    def _():
        y_ref[...] = jnp.zeros_like(y_ref)
        dm_ref[...] = jnp.zeros_like(dm_ref)

    @pl.when(step < TILES)
    def _():
        ffn_tile(mid_ref, midt_ref, g_ref, gt_ref, ia_ref[...], da_ref[...], gia_ref, gda_ref, y_ref, dm_ref)

    @pl.when(step >= TILES)
    def _():
        ffn_tile(mid_ref, midt_ref, g_ref, gt_ref, ib_ref[...], db_ref[...], gib_ref, gdb_ref, y_ref, dm_ref)


def joined(low_ref, own_ref, other_ref, axis):
    own, other = own_ref[...], other_ref[...]
    return jnp.where(
        low_ref[0] == 0,
        jnp.concatenate([own, other], axis=axis),
        jnp.concatenate([other, own], axis=axis),
    )


def ffn_two_kernel(
    pos_ref, low_ref, weight_ref, mid_ref, midt_ref, g_ref, gt_ref,
    ia_ref, ja_ref, da_ref, ea_ref, ib_ref, jb_ref, db_ref, eb_ref,
    y_in_ref, dm_in_ref, first_ref, cot_ref, vec_ref,
    out_ref, gf_ref, gfl_ref, gft_ref, sums_ref, gia_ref, gda_ref, gib_ref, gdb_ref,
    y_ref, dm_ref, *, count,
):
    step = pl.program_id(0)

    @pl.when(step == 0)
    def _():
        y_ref[...] = y_in_ref[...]
        dm_ref[...] = dm_in_ref[...]

    @pl.when(step < TILES)
    def _():
        w_in, w_down = joined(low_ref, ia_ref, ja_ref, 0), joined(low_ref, da_ref, ea_ref, 1)
        ffn_tile(mid_ref, midt_ref, g_ref, gt_ref, w_in, w_down, gia_ref, gda_ref, y_ref, dm_ref)

    @pl.when(step >= TILES)
    def _():
        w_in, w_down = joined(low_ref, ib_ref, jb_ref, 0), joined(low_ref, db_ref, eb_ref, 1)
        ffn_tile(mid_ref, midt_ref, g_ref, gt_ref, w_in, w_down, gib_ref, gdb_ref, y_ref, dm_ref)

    @pl.when(step == pl.num_programs(0) - 1)
    def _():
        rows = first_ref.shape[0]
        sums = [0.0, 0.0, 0.0, 0.0]
        chunk = 128
        for start in range(0, rows, chunk):
            here = slice(start, start + chunk)
            first = first_ref[here]
            normed, inverse = layer_stats(first)
            out_ref[here] = (first + y_ref[here] + vec_ref[5:6]).astype(BF16)
            dmid = dm_ref[here]
            gout = cot_ref[here].astype(F32) * weight_ref[start // PATCHES]
            gfirst = gout + norm_back(dmid * vec_ref[2:3], normed, inverse)
            gf_ref[here] = gfirst
            low = gfirst.astype(BF16)
            gfl_ref[here] = low
            put_turned(gft_ref, low, pos_ref, count, start)
            for index, term in enumerate((dmid * normed, dmid, gfirst, gout)):
                sums[index] += jnp.sum(term, axis=0, keepdims=True)
        sums_ref[...] = jnp.concatenate(sums + sums, axis=0)


def ffn_specs(d, parts):
    tile = d // TILES
    cols = lambda f: pl.BlockSpec((d, tile), lambda i: (0, f(i)))
    w_in = lambda f: pl.BlockSpec((d // parts, tile), lambda i: (0, f(i)))
    w_down = lambda f: pl.BlockSpec((tile, d // parts), lambda i: (f(i), 0))
    fa = lambda i: jnp.minimum(i, TILES - 1)
    fb = lambda i: jnp.maximum(i - TILES, 0)
    weights = [kind(f) for f in (fa, fb) for kind in (w_in, w_down) for _ in range(parts)]
    return weights, [cols(fa), cols(fa), cols(fb), cols(fb)]


def run_ffn_one(mid, midt, g, gt, wa, wb):
    r, d = mid.shape
    w_specs, g_specs = ffn_specs(d, 1)
    grad = jax.ShapeDtypeStruct((d, d), BF16)
    return pl.pallas_call(
        ffn_one_kernel,
        grid=(2 * TILES,),
        out_shape=(jax.ShapeDtypeStruct((r, d), F32),) * 2 + (grad,) * 4,
        in_specs=[full((r, d)), full((d, r)), full((r, d)), full((d, r))] + w_specs,
        out_specs=[full((r, d)), full((r, d))] + g_specs,
        compiler_params=params(BIG),
        cost_estimate=cost(13),
    )(mid, midt, g, gt, *wa, *wb)


def run_ffn_two(pos, low, weight, mid, midt, g, gt, wa, wb, y, dm, first, cot, vectors, count):
    r, d = mid.shape
    w_specs, g_specs = ffn_specs(d, 2)
    grad = jax.ShapeDtypeStruct((d, d), BF16)
    tshape = turned_shape(d, r, count)
    return pl.pallas_call(
        lambda *refs: ffn_two_kernel(*refs, count=count),
        grid=(2 * TILES,),
        out_shape=(
            jax.ShapeDtypeStruct((r, d), BF16),
            jax.ShapeDtypeStruct((r, d), F32),
            jax.ShapeDtypeStruct((r, d), BF16),
            jax.ShapeDtypeStruct(tshape, BF16),
            jax.ShapeDtypeStruct((8, d), F32),
        )
        + (grad,) * 4,
        in_specs=[SMEM, SMEM, SMEM, full((r, d)), full((d, r)), full((r, d)), full((d, r))]
        + w_specs
        + [full((r, d))] * 4
        + [full(vectors.shape)],
        out_specs=[full((r, d)), full((r, d)), full((r, d)), full(tshape), full((8, d))] + g_specs,
        scratch_shapes=[pltpu.VMEM((r, d), F32), pltpu.VMEM((r, d), F32)],
        compiler_params=params(BIG),
        cost_estimate=cost(13),
    )(pos, low, weight, mid, midt, g, gt, *wa, *wb, y, dm, first, cot, vectors)


def attend_back_shard(gf, w_ref, saved_ref, probs_ref, keep_ref):
    cols = w_ref.shape[0] // 4
    start = pl.multiple_of(pl.program_id(0) * PATCHES, PATCHES)
    dmix = mm_nt(gf, w_ref[3 * cols :]).astype(BF16)
    dq, dk, dv = [], [], []
    for h in range(cols // HEAD_DIM):
        at = h * HEAD_DIM
        q = saved_ref[:, at : at + HEAD_DIM]
        k = saved_ref[:, cols + at : cols + at + HEAD_DIM]
        v = saved_ref[:, 2 * cols + at : 2 * cols + at + HEAD_DIM]
        do = dmix[:, at : at + HEAD_DIM]
        probs = probs_ref[h]
        dv.append(mm_tn(probs, do).astype(BF16))
        dp = mm_nt(do, v)
        wide = probs.astype(F32)
        ds = (SCALE * wide * (dp - jnp.sum(wide * dp, axis=-1, keepdims=True))).astype(BF16)
        dq.append(mm(ds, k).astype(BF16))
        dk.append(mm_tn(ds, q).astype(BF16))
    dqkv = jnp.concatenate(dq + dk + dv, axis=1)
    keep_ref[pl.ds(start, PATCHES), : 3 * cols] = dqkv
    keep_ref[pl.ds(start, PATCHES), 3 * cols :] = saved_ref[:, 3 * cols :]
    return mm(dqkv, w_ref[: 3 * cols])


def attn_grad(xt_ref, xt2_ref, gft_ref, keep_ref, g_ref, h_ref):
    cols = keep_ref.shape[1] // 4
    g_ref[...] = mm(xt_ref[...], keep_ref[:, : 2 * cols]).astype(BF16)
    h_ref[:, :cols] = mm(xt2_ref[...], keep_ref[:, 2 * cols : 3 * cols]).astype(BF16)
    h_ref[:, cols:] = mm(gft_ref[...], keep_ref[:, 3 * cols :]).astype(BF16)


def back_body(gf_ref, xt_ref, xt2_ref, gft_ref, w_ref, saved_ref, probs_ref, ga_ref, gb_ref, keep_ref):
    term = attend_back_shard(gf_ref[...], w_ref, saved_ref, probs_ref, keep_ref)

    @pl.when(pl.program_id(0) == pl.num_programs(0) - 1)
    def _():
        attn_grad(xt_ref, xt2_ref, gft_ref, keep_ref, ga_ref, gb_ref)

    return term


def back_far_kernel(
    low_ref, gf_ref, xt_ref, xt2_ref, gft_ref, saved_ref, probs_ref, h_ref, i_ref,
    acc_ref, ga_ref, gb_ref, keep_ref, w_ref,
):
    join_pair(low_ref, ((h_ref, i_ref),), (w_ref,))
    term = back_body(gf_ref, xt_ref, xt2_ref, gft_ref, w_ref, saved_ref, probs_ref, ga_ref, gb_ref, keep_ref)
    acc_ref[...] = jnp.zeros_like(acc_ref)
    acc_ref[...] += term


def back_pair_kernel(
    low_ref, gf_ref, xt_ref, xt2_ref, gft_ref, sa_ref, pa_ref, h_ref, i_ref, sb_ref, pb_ref, w_ref, before_ref,
    acc_ref, ga_ref, gb_ref, gc_ref, gd_ref, keep_ref, joined_ref, keep2_ref,
):
    join_pair(low_ref, ((h_ref, i_ref),), (joined_ref,))
    term = back_body(gf_ref, xt_ref, xt2_ref, gft_ref, joined_ref, sa_ref, pa_ref, ga_ref, gb_ref, keep_ref)
    term += back_body(gf_ref, xt_ref, xt2_ref, gft_ref, w_ref, sb_ref, pb_ref, gc_ref, gd_ref, keep2_ref)
    acc_ref[...] = term + before_ref[...]


def back_last_kernel(
    gf_ref, xt_ref, xt2_ref, gft_ref, saved_ref, probs_ref, w_ref, before_ref, rows_ref, gfirst_ref, vec_ref,
    ig_ref, sums_ref, ga_ref, gb_ref, keep_ref,
):
    term = back_body(gf_ref, xt_ref, xt2_ref, gft_ref, w_ref, saved_ref, probs_ref, ga_ref, gb_ref, keep_ref)
    grad_in = before_ref[...] + term
    normed, inverse = layer_stats(rows_ref[...].astype(F32))
    ig_ref[...] = gfirst_ref[...] + norm_back(grad_in * vec_ref[0:1], normed, inverse)
    one = jnp.sum(grad_in * normed, axis=0, keepdims=True)
    two = jnp.sum(grad_in, axis=0, keepdims=True)
    sums = jnp.concatenate([one, two] * 4, axis=0)

    @pl.when(pl.program_id(0) == 0)
    def _():
        sums_ref[...] = sums

    @pl.when(pl.program_id(0) > 0)
    def _():
        sums_ref[...] += sums


def back_call(kernel, ops, specs, outs, out_specs, far, grads=2):
    gfl = ops[1] if far else ops[0]
    r, d = gfl.shape
    heads = d // 4 // HEAD_DIM
    _, saved_specs = saved_outputs(r, d, heads)
    grad = jax.ShapeDtypeStruct((d, d // 2), BF16)
    scratch = [pltpu.VMEM((r, d), BF16)]
    if far:
        scratch += [pltpu.VMEM((d, d), BF16)]
    if grads == 4:
        scratch += [pltpu.VMEM((r, d), BF16)]
    return pl.pallas_call(
        kernel,
        grid=(r // PATCHES,),
        out_shape=tuple(outs) + (grad,) * grads,
        in_specs=([SMEM] if far else []) + [image_block(d)] + [full((d, r))] * 3 + saved_specs + specs,
        out_specs=out_specs + [full((d, d // 2))] * grads,
        scratch_shapes=scratch,
        compiler_params=params(BIG),
        cost_estimate=cost(3 * grads),
    )(*ops)


def run_back_far(low, gfl, xt, xt2, gft, halves, saved):
    r, d = gfl.shape
    return back_call(
        back_far_kernel,
        [low, gfl, xt, xt2, gft, *saved, *halves],
        [full((d // 2, d))] * 2,
        [jax.ShapeDtypeStruct((r, d), F32)], [image_block(d)], True,
    )


def run_back_pair(low, gfl, xt, xt2, gft, halves, saved_a, weight, saved_b, acc):
    r, d = gfl.shape
    _, saved_specs = saved_outputs(r, d, d // 4 // HEAD_DIM)
    return back_call(
        back_pair_kernel,
        [low, gfl, xt, xt2, gft, *saved_a, *halves, *saved_b, weight, acc],
        [full((d // 2, d))] * 2 + saved_specs + [full((d, d)), image_block(d)],
        [jax.ShapeDtypeStruct((r, d), F32)], [image_block(d)], True, 4,
    )


def run_back_last(gfl, xt, xt2, gft, weight, saved, acc, rows, gfirst, vectors):
    r, d = gfl.shape
    return back_call(
        back_last_kernel,
        [gfl, xt, xt2, gft, *saved, weight, acc, rows, gfirst, vectors],
        [full((d, d))] + [image_block(d)] * 3 + [full(vectors.shape)],
        [jax.ShapeDtypeStruct((r, d), F32), jax.ShapeDtypeStruct((8, d), F32)],
        [image_block(d), full((8, d))], False,
    )


def swap(value, axis, bit):
    size = lax.axis_size(axis)
    return lax.ppermute(value, axis, [(i, i ^ bit) for i in range(size)])


def all_sum(value):
    for axis in ("mp", "dp"):
        bit = 1
        while bit < lax.axis_size(axis):
            value = value + swap(value, axis, bit)
            bit *= 2
    return value


def total(terms, rows=slice(None)):
    return sum(term[rows].astype(F32) for term in terms)


def meet(own, partner):
    return own, swap(partner, "mp", 1)


def upper(terms):
    return total(terms, slice(terms[0].shape[0] // 2, None)).astype(BF16)


def fold(terms, bit, sent=None):
    half = terms[0].shape[0] // 2
    back = swap(upper(terms) if sent is None else sent, "dp", 1 << bit)
    return tuple(term[:half] for term in terms) + (back,)


def finish(near, far, order):
    near = near + (swap(total(far).astype(BF16), "mp", 2),)
    for bit in order[1:]:
        near = fold(near, bit)
    return total(near)


CORRECTION = 1.0 - MOMENT_DECAY**STEP


def lamb_step(grad, master, first, second):
    first_new = MOMENT_DECAY * first + (1.0 - MOMENT_DECAY) * grad
    second_new = MOMENT_DECAY * second + (1.0 - MOMENT_DECAY) * grad * grad
    update = (
        first_new * (1.0 / CORRECTION) / (jnp.sqrt(second_new * (1.0 / CORRECTION)) + ADAM_EPS)
        + WEIGHT_DECAY * master
    )
    return first_new, second_new, update


def whole_sum(value):
    return jnp.sum(jnp.sum(value, axis=0, keepdims=True), axis=1, keepdims=True)


def spread(parts, width):
    lane = lax.broadcasted_iota(jnp.int32, (1, width), 1)
    return sum(jnp.where(lane == index, part, 0.0) for index, part in enumerate(parts))


def dense_step_kernel(*refs):
    ins, outs = refs[:8], refs[8:]
    parts = []
    for at in range(2):
        grad, master, first, second = (ref[...] for ref in ins[4 * at : 4 * at + 4])
        first_new, second_new, update = lamb_step(grad, master, first, second)
        for ref, value in zip(outs[3 * at : 3 * at + 3], (first_new, second_new, update)):
            ref[...] = value
        parts += [whole_sum(master * master), whole_sum(update * update)]
    outs[6][...] = spread(parts, outs[6].shape[1])


def run_dense_step(in_parts, down_parts):
    shape = jax.ShapeDtypeStruct(in_parts[0].shape, F32)
    width = in_parts[0].shape[1]
    return pl.pallas_call(
        dense_step_kernel,
        out_shape=(shape,) * 6 + (jax.ShapeDtypeStruct((1, width), F32),),
        compiler_params=params(BIG),
    )(*in_parts, *down_parts)


def attn_step_kernel(
    left_ref, right_ref, qm_ref, qf_ref, qs_ref, om_ref, of_ref, os_ref, sums_a_ref, sums_b_ref, squares_ref,
    qg_ref, qf_out, qs_out, qu_ref, og_ref, of_out, os_out, ou_ref, small_ref,
):
    cols = qm_ref.shape[2]
    left, right = left_ref[...], right_ref[...]
    master_square, update_square = 0.0, 0.0
    for index, grad in enumerate((left[:, :cols], left[:, cols:], right[:, :cols])):
        master = qm_ref[index]
        first_new, second_new, update = lamb_step(grad, master, qf_ref[index], qs_ref[index])
        qg_ref[index] = grad
        qf_out[index] = first_new
        qs_out[index] = second_new
        qu_ref[index] = update
        master_square += whole_sum(master * master)
        update_square += whole_sum(update * update)
    grad = right[:, cols:].T
    master = om_ref[...]
    first_new, second_new, update = lamb_step(grad, master, of_ref[...], os_ref[...])
    og_ref[...] = grad
    of_out[...] = first_new
    os_out[...] = second_new
    ou_ref[...] = update
    dense = squares_ref[...]
    parts = [
        master_square, whole_sum(master * master), dense[:, 0:1], dense[:, 2:3],
        update_square, whole_sum(update * update), dense[:, 1:2], dense[:, 3:4],
    ]
    width = small_ref.shape[1]
    small_ref[...] = jnp.concatenate(
        [sums_a_ref[0:2], sums_b_ref[0:4], spread(parts, width), jnp.zeros((1, width), F32)], axis=0
    )


def run_attn_step(left, right, qkv, out, sums_a, sums_b, squares):
    q, o = jax.ShapeDtypeStruct(qkv[0].shape, F32), jax.ShapeDtypeStruct(out[0].shape, F32)
    return pl.pallas_call(
        attn_step_kernel,
        out_shape=(q,) * 4 + (o,) * 4 + (jax.ShapeDtypeStruct(sums_a.shape, F32),),
        compiler_params=params(BIG),
    )(left, right, *qkv, *out, sums_a, sums_b, squares)


def final_kernel(*refs):
    small_ref, vec_ref, vf_ref, vs_ref = refs[:4]
    masters, updates, new = refs[4:8], refs[8:12], refs[12:16]
    vg_out, vf_out, vs_out, v_out, norms_ref = refs[16:]
    norms = jnp.sqrt(small_ref[6:7])
    lane = lax.broadcasted_iota(jnp.int32, norms_ref.shape, 1)
    row = lax.broadcasted_iota(jnp.int32, norms_ref.shape, 0)
    table = jnp.zeros(norms_ref.shape, F32)
    for index in range(4):
        weight, update = norms[:, index : index + 1], norms[:, 4 + index : 5 + index]
        trust = weight / (update + ADAM_EPS)
        new[index][...] = masters[index][...] - LEARN_RATE * trust * updates[index][...]
        for at, value in enumerate((weight, update, trust)):
            table = jnp.where((lane == index) & (row == at), value, table)
    norms_ref[...] = table
    grad = small_ref[0:6]
    first_new = MOMENT_DECAY * vf_ref[...] + (1.0 - MOMENT_DECAY) * grad
    second_new = MOMENT_DECAY * vs_ref[...] + (1.0 - MOMENT_DECAY) * grad * grad
    vg_out[...] = grad
    vf_out[...] = first_new
    vs_out[...] = second_new
    v_out[...] = vec_ref[...] - LEARN_RATE * (first_new * (1.0 / CORRECTION)) / (
        jnp.sqrt(second_new * (1.0 / CORRECTION)) + ADAM_EPS
    )


def run_final(small, vectors, vec_first, vec_second, masters, updates):
    shape = lambda value: jax.ShapeDtypeStruct(value.shape, F32)
    flat = lambda value: value.reshape(-1, value.shape[-1])
    outs = pl.pallas_call(
        final_kernel,
        out_shape=tuple(shape(flat(m)) for m in masters)
        + (shape(vectors),) * 4
        + (jax.ShapeDtypeStruct((3, 4), F32),),
        compiler_params=params(BIG),
    )(small, vectors, vec_first, vec_second, *(flat(m) for m in masters), *(flat(u) for u in updates))
    new = [value.reshape(m.shape) for value, m in zip(outs[:4], masters)]
    return new, outs[4:]


def after(value, *others):
    return lax.optimization_barrier((value,) + others)[0]


def shards(
    rows,
    cotangent,
    group_ids,
    qkv_weight,
    out_weight,
    in_weight,
    down_weight,
    vectors,
    qkv_master,
    qkv_first,
    qkv_second,
    out_master,
    out_first,
    out_second,
    in_master,
    in_first,
    in_second,
    down_master,
    down_first,
    down_second,
    vec_first,
    vec_second,
):
    count = lax.axis_size("dp")
    width = rows.shape[1]
    half = width // 2
    nbits = count.bit_length() - 1
    me = lax.axis_index("dp").astype(jnp.int32)
    rel = jnp.arange(count, dtype=jnp.int32) ^ me
    order1 = tuple(range(nbits))
    order2 = (1, 0) + order1[2:]
    pos, pos2 = (
        sum(((rel >> bit) & 1) << (nbits - 1 - place) for place, bit in enumerate(order))
        for order in (order1, order2)
    )
    low = (me & 1).reshape(1)

    onehot = (group_ids[:, None] == jnp.arange(GROUPS, dtype=jnp.int32)[None, :]).astype(F32)
    counts = jnp.sum(onehot, axis=0)
    counts = counts + swap(counts, "mp", 2)

    attn_w = jnp.concatenate(
        [jnp.swapaxes(qkv_weight, 1, 2).reshape(-1, width), out_weight], axis=0
    )
    pieces = [
        lax.dynamic_slice_in_dim(weight, low[0] * half, half, axis)
        for weight, axis in ((attn_w, 0), (in_weight, 0), (down_weight, 1))
    ]
    counts, *pieces = lax.optimization_barrier((counts, *pieces))
    attn_far, in_far, down_far = (swap(piece, "mp", 2) for piece in pieces)
    attn_one, in_one, down_one = (swap(weight, "mp", 1) for weight in (attn_w, in_weight, down_weight))
    counts = counts + swap(counts, "dp", 1)
    attn_two = (attn_far, swap(after(attn_far, counts), "dp", 1))
    in_two = (in_far, swap(in_far, "dp", 1))
    down_two = (down_far, swap(down_far, "dp", 1))
    attn_three, in_three, down_three = (
        tuple(swap(piece, "mp", 1) for piece in pieces) for pieces in (attn_two, in_two, down_two)
    )
    counts = counts + swap(counts, "mp", 1)
    for bit in order1[1:]:
        counts = counts + swap(counts, "dp", 1 << bit)
    image_weight = jnp.sqrt(jnp.sum(counts) / (GROUPS * jnp.sum(onehot * counts, axis=1)))

    x, xt, xt2 = run_start(pos, pos2, rows, vectors, count)
    xt, xt2 = turned_order(xt, pos, count), turned_order(xt2, pos2, count)
    gout, goutt = run_gout(pos2, image_weight, cotangent, count)
    goutt = turned_order(goutt, pos2, count)
    acc, s1, p1, s0, p0 = run_attn_one(after(x, in_far), rows, vectors, attn_one, attn_w)
    first, mid, midt, s3, p3, s2, p2 = run_attn_two(
        pos, low, x, acc, vectors, attn_three, attn_two, count
    )
    midt = turned_order(midt, pos, count)
    y, dm, gi1, gd1, gi0, gd0 = run_ffn_one(
        after(mid, in_two[1], down_far), midt, gout, goutt, (in_one, down_one), (in_weight, down_weight)
    )
    gi1, gd1, _ = lax.optimization_barrier((gi1, gd1, down_two[1]))
    in_near, down_near = meet(gi0, gi1), meet(gd0, gd1)
    y, in_sent, down_sent = lax.optimization_barrier((y, upper(in_near), upper(down_near)))
    in_near, down_near = fold(in_near, order1[0], in_sent), fold(down_near, order2[0], down_sent)
    out_rows, gfirst, gfl, gft, sums_b, gi3, gd3, gi2, gd2 = run_ffn_two(
        pos2, low, image_weight, mid, midt, gout, goutt,
        in_three + down_three, in_two + down_two, y, dm, first, cotangent, vectors, count,
    )
    gft = turned_order(gft, pos2, count)
    gi3, gd3, _, _ = lax.optimization_barrier((gi3, gd3, in_near[-1], down_near[-1]))
    in_far, down_far = meet(gi2, gi3), meet(gd2, gd3)
    gin, gl3, gr3 = run_back_far(low, gfl, xt, xt2, gft, attn_three, (s3, p3))
    gin, in_sent, down_sent = lax.optimization_barrier((gin, upper(in_far), upper(down_far)))
    in_far, down_far = fold(in_far, order1[0], in_sent), fold(down_far, order2[0], down_sent)
    gin, gl2, gr2, gl1, gr1 = run_back_pair(
        low, gfl, xt, xt2, gft, attn_two, (s2, p2), attn_one, (s1, p1), gin
    )
    left_far, right_far = meet(gl2, gl3), meet(gr2, gr3)
    gin, left_sent, right_sent, _, _ = lax.optimization_barrier(
        (gin, upper(left_far), upper(right_far), in_far[-1], down_far[-1])
    )
    left_far, right_far = fold(left_far, order1[0], left_sent), fold(right_far, order2[0], right_sent)
    input_grad, sums_a, gl0, gr0 = run_back_last(
        gfl, xt, xt2, gft, attn_w, (s0, p0), gin, rows, gfirst, vectors
    )
    left_near, right_near = meet(gl0, gl1), meet(gr0, gr1)
    left_near, right_near = fold(left_near, order1[0]), fold(right_near, order2[0])
    in_grad, down_grad = finish(in_near, in_far, order1), finish(down_near, down_far, order2)
    left, right = finish(left_near, left_far, order1), finish(right_near, right_far, order2)

    down_state = (down_master.T, down_first.T, down_second.T)
    in_fn, in_sn, in_up, down_fn, down_sn, down_up, squares = run_dense_step(
        (in_grad, in_master, in_first, in_second), (down_grad,) + down_state
    )
    qkv_grad, qkv_fn, qkv_sn, qkv_up, out_grad, out_fn, out_sn, out_up, small = run_attn_step(
        left, right, (qkv_master, qkv_first, qkv_second), (out_master, out_first, out_second),
        sums_a, sums_b, squares,
    )
    new, vec_outs = run_final(
        all_sum(small), vectors, vec_first, vec_second,
        (qkv_master, out_master, in_master, down_state[0]), (qkv_up, out_up, in_up, down_up),
    )
    return (
        out_rows,
        input_grad,
        qkv_grad,
        out_grad,
        in_grad,
        down_grad.T,
        qkv_fn,
        qkv_sn,
        new[0],
        out_fn,
        out_sn,
        new[1],
        in_fn,
        in_sn,
        new[2],
        down_fn.T,
        down_sn.T,
        new[3].T,
    ) + tuple(vec_outs)


def solution(mesh):
    rows = P(("dp", "mp"), None)
    qkv_state = P(None, "dp", "mp")
    out_state = P("mp", "dp")
    in_state = P("dp", "mp")
    in_specs = (
        (rows, rows, P(("dp", "mp")), P(None, None, "mp"), P("mp", None), P(None, "mp"), P("mp", None), P())
        + (qkv_state,) * 3
        + (out_state,) * 3
        + (in_state,) * 3
        + (out_state,) * 3
        + (P(), P())
    )
    out_specs = (
        (rows, rows, qkv_state, out_state, in_state, out_state)
        + (qkv_state,) * 3
        + (out_state,) * 3
        + (in_state,) * 3
        + (out_state,) * 3
        + (P(),) * 5
    )
    return jax.shard_map(shards, mesh=mesh, in_specs=in_specs, out_specs=out_specs, check_vma=False)
```

```python
import math

import jax
import jax.numpy as jnp
from jax import lax
from jax.experimental import pallas as pl
from jax.experimental.pallas import tpu as pltpu
from jax.sharding import PartitionSpec as P

HEAD_DIM = 64
PATCHES = 256
GROUPS = 8
STEP = 5

NORM_EPS = 1e-06
ADAM_EPS = 1e-06
MOMENT_DECAY = 0.5
LEARN_RATE = 0.5
WEIGHT_DECAY = 0.01
SCALE = HEAD_DIM ** (-0.5)

F32 = jnp.float32
BF16 = jnp.bfloat16
MB = 1024 * 1024
BIG = 16


def mm(left, right):
    return jnp.dot(left, right, preferred_element_type=F32)


def mm_nt(left, right):
    return lax.dot_general(left, right, (((1,), (1,)), ((), ())), preferred_element_type=F32)


def mm_tn(left, right):
    return lax.dot_general(left, right, (((0,), (0,)), ((), ())), preferred_element_type=F32)


def layer_stats(values):
    center = values - jnp.mean(values, axis=-1, keepdims=True)
    inverse = lax.rsqrt(jnp.mean(center * center, axis=-1, keepdims=True) + NORM_EPS)
    return center * inverse, inverse


def norm_back(grad_normed, normed, inverse):
    return inverse * (
        grad_normed
        - jnp.mean(grad_normed, axis=-1, keepdims=True)
        - normed * jnp.mean(grad_normed * normed, axis=-1, keepdims=True)
    )


def gelu_pair(t):
    size = jnp.abs(t) * (2.0**-0.5)
    k = 1.0 / (1.0 + 0.3275911 * size)
    bell = jnp.exp(-size * size)
    poly = k * (
        0.254829592
        + k * (-0.284496736 + k * (1.421413741 + k * (-1.453152027 + k * 1.061405429)))
    )
    tail = 0.5 * poly * bell
    cdf = jnp.where(t < 0, tail, 1.0 - tail)
    return t * cdf, cdf + t * bell * (1.0 / math.sqrt(2.0 * math.pi))


def put_turned(out_ref, value, pos_ref, count, start):
    turned = value.T
    part = turned.shape[0] // count
    width = turned.shape[1]
    if len(out_ref.shape) == 2:
        out_ref[:, start : start + width] = turned
        return
    for j in range(count):
        out_ref[pos_ref[j], :, start : start + width] = turned[j * part : (j + 1) * part]


def turned_shape(width, rows, count):
    part = width // count
    if part % 16 == 0:
        return (count, part, rows)
    return (width, rows)


def turned_order(turned, pos, count):
    width = turned.shape[0] if turned.ndim == 2 else turned.shape[0] * turned.shape[1]
    rows = turned.shape[-1]
    if turned.ndim == 2:
        shaped = turned.reshape(count, width // count, rows)
        turned = jnp.zeros_like(shaped).at[pos].set(shaped)
    return turned.reshape(width, rows)


def params(limit, **more):
    return pltpu.CompilerParams(vmem_limit_bytes=limit * MB, **more)


def full(shape):
    return pl.BlockSpec(shape, lambda *_: (0,) * len(shape), pipeline_mode=pl.Buffered(1))


SMEM = pl.BlockSpec(memory_space=pltpu.SMEM)


def start_kernel(pos_ref, pos2_ref, rows_ref, vec_ref, x_ref, xt_ref, xt2_ref, *, count):
    width, rows = rows_ref.shape[1], rows_ref.shape[0]
    for start in range(0, rows, PATCHES):
        normed, _ = layer_stats(rows_ref[start : start + PATCHES].astype(F32))
        low = (normed * vec_ref[0:1] + vec_ref[1:2]).astype(BF16)
        x_ref[start : start + PATCHES] = low
        put_turned(xt_ref, low, pos_ref, count, start)
        put_turned(xt2_ref, low, pos2_ref, count, start)


def run_start(pos, pos2, rows, vectors, count):
    r, d = rows.shape
    return pl.pallas_call(
        lambda *refs: start_kernel(*refs, count=count),
        out_shape=(
            jax.ShapeDtypeStruct((r, d), BF16),
            jax.ShapeDtypeStruct(turned_shape(d, r, count), BF16),
            jax.ShapeDtypeStruct(turned_shape(d, r, count), BF16),
        ),
        in_specs=[SMEM, SMEM, pl.BlockSpec(memory_space=pltpu.VMEM), pl.BlockSpec(memory_space=pltpu.VMEM)],
        compiler_params=params(BIG),
    )(pos, pos2, rows, vectors)


def gout_kernel(pos_ref, weight_ref, cot_ref, g_ref, gt_ref, *, count):
    rows = cot_ref.shape[0]
    for index in range(rows // PATCHES):
        start = index * PATCHES
        low = (cot_ref[start : start + PATCHES].astype(F32) * weight_ref[index]).astype(BF16)
        g_ref[start : start + PATCHES] = low
        put_turned(gt_ref, low, pos_ref, count, start)


def run_gout(pos, weight, cot, count):
    r, d = cot.shape
    return pl.pallas_call(
        lambda *refs: gout_kernel(*refs, count=count),
        out_shape=(
            jax.ShapeDtypeStruct((r, d), BF16),
            jax.ShapeDtypeStruct(turned_shape(d, r, count), BF16),
        ),
        in_specs=[SMEM, SMEM, pl.BlockSpec(memory_space=pltpu.VMEM)],
        compiler_params=params(BIG),
    )(pos, weight, cot)


def attend_shard(x, w_ref, saved_ref, probs_ref):
    cols = w_ref.shape[0] // 4
    qkv = mm_nt(x, w_ref[: 3 * cols]).astype(BF16)
    saved_ref[:, : 3 * cols] = qkv
    mixed = []
    for h in range(cols // HEAD_DIM):
        at = h * HEAD_DIM
        q = qkv[:, at : at + HEAD_DIM] * SCALE
        k = qkv[:, cols + at : cols + at + HEAD_DIM]
        v = qkv[:, 2 * cols + at : 2 * cols + at + HEAD_DIM]
        scores = mm_nt(q, k)
        expo = jnp.exp(scores - jnp.max(scores, axis=-1, keepdims=True))
        probs = (expo * (1.0 / jnp.sum(expo, axis=-1, keepdims=True))).astype(BF16)
        probs_ref[h] = probs
        mixed.append(mm(probs, v).astype(BF16))
    mixed = jnp.concatenate(mixed, axis=1)
    saved_ref[:, 3 * cols :] = mixed
    return mm(mixed, w_ref[3 * cols :])


def attn_one_kernel(x_ref, rows_ref, vec_ref, wa_ref, wb_ref, acc_ref, sa_ref, pa_ref, sb_ref, pb_ref):
    x = x_ref[...]
    term = attend_shard(x, wa_ref, sa_ref, pa_ref)
    term += attend_shard(x, wb_ref, sb_ref, pb_ref)
    acc_ref[...] = rows_ref[...].astype(F32) + term + vec_ref[4:5]


def join_halves(low_ref, own_ref, other_ref, whole_ref):
    half = own_ref.shape[0]

    @pl.when(low_ref[0] == 0)
    def _():
        whole_ref[:half] = own_ref[...]
        whole_ref[half:] = other_ref[...]

    @pl.when(low_ref[0] != 0)
    def _():
        whole_ref[:half] = other_ref[...]
        whole_ref[half:] = own_ref[...]


def join_pair(low_ref, halves, wholes):
    @pl.when(pl.program_id(0) == 0)
    def _():
        for (own, other), whole in zip(halves, wholes):
            join_halves(low_ref, own, other, whole)


def attn_two_kernel(
    pos_ref, low_ref, x_ref, acc_ref, vec_ref, ha_ref, ia_ref, hb_ref, ib_ref,
    first_ref, mid_ref, midt_ref, sa_ref, pa_ref, sb_ref, pb_ref, wa_ref, wb_ref, *, count,
):
    join_pair(low_ref, ((ha_ref, ia_ref), (hb_ref, ib_ref)), (wa_ref, wb_ref))
    x = x_ref[...]
    term = attend_shard(x, wa_ref, sa_ref, pa_ref)
    term += attend_shard(x, wb_ref, sb_ref, pb_ref)
    first = acc_ref[...] + term
    first_ref[...] = first
    normed, _ = layer_stats(first)
    low = (normed * vec_ref[2:3] + vec_ref[3:4]).astype(BF16)
    mid_ref[...] = low
    put_turned(midt_ref, low, pos_ref, count, 0)


def image_block(d):
    return pl.BlockSpec((PATCHES, d), lambda i: (i, 0))


def saved_outputs(r, d, heads):
    images = r // PATCHES
    shapes = (
        jax.ShapeDtypeStruct((r, d), BF16),
        jax.ShapeDtypeStruct((images * heads, PATCHES, PATCHES), BF16),
    )
    specs = [image_block(d), pl.BlockSpec((heads, PATCHES, PATCHES), lambda i: (i, 0, 0))]
    return shapes, specs


def cost(micros):
    return pl.CostEstimate(flops=int(micros * 10 * 1e9), bytes_accessed=int(micros * 10 * 3e6), transcendentals=0)


def run_attn_one(x, rows, vectors, wa, wb):
    r, d = x.shape
    heads = d // 4 // HEAD_DIM
    shapes, specs = saved_outputs(r, d, heads)
    return pl.pallas_call(
        attn_one_kernel,
        grid=(r // PATCHES,),
        out_shape=(jax.ShapeDtypeStruct((r, d), F32),) + shapes * 2,
        in_specs=[image_block(d), image_block(d), full(vectors.shape), full((d, d)), full((d, d))],
        out_specs=[image_block(d)] + specs * 2,
        compiler_params=params(BIG),
        cost_estimate=cost(7),
    )(x, rows, vectors, wa, wb)


def run_attn_two(pos, low, x, acc, vectors, wa, wb, count):
    r, d = x.shape
    heads = d // 4 // HEAD_DIM
    shapes, specs = saved_outputs(r, d, heads)
    tshape = turned_shape(d, r, count)
    tspec = pl.BlockSpec(
        tshape[:-1] + (PATCHES,), lambda i: (0,) * (len(tshape) - 1) + (i,)
    )
    return pl.pallas_call(
        lambda *refs: attn_two_kernel(*refs, count=count),
        grid=(r // PATCHES,),
        out_shape=(
            jax.ShapeDtypeStruct((r, d), F32),
            jax.ShapeDtypeStruct((r, d), BF16),
            jax.ShapeDtypeStruct(tshape, BF16),
        )
        + shapes * 2,
        in_specs=[SMEM, SMEM, image_block(d), image_block(d), full(vectors.shape)]
        + [full((d // 2, d))] * 4,
        out_specs=[image_block(d), image_block(d), tspec] + specs * 2,
        scratch_shapes=[pltpu.VMEM((d, d), BF16)] * 2,
        compiler_params=params(BIG),
        cost_estimate=cost(7),
    )(pos, low, x, acc, vectors, *wa, *wb)


TILES = 3


def ffn_tile(mid_ref, midt_ref, g_ref, gt_ref, w_in, w_down, gi_ref, gd_ref, y_ref, dm_ref):
    pre = mm(mid_ref[...], w_in)
    dact = mm_nt(g_ref[...], w_down)
    activ, slope = gelu_pair(pre)
    activ = activ.astype(BF16)
    dpre = (dact * slope).astype(BF16)
    y_ref[...] += mm(activ, w_down)
    dm_ref[...] += mm_nt(dpre, w_in)
    gd_ref[...] = mm(gt_ref[...], activ).astype(BF16)
    gi_ref[...] = mm(midt_ref[...], dpre).astype(BF16)


def joined(low_ref, own_ref, other_ref, axis):
    own, other = own_ref[...], other_ref[...]
    return jnp.where(
        low_ref[0] == 0,
        jnp.concatenate([own, other], axis=axis),
        jnp.concatenate([other, own], axis=axis),
    )


def ffn_near_kernel(mid_ref, midt_ref, g_ref, gt_ref, in_ref, down_ref, *rest):
    *before, y_ref, dm_ref, gi_ref, gd_ref = rest

    @pl.when(pl.program_id(0) == 0)
    def _():
        y_ref[...] = before[0][...] if before else jnp.zeros_like(y_ref)
        dm_ref[...] = before[1][...] if before else jnp.zeros_like(dm_ref)

    ffn_tile(mid_ref, midt_ref, g_ref, gt_ref, in_ref[...], down_ref[...], gi_ref, gd_ref, y_ref, dm_ref)


def ffn_far_kernel(
    low_ref, mid_ref, midt_ref, g_ref, gt_ref, ia_ref, ib_ref, da_ref, db_ref, y_in_ref, dm_in_ref,
    y_ref, dm_ref, gi_ref, gd_ref,
):
    @pl.when(pl.program_id(0) == 0)
    def _():
        y_ref[...] = y_in_ref[...]
        dm_ref[...] = dm_in_ref[...]

    w_in, w_down = joined(low_ref, ia_ref, ib_ref, 0), joined(low_ref, da_ref, db_ref, 1)
    ffn_tile(mid_ref, midt_ref, g_ref, gt_ref, w_in, w_down, gi_ref, gd_ref, y_ref, dm_ref)


def ffn_last_kernel(
    pos_ref, low_ref, weight_ref, mid_ref, midt_ref, g_ref, gt_ref, ia_ref, ib_ref, da_ref, db_ref,
    y_in_ref, dm_in_ref, first_ref, cot_ref, vec_ref,
    out_ref, gf_ref, gfl_ref, gft_ref, sums_ref, gi_ref, gd_ref, y_ref, dm_ref, *, count,
):
    ffn_far_kernel(
        low_ref, mid_ref, midt_ref, g_ref, gt_ref, ia_ref, ib_ref, da_ref, db_ref, y_in_ref, dm_in_ref,
        y_ref, dm_ref, gi_ref, gd_ref,
    )

    @pl.when(pl.program_id(0) == pl.num_programs(0) - 1)
    def _():
        rows = first_ref.shape[0]
        sums = [0.0, 0.0, 0.0, 0.0]
        chunk = 128
        for start in range(0, rows, chunk):
            here = slice(start, start + chunk)
            first = first_ref[here]
            normed, inverse = layer_stats(first)
            out_ref[here] = (first + y_ref[here] + vec_ref[5:6]).astype(BF16)
            dmid = dm_ref[here]
            gout = cot_ref[here].astype(F32) * weight_ref[start // PATCHES]
            gfirst = gout + norm_back(dmid * vec_ref[2:3], normed, inverse)
            gf_ref[here] = gfirst
            low = gfirst.astype(BF16)
            gfl_ref[here] = low
            put_turned(gft_ref, low, pos_ref, count, start)
            for index, term in enumerate((dmid * normed, dmid, gfirst, gout)):
                sums[index] += jnp.sum(term, axis=0, keepdims=True)
        sums_ref[...] = jnp.concatenate(sums + sums, axis=0)


def ffn_specs(d, parts):
    tile = d // TILES
    cols = lambda rows: pl.BlockSpec((rows, tile), lambda i: (0, i))
    w_down = pl.BlockSpec((tile, d // parts), lambda i: (i, 0))
    return [cols(d // parts)] * parts + [w_down] * parts, [cols(d)] * 2


def run_ffn_near(mid, midt, g, gt, w_in, w_down, *before):
    r, d = mid.shape
    w_specs, g_specs = ffn_specs(d, 1)
    grad = jax.ShapeDtypeStruct((d, d), BF16)
    return pl.pallas_call(
        ffn_near_kernel,
        grid=(TILES,),
        out_shape=(jax.ShapeDtypeStruct((r, d), F32),) * 2 + (grad,) * 2,
        in_specs=[full((r, d)), full((d, r)), full((r, d)), full((d, r))] + w_specs + [full((r, d))] * len(before),
        out_specs=[full((r, d))] * 2 + g_specs,
        compiler_params=params(BIG),
        cost_estimate=cost(6),
    )(mid, midt, g, gt, w_in, w_down, *before)


def run_ffn_far(low, mid, midt, g, gt, w_in, w_down, y, dm):
    r, d = mid.shape
    w_specs, g_specs = ffn_specs(d, 2)
    grad = jax.ShapeDtypeStruct((d, d), BF16)
    return pl.pallas_call(
        ffn_far_kernel,
        grid=(TILES,),
        out_shape=(jax.ShapeDtypeStruct((r, d), F32),) * 2 + (grad,) * 2,
        in_specs=[SMEM, full((r, d)), full((d, r)), full((r, d)), full((d, r))] + w_specs + [full((r, d))] * 2,
        out_specs=[full((r, d))] * 2 + g_specs,
        compiler_params=params(BIG),
        cost_estimate=cost(6),
    )(low, mid, midt, g, gt, *w_in, *w_down, y, dm)


def run_ffn_last(pos, low, weight, mid, midt, g, gt, w_in, w_down, y, dm, first, cot, vectors, count):
    r, d = mid.shape
    w_specs, g_specs = ffn_specs(d, 2)
    grad = jax.ShapeDtypeStruct((d, d), BF16)
    tshape = turned_shape(d, r, count)
    return pl.pallas_call(
        lambda *refs: ffn_last_kernel(*refs, count=count),
        grid=(TILES,),
        out_shape=(
            jax.ShapeDtypeStruct((r, d), BF16),
            jax.ShapeDtypeStruct((r, d), F32),
            jax.ShapeDtypeStruct((r, d), BF16),
            jax.ShapeDtypeStruct(tshape, BF16),
            jax.ShapeDtypeStruct((8, d), F32),
        )
        + (grad,) * 2,
        in_specs=[SMEM, SMEM, SMEM, full((r, d)), full((d, r)), full((r, d)), full((d, r))]
        + w_specs
        + [full((r, d))] * 4
        + [full(vectors.shape)],
        out_specs=[full((r, d)), full((r, d)), full((r, d)), full(tshape), full((8, d))] + g_specs,
        scratch_shapes=[pltpu.VMEM((r, d), F32)] * 2,
        compiler_params=params(BIG),
        cost_estimate=cost(8),
    )(pos, low, weight, mid, midt, g, gt, *w_in, *w_down, y, dm, first, cot, vectors)


def attend_back_shard(gf, w_ref, saved_ref, probs_ref, keep_ref):
    cols = w_ref.shape[0] // 4
    start = pl.multiple_of(pl.program_id(0) * PATCHES, PATCHES)
    dmix = mm_nt(gf, w_ref[3 * cols :]).astype(BF16)
    dq, dk, dv = [], [], []
    for h in range(cols // HEAD_DIM):
        at = h * HEAD_DIM
        q = saved_ref[:, at : at + HEAD_DIM]
        k = saved_ref[:, cols + at : cols + at + HEAD_DIM]
        v = saved_ref[:, 2 * cols + at : 2 * cols + at + HEAD_DIM]
        do = dmix[:, at : at + HEAD_DIM]
        probs = probs_ref[h]
        dv.append(mm_tn(probs, do).astype(BF16))
        dp = mm_nt(do, v)
        wide = probs.astype(F32)
        ds = (SCALE * wide * (dp - jnp.sum(wide * dp, axis=-1, keepdims=True))).astype(BF16)
        dq.append(mm(ds, k).astype(BF16))
        dk.append(mm_tn(ds, q).astype(BF16))
    dqkv = jnp.concatenate(dq + dk + dv, axis=1)
    keep_ref[pl.ds(start, PATCHES), : 3 * cols] = dqkv
    keep_ref[pl.ds(start, PATCHES), 3 * cols :] = saved_ref[:, 3 * cols :]
    return mm(dqkv, w_ref[: 3 * cols])


def attn_grad(xt_ref, xt2_ref, gft_ref, keep_ref, g_ref):
    cols = keep_ref.shape[1] // 4
    g_ref[:, : 2 * cols] = mm(xt_ref[...], keep_ref[:, : 2 * cols]).astype(BF16)
    g_ref[:, 2 * cols : 3 * cols] = mm(xt2_ref[...], keep_ref[:, 2 * cols : 3 * cols]).astype(BF16)
    g_ref[:, 3 * cols :] = mm(gft_ref[...], keep_ref[:, 3 * cols :]).astype(BF16)


def back_body(gf_ref, xt_ref, xt2_ref, gft_ref, w_ref, saved_ref, probs_ref, g_ref, keep_ref):
    term = attend_back_shard(gf_ref[...], w_ref, saved_ref, probs_ref, keep_ref)

    @pl.when(pl.program_id(0) == pl.num_programs(0) - 1)
    def _():
        attn_grad(xt_ref, xt2_ref, gft_ref, keep_ref, g_ref)

    return term


def back_far_kernel(
    low_ref, gf_ref, xt_ref, xt2_ref, gft_ref, saved_ref, probs_ref, h_ref, i_ref, *rest
):
    *before, acc_ref, g_ref, keep_ref, w_ref = rest
    join_pair(low_ref, ((h_ref, i_ref),), (w_ref,))
    term = back_body(gf_ref, xt_ref, xt2_ref, gft_ref, w_ref, saved_ref, probs_ref, g_ref, keep_ref)
    if before:
        acc_ref[...] = term + before[0][...]
    else:
        acc_ref[...] = jnp.zeros_like(acc_ref)
        acc_ref[...] += term


def back_near_kernel(
    gf_ref, xt_ref, xt2_ref, gft_ref, saved_ref, probs_ref, w_ref, before_ref, acc_ref, g_ref, keep_ref
):
    term = back_body(gf_ref, xt_ref, xt2_ref, gft_ref, w_ref, saved_ref, probs_ref, g_ref, keep_ref)
    acc_ref[...] = term + before_ref[...]


def back_last_kernel(
    gf_ref, xt_ref, xt2_ref, gft_ref, saved_ref, probs_ref, w_ref, before_ref, rows_ref, gfirst_ref, vec_ref,
    ig_ref, sums_ref, g_ref, keep_ref,
):
    term = back_body(gf_ref, xt_ref, xt2_ref, gft_ref, w_ref, saved_ref, probs_ref, g_ref, keep_ref)
    grad_in = before_ref[...] + term
    normed, inverse = layer_stats(rows_ref[...].astype(F32))
    ig_ref[...] = gfirst_ref[...] + norm_back(grad_in * vec_ref[0:1], normed, inverse)
    one = jnp.sum(grad_in * normed, axis=0, keepdims=True)
    two = jnp.sum(grad_in, axis=0, keepdims=True)
    sums = jnp.concatenate([one, two] * 4, axis=0)

    @pl.when(pl.program_id(0) == 0)
    def _():
        sums_ref[...] = sums

    @pl.when(pl.program_id(0) > 0)
    def _():
        sums_ref[...] += sums


def back_call(kernel, ops, specs, outs, out_specs, far):
    gfl = ops[1] if far else ops[0]
    r, d = gfl.shape
    heads = d // 4 // HEAD_DIM
    _, saved_specs = saved_outputs(r, d, heads)
    keep, whole = pltpu.VMEM((r, d), BF16), pltpu.VMEM((d, d), BF16)
    return pl.pallas_call(
        kernel,
        grid=(r // PATCHES,),
        out_shape=tuple(outs) + (jax.ShapeDtypeStruct((d, d), BF16),),
        in_specs=([SMEM] if far else []) + [image_block(d)] + [full((d, r))] * 3 + saved_specs + specs,
        out_specs=out_specs + [full((d, d))],
        scratch_shapes=[keep, whole] if far else [keep],
        compiler_params=params(BIG),
        cost_estimate=cost(6),
    )(*ops)


def run_back_far(low, gfl, xt, xt2, gft, halves, saved, *acc):
    r, d = gfl.shape
    return back_call(
        back_far_kernel,
        [low, gfl, xt, xt2, gft, *saved, *halves, *acc],
        [full((d // 2, d))] * 2 + [image_block(d)] * len(acc),
        [jax.ShapeDtypeStruct((r, d), F32)], [image_block(d)], True,
    )


def run_back_near(gfl, xt, xt2, gft, weight, saved, acc):
    r, d = gfl.shape
    return back_call(
        back_near_kernel,
        [gfl, xt, xt2, gft, *saved, weight, acc],
        [full((d, d)), image_block(d)],
        [jax.ShapeDtypeStruct((r, d), F32)], [image_block(d)], False,
    )


def run_back_last(gfl, xt, xt2, gft, weight, saved, acc, rows, gfirst, vectors):
    r, d = gfl.shape
    return back_call(
        back_last_kernel,
        [gfl, xt, xt2, gft, *saved, weight, acc, rows, gfirst, vectors],
        [full((d, d))] + [image_block(d)] * 3 + [full(vectors.shape)],
        [jax.ShapeDtypeStruct((r, d), F32), jax.ShapeDtypeStruct((8, d), F32)],
        [image_block(d), full((8, d))], False,
    )


def swap(value, axis, bit):
    size = lax.axis_size(axis)
    return lax.ppermute(value, axis, [(i, i ^ bit) for i in range(size)])


def all_sum(value):
    for axis in ("mp", "dp"):
        bit = 1
        while bit < lax.axis_size(axis):
            value = value + swap(value, axis, bit)
            bit *= 2
    return value


def total(terms, rows=slice(None)):
    return sum(term[rows].astype(F32) for term in terms)


def columns(terms, cut):
    return tuple(term[:, cut] for term in terms)


def meet(own, partner):
    return own, swap(partner, "mp", 1)


def upper(terms):
    return total(terms, slice(terms[0].shape[0] // 2, None)).astype(BF16)


def fold(terms, bit, sent=None):
    half = terms[0].shape[0] // 2
    back = swap(upper(terms) if sent is None else sent, "dp", 1 << bit)
    return tuple(term[:half] for term in terms) + (back,)


def stacked(move, *sums):
    moved = move(jnp.concatenate(sums, axis=0))
    edges = [0]
    for value in sums:
        edges.append(edges[-1] + value.shape[0])
    return [moved[low:high] for low, high in zip(edges, edges[1:])]


def join(near, far, sent=None):
    return near + (swap(total(far).astype(BF16) if sent is None else sent, "mp", 2),)


def join_two(near_a, far_a, near_b, far_b):
    a, b = stacked(
        lambda value: swap(value, "mp", 2), total(far_a).astype(BF16), total(far_b).astype(BF16)
    )
    return near_a + (a,), near_b + (b,)


def fold_two(terms_a, terms_b, bit):
    half_a, half_b = terms_a[0].shape[0] // 2, terms_b[0].shape[0] // 2
    a, b = stacked(lambda value: swap(value, "dp", 1 << bit), upper(terms_a), upper(terms_b))
    return tuple(term[:half_a] for term in terms_a) + (a,), tuple(term[:half_b] for term in terms_b) + (b,)


CORRECTION = 1.0 - MOMENT_DECAY**STEP


def lamb_step(grad, master, first, second):
    first_new = MOMENT_DECAY * first + (1.0 - MOMENT_DECAY) * grad
    second_new = MOMENT_DECAY * second + (1.0 - MOMENT_DECAY) * grad * grad
    update = (
        first_new * (1.0 / CORRECTION) / (jnp.sqrt(second_new * (1.0 / CORRECTION)) + ADAM_EPS)
        + WEIGHT_DECAY * master
    )
    return first_new, second_new, update


def whole_sum(value):
    return jnp.sum(jnp.sum(value, axis=0, keepdims=True), axis=1, keepdims=True)


def spread(parts, width):
    lane = lax.broadcasted_iota(jnp.int32, (1, width), 1)
    return sum(jnp.where(lane == index, part, 0.0) for index, part in enumerate(parts))


def dense_step_kernel(*refs):
    ins, outs = refs[:8], refs[8:]
    parts = []
    for at in range(2):
        grad, master, first, second = (ref[...] for ref in ins[4 * at : 4 * at + 4])
        first_new, second_new, update = lamb_step(grad, master, first, second)
        for ref, value in zip(outs[3 * at : 3 * at + 3], (first_new, second_new, update)):
            ref[...] = value
        parts += [whole_sum(master * master), whole_sum(update * update)]
    outs[6][...] = spread(parts, outs[6].shape[1])


def run_dense_step(in_parts, down_parts):
    shape = jax.ShapeDtypeStruct(in_parts[0].shape, F32)
    width = in_parts[0].shape[1]
    return pl.pallas_call(
        dense_step_kernel,
        out_shape=(shape,) * 6 + (jax.ShapeDtypeStruct((1, width), F32),),
        compiler_params=params(BIG),
    )(*in_parts, *down_parts)


def attn_step_kernel(
    left_ref, right_ref, qm_ref, qf_ref, qs_ref, om_ref, of_ref, os_ref, sums_a_ref, sums_b_ref, squares_ref,
    qg_ref, qf_out, qs_out, qu_ref, og_ref, of_out, os_out, ou_ref, small_ref,
):
    cols = qm_ref.shape[2]
    left, right = left_ref[...], right_ref[...]
    master_square, update_square = 0.0, 0.0
    for index, grad in enumerate((left[:, :cols], left[:, cols:], right[:, :cols])):
        master = qm_ref[index]
        first_new, second_new, update = lamb_step(grad, master, qf_ref[index], qs_ref[index])
        qg_ref[index] = grad
        qf_out[index] = first_new
        qs_out[index] = second_new
        qu_ref[index] = update
        master_square += whole_sum(master * master)
        update_square += whole_sum(update * update)
    grad = right[:, cols:].T
    master = om_ref[...]
    first_new, second_new, update = lamb_step(grad, master, of_ref[...], os_ref[...])
    og_ref[...] = grad
    of_out[...] = first_new
    os_out[...] = second_new
    ou_ref[...] = update
    dense = squares_ref[...]
    parts = [
        master_square, whole_sum(master * master), dense[:, 0:1], dense[:, 2:3],
        update_square, whole_sum(update * update), dense[:, 1:2], dense[:, 3:4],
    ]
    width = small_ref.shape[1]
    small_ref[...] = jnp.concatenate(
        [sums_a_ref[0:2], sums_b_ref[0:4], spread(parts, width), jnp.zeros((1, width), F32)], axis=0
    )


def run_attn_step(left, right, qkv, out, sums_a, sums_b, squares):
    q, o = jax.ShapeDtypeStruct(qkv[0].shape, F32), jax.ShapeDtypeStruct(out[0].shape, F32)
    return pl.pallas_call(
        attn_step_kernel,
        out_shape=(q,) * 4 + (o,) * 4 + (jax.ShapeDtypeStruct(sums_a.shape, F32),),
        compiler_params=params(BIG),
    )(left, right, *qkv, *out, sums_a, sums_b, squares)


def final_kernel(*refs):
    small_ref, vec_ref, vf_ref, vs_ref = refs[:4]
    masters, updates, new = refs[4:8], refs[8:12], refs[12:16]
    vg_out, vf_out, vs_out, v_out, norms_ref = refs[16:]
    norms = jnp.sqrt(small_ref[6:7])
    lane = lax.broadcasted_iota(jnp.int32, norms_ref.shape, 1)
    row = lax.broadcasted_iota(jnp.int32, norms_ref.shape, 0)
    table = jnp.zeros(norms_ref.shape, F32)
    for index in range(4):
        weight, update = norms[:, index : index + 1], norms[:, 4 + index : 5 + index]
        trust = weight / (update + ADAM_EPS)
        new[index][...] = masters[index][...] - LEARN_RATE * trust * updates[index][...]
        for at, value in enumerate((weight, update, trust)):
            table = jnp.where((lane == index) & (row == at), value, table)
    norms_ref[...] = table
    grad = small_ref[0:6]
    first_new = MOMENT_DECAY * vf_ref[...] + (1.0 - MOMENT_DECAY) * grad
    second_new = MOMENT_DECAY * vs_ref[...] + (1.0 - MOMENT_DECAY) * grad * grad
    vg_out[...] = grad
    vf_out[...] = first_new
    vs_out[...] = second_new
    v_out[...] = vec_ref[...] - LEARN_RATE * (first_new * (1.0 / CORRECTION)) / (
        jnp.sqrt(second_new * (1.0 / CORRECTION)) + ADAM_EPS
    )


def run_final(small, vectors, vec_first, vec_second, masters, updates):
    shape = lambda value: jax.ShapeDtypeStruct(value.shape, F32)
    flat = lambda value: value.reshape(-1, value.shape[-1])
    outs = pl.pallas_call(
        final_kernel,
        out_shape=tuple(shape(flat(m)) for m in masters)
        + (shape(vectors),) * 4
        + (jax.ShapeDtypeStruct((3, 4), F32),),
        compiler_params=params(BIG),
    )(small, vectors, vec_first, vec_second, *(flat(m) for m in masters), *(flat(u) for u in updates))
    new = [value.reshape(m.shape) for value, m in zip(outs[:4], masters)]
    return new, outs[4:]


def after(value, *others):
    return lax.optimization_barrier((value,) + others)[0]


def shards(
    rows,
    cotangent,
    group_ids,
    qkv_weight,
    out_weight,
    in_weight,
    down_weight,
    vectors,
    qkv_master,
    qkv_first,
    qkv_second,
    out_master,
    out_first,
    out_second,
    in_master,
    in_first,
    in_second,
    down_master,
    down_first,
    down_second,
    vec_first,
    vec_second,
):
    count = lax.axis_size("dp")
    width = rows.shape[1]
    half = width // 2
    nbits = count.bit_length() - 1
    me = lax.axis_index("dp").astype(jnp.int32)
    rel = jnp.arange(count, dtype=jnp.int32) ^ me
    order1 = tuple(range(nbits))
    order2 = (1, 0) + order1[2:]
    pos, pos2 = (
        sum(((rel >> bit) & 1) << (nbits - 1 - place) for place, bit in enumerate(order))
        for order in (order1, order2)
    )
    low = (me & 1).reshape(1)

    onehot = (group_ids[:, None] == jnp.arange(GROUPS, dtype=jnp.int32)[None, :]).astype(F32)
    counts = jnp.sum(onehot, axis=0)

    attn_w = jnp.concatenate(
        [jnp.swapaxes(qkv_weight, 1, 2).reshape(-1, width), out_weight], axis=0
    )
    pieces = [
        lax.dynamic_slice_in_dim(weight, low[0] * half, half, axis)
        for weight, axis in ((attn_w, 0), (in_weight, 0), (down_weight, 1))
    ]
    counts, pieces[0] = lax.optimization_barrier((counts, pieces[0]))
    attn_far = swap(pieces[0], "mp", 2)
    counts = counts + swap(counts, "mp", 2)
    counts, *pieces = lax.optimization_barrier((counts, *pieces[1:]))
    in_far, down_far = (swap(piece, "mp", 2) for piece in pieces)
    near = [swap(weight, "mp", 1) for weight in (attn_w, in_weight, down_weight)]
    counts, attn_one, in_one, down_one = lax.optimization_barrier((counts, *near))
    counts = counts + swap(counts, "dp", 1)
    x, xt, xt2 = run_start(pos, pos2, rows, vectors, count)
    xt, xt2 = turned_order(xt, pos, count), turned_order(xt2, pos2, count)
    acc, s1, p1, s0, p0 = run_attn_one(x, rows, vectors, attn_one, attn_w)
    attn_far, counts, acc = lax.optimization_barrier((attn_far, counts, acc))
    attn_two = (attn_far, swap(attn_far, "dp", 1))
    counts = counts + swap(counts, "mp", 1)
    for bit in order1[1:]:
        counts = counts + swap(counts, "dp", 1 << bit)
    image_weight = jnp.sqrt(jnp.sum(counts) / (GROUPS * jnp.sum(onehot * counts, axis=1)))
    gout, goutt = run_gout(pos2, image_weight, cotangent, count)
    goutt = turned_order(goutt, pos2, count)
    attn_other, in_far, gout, acc = lax.optimization_barrier((attn_two[1], in_far, gout, acc))
    in_two = (in_far, swap(in_far, "dp", 1))
    attn_two = (attn_far, attn_other)
    attn_three = tuple(swap(piece, "mp", 1) for piece in attn_two)
    first, mid, midt, s3, p3, s2, p2 = run_attn_two(
        pos, low, x, acc, vectors, attn_three, attn_two, count
    )
    midt = turned_order(midt, pos, count)
    y, dm, gi1, gd1 = run_ffn_near(mid, midt, gout, goutt, in_one, down_one)
    gi1, gd1, y, down_far, _ = lax.optimization_barrier((gi1, gd1, y, down_far, in_two[1]))
    down_two = (down_far, swap(down_far, "dp", 1))
    y, dm, gi0, gd0 = run_ffn_near(mid, midt, gout, goutt, in_weight, down_weight, y, dm)
    in_near, down_near = meet(gi0, gi1), meet(gd0, gd1)
    y, down_other, in_sent, down_sent = lax.optimization_barrier(
        (y, down_two[1], upper(in_near), upper(down_near))
    )
    in_near, down_near = fold(in_near, order1[0], in_sent), fold(down_near, order2[0], down_sent)
    down_two = (down_far, down_other)
    in_three, down_three = (
        tuple(swap(piece, "mp", 1) for piece in pieces) for pieces in (in_two, down_two)
    )
    y, dm, gi3, gd3 = run_ffn_far(low, mid, midt, gout, goutt, in_three, down_three, y, dm)
    out_rows, gfirst, gfl, gft, sums_b, gi2, gd2 = run_ffn_last(
        pos2, low, image_weight, mid, midt, gout, goutt, in_two, down_two,
        y, dm, first, cotangent, vectors, count,
    )
    gft = turned_order(gft, pos2, count)
    in_far, down_far = meet(gi2, gi3), meet(gd2, gd3)
    gfl, in_sent, down_sent, _, _ = lax.optimization_barrier(
        (gfl, upper(in_far), upper(down_far), in_near[-1], down_near[-1])
    )
    in_far, down_far = fold(in_far, order1[0], in_sent), fold(down_far, order2[0], down_sent)
    gin, ga3 = run_back_far(low, gfl, xt, xt2, gft, attn_three, (s3, p3))
    gin, ga2 = run_back_far(low, gfl, xt, xt2, gft, attn_two, (s2, p2), gin)
    both = meet(ga2, ga3)
    left_far, right_far = columns(both, slice(0, half)), columns(both, slice(half, None))
    gin, left_sent, right_sent, in_sent, down_sent = lax.optimization_barrier(
        (gin, upper(left_far), upper(right_far), total(in_far).astype(BF16), total(down_far).astype(BF16))
    )
    left_far, right_far = fold(left_far, order1[0], left_sent), fold(right_far, order2[0], right_sent)
    in_grad, down_grad = join(in_near, None, in_sent), join(down_near, None, down_sent)
    gin, ga1 = run_back_near(gfl, xt, xt2, gft, attn_one, (s1, p1), gin)
    ga1, *_ = lax.optimization_barrier((ga1, left_far[-1], right_far[-1]))
    input_grad, sums_a, ga0 = run_back_last(
        gfl, xt, xt2, gft, attn_w, (s0, p0), gin, rows, gfirst, vectors
    )
    both = meet(ga0, ga1)
    left_near, right_near = columns(both, slice(0, half)), columns(both, slice(half, None))
    left_far, right_far = fold(left_far, order1[1]), fold(right_far, order2[1])
    left_near, right_near = fold(left_near, order1[0]), fold(right_near, order2[0])
    near_back, far_back = lax.optimization_barrier(
        ((left_near[-1], right_near[-1]), (left_far[-1], right_far[-1]))
    )
    left_near, right_near = left_near[:-1] + near_back[:1], right_near[:-1] + near_back[1:]
    left_far, right_far = left_far[:-1] + far_back[:1], right_far[:-1] + far_back[1:]
    left_near, right_near = fold(left_near, order1[1]), fold(right_near, order2[1])
    in_grad, down_grad = fold(in_grad, order1[1]), fold(down_grad, order2[1])
    for bit in order1[2:]:
        in_grad, down_grad = fold(in_grad, bit), fold(down_grad, bit)
        left_far, right_far = fold_two(left_far, right_far, bit)
        left_near, right_near = fold_two(left_near, right_near, bit)
    left, right = join_two(left_near, left_far, right_near, right_far)
    in_grad, down_grad, left, right = (total(terms) for terms in (in_grad, down_grad, left, right))

    down_state = (down_master.T, down_first.T, down_second.T)
    in_fn, in_sn, in_up, down_fn, down_sn, down_up, squares = run_dense_step(
        (in_grad, in_master, in_first, in_second), (down_grad,) + down_state
    )
    qkv_grad, qkv_fn, qkv_sn, qkv_up, out_grad, out_fn, out_sn, out_up, small = run_attn_step(
        left, right, (qkv_master, qkv_first, qkv_second), (out_master, out_first, out_second),
        sums_a, sums_b, squares,
    )
    new, vec_outs = run_final(
        all_sum(small), vectors, vec_first, vec_second,
        (qkv_master, out_master, in_master, down_state[0]), (qkv_up, out_up, in_up, down_up),
    )
    return (
        out_rows,
        input_grad,
        qkv_grad,
        out_grad,
        in_grad,
        down_grad.T,
        qkv_fn,
        qkv_sn,
        new[0],
        out_fn,
        out_sn,
        new[1],
        in_fn,
        in_sn,
        new[2],
        down_fn.T,
        down_sn.T,
        new[3].T,
    ) + tuple(vec_outs)


def solution(mesh):
    rows = P(("dp", "mp"), None)
    qkv_state = P(None, "dp", "mp")
    out_state = P("mp", "dp")
    in_state = P("dp", "mp")
    in_specs = (
        (rows, rows, P(("dp", "mp")), P(None, None, "mp"), P("mp", None), P(None, "mp"), P("mp", None), P())
        + (qkv_state,) * 3
        + (out_state,) * 3
        + (in_state,) * 3
        + (out_state,) * 3
        + (P(), P())
    )
    out_specs = (
        (rows, rows, qkv_state, out_state, in_state, out_state)
        + (qkv_state,) * 3
        + (out_state,) * 3
        + (in_state,) * 3
        + (out_state,) * 3
        + (P(),) * 5
    )
    return jax.shard_map(shards, mesh=mesh, in_specs=in_specs, out_specs=out_specs, check_vma=False)
```

```python
import math

import jax
import jax.numpy as jnp
from jax import lax
from jax.experimental import pallas as pl
from jax.experimental.pallas import tpu as pltpu
from jax.sharding import PartitionSpec as P

HEAD_DIM = 64
PATCHES = 256
GROUPS = 8
STEP = 5

NORM_EPS = 1e-06
ADAM_EPS = 1e-06
MOMENT_DECAY = 0.5
LEARN_RATE = 0.5
WEIGHT_DECAY = 0.01
SCALE = HEAD_DIM ** (-0.5)

F32 = jnp.float32
BF16 = jnp.bfloat16
MB = 1024 * 1024
BIG = 16


def mm(left, right):
    return jnp.dot(left, right, preferred_element_type=F32)


def mm_nt(left, right):
    return lax.dot_general(left, right, (((1,), (1,)), ((), ())), preferred_element_type=F32)


def mm_tn(left, right):
    return lax.dot_general(left, right, (((0,), (0,)), ((), ())), preferred_element_type=F32)


def layer_stats(values):
    center = values - jnp.mean(values, axis=-1, keepdims=True)
    inverse = lax.rsqrt(jnp.mean(center * center, axis=-1, keepdims=True) + NORM_EPS)
    return center * inverse, inverse


def norm_back(grad_normed, normed, inverse):
    return inverse * (
        grad_normed
        - jnp.mean(grad_normed, axis=-1, keepdims=True)
        - normed * jnp.mean(grad_normed * normed, axis=-1, keepdims=True)
    )


def gelu_pair(t):
    size = jnp.abs(t) * (2.0**-0.5)
    k = 1.0 / (1.0 + 0.3275911 * size)
    bell = jnp.exp(-size * size)
    poly = k * (
        0.254829592
        + k * (-0.284496736 + k * (1.421413741 + k * (-1.453152027 + k * 1.061405429)))
    )
    tail = 0.5 * poly * bell
    cdf = jnp.where(t < 0, tail, 1.0 - tail)
    return t * cdf, cdf + t * bell * (1.0 / math.sqrt(2.0 * math.pi))


def put_turned(out_ref, value, pos_ref, count, start):
    turned = value.T
    part = turned.shape[0] // count
    width = turned.shape[1]
    here = pl.ds(start, width)
    if len(out_ref.shape) == 2:
        out_ref[:, here] = turned
        return
    for j in range(count):
        out_ref[pos_ref[j], :, here] = turned[j * part : (j + 1) * part]


def turned_shape(width, rows, count):
    part = width // count
    if part % 16 == 0:
        return (count, part, rows)
    return (width, rows)


def turned_order(turned, pos, count):
    width = turned.shape[0] if turned.ndim == 2 else turned.shape[0] * turned.shape[1]
    rows = turned.shape[-1]
    if turned.ndim == 2:
        shaped = turned.reshape(count, width // count, rows)
        turned = jnp.zeros_like(shaped).at[pos].set(shaped)
    return turned.reshape(width, rows)


def params(limit, **more):
    return pltpu.CompilerParams(vmem_limit_bytes=limit * MB, **more)


def full(shape):
    return pl.BlockSpec(shape, lambda *_: (0,) * len(shape), pipeline_mode=pl.Buffered(1))


SMEM = pl.BlockSpec(memory_space=pltpu.SMEM)


def start_kernel(pos_ref, pos2_ref, rows_ref, vec_ref, x_ref, xt_ref, xt2_ref, *, count):
    width, rows = rows_ref.shape[1], rows_ref.shape[0]
    for start in range(0, rows, PATCHES):
        normed, _ = layer_stats(rows_ref[start : start + PATCHES].astype(F32))
        low = (normed * vec_ref[0:1] + vec_ref[1:2]).astype(BF16)
        x_ref[start : start + PATCHES] = low
        put_turned(xt_ref, low, pos_ref, count, start)
        put_turned(xt2_ref, low, pos2_ref, count, start)


def run_start(pos, pos2, rows, vectors, count):
    r, d = rows.shape
    return pl.pallas_call(
        lambda *refs: start_kernel(*refs, count=count),
        out_shape=(
            jax.ShapeDtypeStruct((r, d), BF16),
            jax.ShapeDtypeStruct(turned_shape(d, r, count), BF16),
            jax.ShapeDtypeStruct(turned_shape(d, r, count), BF16),
        ),
        in_specs=[SMEM, SMEM, pl.BlockSpec(memory_space=pltpu.VMEM), pl.BlockSpec(memory_space=pltpu.VMEM)],
        compiler_params=params(BIG),
    )(pos, pos2, rows, vectors)


def gout_kernel(pos_ref, weight_ref, cot_ref, g_ref, gt_ref, *, count):
    rows = cot_ref.shape[0]
    for index in range(rows // PATCHES):
        start = index * PATCHES
        low = (cot_ref[start : start + PATCHES].astype(F32) * weight_ref[index]).astype(BF16)
        g_ref[start : start + PATCHES] = low
        put_turned(gt_ref, low, pos_ref, count, start)


def run_gout(pos, weight, cot, count):
    r, d = cot.shape
    return pl.pallas_call(
        lambda *refs: gout_kernel(*refs, count=count),
        out_shape=(
            jax.ShapeDtypeStruct((r, d), BF16),
            jax.ShapeDtypeStruct(turned_shape(d, r, count), BF16),
        ),
        in_specs=[SMEM, SMEM, pl.BlockSpec(memory_space=pltpu.VMEM)],
        compiler_params=params(BIG),
    )(pos, weight, cot)


def attend_shard(x, w_ref, saved_ref, probs_ref):
    cols = w_ref.shape[0] // 4
    qkv = mm_nt(x, w_ref[: 3 * cols]).astype(BF16)
    saved_ref[:, : 3 * cols] = qkv
    mixed = []
    for h in range(cols // HEAD_DIM):
        at = h * HEAD_DIM
        q = qkv[:, at : at + HEAD_DIM] * SCALE
        k = qkv[:, cols + at : cols + at + HEAD_DIM]
        v = qkv[:, 2 * cols + at : 2 * cols + at + HEAD_DIM]
        scores = mm_nt(q, k)
        expo = jnp.exp(scores - jnp.max(scores, axis=-1, keepdims=True))
        probs = (expo * (1.0 / jnp.sum(expo, axis=-1, keepdims=True))).astype(BF16)
        probs_ref[h] = probs
        mixed.append(mm(probs, v).astype(BF16))
    mixed = jnp.concatenate(mixed, axis=1)
    saved_ref[:, 3 * cols :] = mixed
    return mm(mixed, w_ref[3 * cols :])


def attn_one_kernel(x_ref, rows_ref, vec_ref, wa_ref, wb_ref, acc_ref, sa_ref, pa_ref, sb_ref, pb_ref):
    x = x_ref[...]
    term = attend_shard(x, wa_ref, sa_ref, pa_ref)
    term += attend_shard(x, wb_ref, sb_ref, pb_ref)
    acc_ref[...] = rows_ref[...].astype(F32) + term + vec_ref[4:5]


def join_halves(low_ref, own_ref, other_ref, whole_ref):
    half = own_ref.shape[0]

    @pl.when(low_ref[0] == 0)
    def _():
        whole_ref[:half] = own_ref[...]
        whole_ref[half:] = other_ref[...]

    @pl.when(low_ref[0] != 0)
    def _():
        whole_ref[:half] = other_ref[...]
        whole_ref[half:] = own_ref[...]


def join_pair(low_ref, halves, wholes):
    @pl.when(pl.program_id(0) == 0)
    def _():
        for (own, other), whole in zip(halves, wholes):
            join_halves(low_ref, own, other, whole)


def attn_two_kernel(
    pos_ref, low_ref, x_ref, acc_ref, vec_ref, ha_ref, ia_ref, hb_ref, ib_ref,
    first_ref, mid_ref, midt_ref, sa_ref, pa_ref, sb_ref, pb_ref, wa_ref, wb_ref, *, count,
):
    join_pair(low_ref, ((ha_ref, ia_ref), (hb_ref, ib_ref)), (wa_ref, wb_ref))
    x = x_ref[...]
    term = attend_shard(x, wa_ref, sa_ref, pa_ref)
    term += attend_shard(x, wb_ref, sb_ref, pb_ref)
    first = acc_ref[...] + term
    first_ref[...] = first
    normed, _ = layer_stats(first)
    low = (normed * vec_ref[2:3] + vec_ref[3:4]).astype(BF16)
    mid_ref[...] = low
    put_turned(midt_ref, low, pos_ref, count, 0)


def image_block(d):
    return pl.BlockSpec((PATCHES, d), lambda i: (i, 0))


def saved_outputs(r, d, heads):
    images = r // PATCHES
    shapes = (
        jax.ShapeDtypeStruct((r, d), BF16),
        jax.ShapeDtypeStruct((images * heads, PATCHES, PATCHES), BF16),
    )
    specs = [image_block(d), pl.BlockSpec((heads, PATCHES, PATCHES), lambda i: (i, 0, 0))]
    return shapes, specs


def cost(micros):
    return pl.CostEstimate(flops=int(micros * 10 * 1e9), bytes_accessed=int(micros * 10 * 3e6), transcendentals=0)


def run_attn_one(x, rows, vectors, wa, wb):
    r, d = x.shape
    heads = d // 4 // HEAD_DIM
    shapes, specs = saved_outputs(r, d, heads)
    return pl.pallas_call(
        attn_one_kernel,
        grid=(r // PATCHES,),
        out_shape=(jax.ShapeDtypeStruct((r, d), F32),) + shapes * 2,
        in_specs=[image_block(d), image_block(d), full(vectors.shape), full((d, d)), full((d, d))],
        out_specs=[image_block(d)] + specs * 2,
        compiler_params=params(BIG),
        cost_estimate=cost(7),
    )(x, rows, vectors, wa, wb)


def run_attn_two(pos, low, x, acc, vectors, wa, wb, count):
    r, d = x.shape
    heads = d // 4 // HEAD_DIM
    shapes, specs = saved_outputs(r, d, heads)
    tshape = turned_shape(d, r, count)
    tspec = pl.BlockSpec(
        tshape[:-1] + (PATCHES,), lambda i: (0,) * (len(tshape) - 1) + (i,)
    )
    return pl.pallas_call(
        lambda *refs: attn_two_kernel(*refs, count=count),
        grid=(r // PATCHES,),
        out_shape=(
            jax.ShapeDtypeStruct((r, d), F32),
            jax.ShapeDtypeStruct((r, d), BF16),
            jax.ShapeDtypeStruct(tshape, BF16),
        )
        + shapes * 2,
        in_specs=[SMEM, SMEM, image_block(d), image_block(d), full(vectors.shape)]
        + [full((d // 2, d))] * 4,
        out_specs=[image_block(d), image_block(d), tspec] + specs * 2,
        scratch_shapes=[pltpu.VMEM((d, d), BF16)] * 2,
        compiler_params=params(BIG),
        cost_estimate=cost(7),
    )(pos, low, x, acc, vectors, *wa, *wb)


TILES = 3


def ffn_tile(mid_ref, midt_ref, g_ref, gt_ref, w_in, w_down, gi_ref, gd_ref, y_ref, dm_ref):
    pre = mm(mid_ref[...], w_in)
    dact = mm_nt(g_ref[...], w_down)
    activ, slope = gelu_pair(pre)
    activ = activ.astype(BF16)
    dpre = (dact * slope).astype(BF16)
    y_ref[...] += mm(activ, w_down)
    dm_ref[...] += mm_nt(dpre, w_in)
    gd_ref[...] = mm(gt_ref[...], activ).astype(BF16)
    gi_ref[...] = mm(midt_ref[...], dpre).astype(BF16)


def joined(low_ref, own_ref, other_ref, axis):
    own, other = own_ref[...], other_ref[...]
    return jnp.where(
        low_ref[0] == 0,
        jnp.concatenate([own, other], axis=axis),
        jnp.concatenate([other, own], axis=axis),
    )


def ffn_near_kernel(mid_ref, midt_ref, g_ref, gt_ref, in_ref, down_ref, *rest):
    *before, y_ref, dm_ref, gi_ref, gd_ref = rest

    @pl.when(pl.program_id(0) == 0)
    def _():
        y_ref[...] = before[0][...] if before else jnp.zeros_like(y_ref)
        dm_ref[...] = before[1][...] if before else jnp.zeros_like(dm_ref)

    ffn_tile(mid_ref, midt_ref, g_ref, gt_ref, in_ref[...], down_ref[...], gi_ref, gd_ref, y_ref, dm_ref)


def ffn_far_kernel(
    low_ref, mid_ref, midt_ref, g_ref, gt_ref, ia_ref, ib_ref, da_ref, db_ref, y_in_ref, dm_in_ref,
    y_ref, dm_ref, gi_ref, gd_ref,
):
    @pl.when(pl.program_id(0) == 0)
    def _():
        y_ref[...] = y_in_ref[...]
        dm_ref[...] = dm_in_ref[...]

    w_in, w_down = joined(low_ref, ia_ref, ib_ref, 0), joined(low_ref, da_ref, db_ref, 1)
    ffn_tile(mid_ref, midt_ref, g_ref, gt_ref, w_in, w_down, gi_ref, gd_ref, y_ref, dm_ref)


def ffn_last_kernel(
    pos_ref, low_ref, weight_ref, mid_ref, midt_ref, g_ref, gt_ref, ia_ref, ib_ref, da_ref, db_ref,
    y_in_ref, dm_in_ref, first_ref, cot_ref, vec_ref,
    out_ref, gf_ref, gfl_ref, gft_ref, sums_ref, gi_ref, gd_ref, y_ref, dm_ref, *, count,
):
    ffn_far_kernel(
        low_ref, mid_ref, midt_ref, g_ref, gt_ref, ia_ref, ib_ref, da_ref, db_ref, y_in_ref, dm_in_ref,
        y_ref, dm_ref, gi_ref, gd_ref,
    )

    @pl.when(pl.program_id(0) == pl.num_programs(0) - 1)
    def _():
        chunk = 128

        def body(index, sums):
            start = pl.multiple_of(index * chunk, chunk)
            here = pl.ds(start, chunk)
            first = first_ref[here, :]
            normed, inverse = layer_stats(first)
            out_ref[here, :] = (first + y_ref[here, :] + vec_ref[5:6]).astype(BF16)
            dmid = dm_ref[here, :]
            gout = cot_ref[here, :].astype(F32) * weight_ref[start // PATCHES]
            gfirst = gout + norm_back(dmid * vec_ref[2:3], normed, inverse)
            gf_ref[here, :] = gfirst
            low = gfirst.astype(BF16)
            gfl_ref[here, :] = low
            put_turned(gft_ref, low, pos_ref, count, start)
            terms = (dmid * normed, dmid, gfirst, gout)
            return tuple(a + jnp.sum(b, axis=0, keepdims=True) for a, b in zip(sums, terms))

        zero = jnp.zeros((1, first_ref.shape[1]), F32)
        sums = lax.fori_loop(0, first_ref.shape[0] // chunk, body, (zero,) * 4)
        sums_ref[...] = jnp.concatenate(sums + sums, axis=0)


def ffn_specs(d, parts):
    tile = d // TILES
    cols = lambda rows: pl.BlockSpec((rows, tile), lambda i: (0, i))
    w_down = pl.BlockSpec((tile, d // parts), lambda i: (i, 0))
    return [cols(d // parts)] * parts + [w_down] * parts, [cols(d)] * 2


def run_ffn_near(mid, midt, g, gt, w_in, w_down, *before):
    r, d = mid.shape
    w_specs, g_specs = ffn_specs(d, 1)
    grad = jax.ShapeDtypeStruct((d, d), BF16)
    return pl.pallas_call(
        ffn_near_kernel,
        grid=(TILES,),
        out_shape=(jax.ShapeDtypeStruct((r, d), F32),) * 2 + (grad,) * 2,
        in_specs=[full((r, d)), full((d, r)), full((r, d)), full((d, r))] + w_specs + [full((r, d))] * len(before),
        out_specs=[full((r, d))] * 2 + g_specs,
        compiler_params=params(BIG),
        cost_estimate=cost(6),
    )(mid, midt, g, gt, w_in, w_down, *before)


def run_ffn_far(low, mid, midt, g, gt, w_in, w_down, y, dm):
    r, d = mid.shape
    w_specs, g_specs = ffn_specs(d, 2)
    grad = jax.ShapeDtypeStruct((d, d), BF16)
    return pl.pallas_call(
        ffn_far_kernel,
        grid=(TILES,),
        out_shape=(jax.ShapeDtypeStruct((r, d), F32),) * 2 + (grad,) * 2,
        in_specs=[SMEM, full((r, d)), full((d, r)), full((r, d)), full((d, r))] + w_specs + [full((r, d))] * 2,
        out_specs=[full((r, d))] * 2 + g_specs,
        compiler_params=params(BIG),
        cost_estimate=cost(6),
    )(low, mid, midt, g, gt, *w_in, *w_down, y, dm)


def run_ffn_last(pos, low, weight, mid, midt, g, gt, w_in, w_down, y, dm, first, cot, vectors, count):
    r, d = mid.shape
    w_specs, g_specs = ffn_specs(d, 2)
    grad = jax.ShapeDtypeStruct((d, d), BF16)
    tshape = turned_shape(d, r, count)
    return pl.pallas_call(
        lambda *refs: ffn_last_kernel(*refs, count=count),
        grid=(TILES,),
        out_shape=(
            jax.ShapeDtypeStruct((r, d), BF16),
            jax.ShapeDtypeStruct((r, d), F32),
            jax.ShapeDtypeStruct((r, d), BF16),
            jax.ShapeDtypeStruct(tshape, BF16),
            jax.ShapeDtypeStruct((8, d), F32),
        )
        + (grad,) * 2,
        in_specs=[SMEM, SMEM, SMEM, full((r, d)), full((d, r)), full((r, d)), full((d, r))]
        + w_specs
        + [full((r, d))] * 4
        + [full(vectors.shape)],
        out_specs=[full((r, d)), full((r, d)), full((r, d)), full(tshape), full((8, d))] + g_specs,
        scratch_shapes=[pltpu.VMEM((r, d), F32)] * 2,
        compiler_params=params(BIG),
        cost_estimate=cost(8),
    )(pos, low, weight, mid, midt, g, gt, *w_in, *w_down, y, dm, first, cot, vectors)


def attend_back_shard(gf, w_ref, saved_ref, probs_ref, keep_ref):
    cols = w_ref.shape[0] // 4
    start = pl.multiple_of(pl.program_id(0) * PATCHES, PATCHES)
    dmix = mm_nt(gf, w_ref[3 * cols :]).astype(BF16)
    dq, dk, dv = [], [], []
    for h in range(cols // HEAD_DIM):
        at = h * HEAD_DIM
        q = saved_ref[:, at : at + HEAD_DIM]
        k = saved_ref[:, cols + at : cols + at + HEAD_DIM]
        v = saved_ref[:, 2 * cols + at : 2 * cols + at + HEAD_DIM]
        do = dmix[:, at : at + HEAD_DIM]
        probs = probs_ref[h]
        dv.append(mm_tn(probs, do).astype(BF16))
        dp = mm_nt(do, v)
        wide = probs.astype(F32)
        ds = (SCALE * wide * (dp - jnp.sum(wide * dp, axis=-1, keepdims=True))).astype(BF16)
        dq.append(mm(ds, k).astype(BF16))
        dk.append(mm_tn(ds, q).astype(BF16))
    dqkv = jnp.concatenate(dq + dk + dv, axis=1)
    keep_ref[pl.ds(start, PATCHES), : 3 * cols] = dqkv
    keep_ref[pl.ds(start, PATCHES), 3 * cols :] = saved_ref[:, 3 * cols :]
    return mm(dqkv, w_ref[: 3 * cols])


def attn_grad(xt_ref, xt2_ref, gft_ref, keep_ref, g_ref):
    cols = keep_ref.shape[1] // 4
    g_ref[:, : 2 * cols] = mm(xt_ref[...], keep_ref[:, : 2 * cols]).astype(BF16)
    g_ref[:, 2 * cols : 3 * cols] = mm(xt2_ref[...], keep_ref[:, 2 * cols : 3 * cols]).astype(BF16)
    g_ref[:, 3 * cols :] = mm(gft_ref[...], keep_ref[:, 3 * cols :]).astype(BF16)


def back_body(gf_ref, xt_ref, xt2_ref, gft_ref, w_ref, saved_ref, probs_ref, g_ref, keep_ref):
    term = attend_back_shard(gf_ref[...], w_ref, saved_ref, probs_ref, keep_ref)

    @pl.when(pl.program_id(0) == pl.num_programs(0) - 1)
    def _():
        attn_grad(xt_ref, xt2_ref, gft_ref, keep_ref, g_ref)

    return term


def back_far_kernel(
    low_ref, gf_ref, xt_ref, xt2_ref, gft_ref, saved_ref, probs_ref, h_ref, i_ref, *rest
):
    *before, acc_ref, g_ref, keep_ref, w_ref = rest
    join_pair(low_ref, ((h_ref, i_ref),), (w_ref,))
    term = back_body(gf_ref, xt_ref, xt2_ref, gft_ref, w_ref, saved_ref, probs_ref, g_ref, keep_ref)
    if before:
        acc_ref[...] = term + before[0][...]
    else:
        acc_ref[...] = jnp.zeros_like(acc_ref)
        acc_ref[...] += term


def back_near_kernel(
    gf_ref, xt_ref, xt2_ref, gft_ref, saved_ref, probs_ref, w_ref, before_ref, acc_ref, g_ref, keep_ref
):
    term = back_body(gf_ref, xt_ref, xt2_ref, gft_ref, w_ref, saved_ref, probs_ref, g_ref, keep_ref)
    acc_ref[...] = term + before_ref[...]


def back_last_kernel(
    gf_ref, xt_ref, xt2_ref, gft_ref, saved_ref, probs_ref, w_ref, before_ref, rows_ref, gfirst_ref, vec_ref,
    ig_ref, sums_ref, g_ref, keep_ref,
):
    term = back_body(gf_ref, xt_ref, xt2_ref, gft_ref, w_ref, saved_ref, probs_ref, g_ref, keep_ref)
    grad_in = before_ref[...] + term
    normed, inverse = layer_stats(rows_ref[...].astype(F32))
    ig_ref[...] = gfirst_ref[...] + norm_back(grad_in * vec_ref[0:1], normed, inverse)
    one = jnp.sum(grad_in * normed, axis=0, keepdims=True)
    two = jnp.sum(grad_in, axis=0, keepdims=True)
    sums = jnp.concatenate([one, two] * 4, axis=0)

    @pl.when(pl.program_id(0) == 0)
    def _():
        sums_ref[...] = sums

    @pl.when(pl.program_id(0) > 0)
    def _():
        sums_ref[...] += sums


def back_call(kernel, ops, specs, outs, out_specs, far):
    gfl = ops[1] if far else ops[0]
    r, d = gfl.shape
    heads = d // 4 // HEAD_DIM
    _, saved_specs = saved_outputs(r, d, heads)
    keep, whole = pltpu.VMEM((r, d), BF16), pltpu.VMEM((d, d), BF16)
    return pl.pallas_call(
        kernel,
        grid=(r // PATCHES,),
        out_shape=tuple(outs) + (jax.ShapeDtypeStruct((d, d), BF16),),
        in_specs=([SMEM] if far else []) + [image_block(d)] + [full((d, r))] * 3 + saved_specs + specs,
        out_specs=out_specs + [full((d, d))],
        scratch_shapes=[keep, whole] if far else [keep],
        compiler_params=params(BIG),
        cost_estimate=cost(6),
    )(*ops)


def run_back_far(low, gfl, xt, xt2, gft, halves, saved, *acc):
    r, d = gfl.shape
    return back_call(
        back_far_kernel,
        [low, gfl, xt, xt2, gft, *saved, *halves, *acc],
        [full((d // 2, d))] * 2 + [image_block(d)] * len(acc),
        [jax.ShapeDtypeStruct((r, d), F32)], [image_block(d)], True,
    )


def run_back_near(gfl, xt, xt2, gft, weight, saved, acc):
    r, d = gfl.shape
    return back_call(
        back_near_kernel,
        [gfl, xt, xt2, gft, *saved, weight, acc],
        [full((d, d)), image_block(d)],
        [jax.ShapeDtypeStruct((r, d), F32)], [image_block(d)], False,
    )


def run_back_last(gfl, xt, xt2, gft, weight, saved, acc, rows, gfirst, vectors):
    r, d = gfl.shape
    return back_call(
        back_last_kernel,
        [gfl, xt, xt2, gft, *saved, weight, acc, rows, gfirst, vectors],
        [full((d, d))] + [image_block(d)] * 3 + [full(vectors.shape)],
        [jax.ShapeDtypeStruct((r, d), F32), jax.ShapeDtypeStruct((8, d), F32)],
        [image_block(d), full((8, d))], False,
    )


def swap(value, axis, bit):
    size = lax.axis_size(axis)
    return lax.ppermute(value, axis, [(i, i ^ bit) for i in range(size)])


def all_sum(value):
    for axis in ("mp", "dp"):
        bit = 1
        while bit < lax.axis_size(axis):
            value = value + swap(value, axis, bit)
            bit *= 2
    return value


def total(terms, rows=slice(None)):
    return sum(term[rows].astype(F32) for term in terms)


def columns(terms, cut):
    return tuple(term[:, cut] for term in terms)


def meet(own, partner):
    return own, swap(partner, "mp", 1)


def upper(terms):
    return total(terms, slice(terms[0].shape[0] // 2, None)).astype(BF16)


def fold(terms, bit, sent=None):
    half = terms[0].shape[0] // 2
    back = swap(upper(terms) if sent is None else sent, "dp", 1 << bit)
    return tuple(term[:half] for term in terms) + (back,)


def stacked(move, *sums):
    moved = move(jnp.concatenate(sums, axis=0))
    edges = [0]
    for value in sums:
        edges.append(edges[-1] + value.shape[0])
    return [moved[low:high] for low, high in zip(edges, edges[1:])]


def join(near, far, sent=None):
    return near + (swap(total(far).astype(BF16) if sent is None else sent, "mp", 2),)


def join_two(near_a, far_a, near_b, far_b):
    a, b = stacked(
        lambda value: swap(value, "mp", 2), total(far_a).astype(BF16), total(far_b).astype(BF16)
    )
    return near_a + (a,), near_b + (b,)


def fold_two(terms_a, terms_b, bit):
    half_a, half_b = terms_a[0].shape[0] // 2, terms_b[0].shape[0] // 2
    a, b = stacked(lambda value: swap(value, "dp", 1 << bit), upper(terms_a), upper(terms_b))
    return tuple(term[:half_a] for term in terms_a) + (a,), tuple(term[:half_b] for term in terms_b) + (b,)


CORRECTION = 1.0 - MOMENT_DECAY**STEP


def lamb_step(grad, master, first, second):
    first_new = MOMENT_DECAY * first + (1.0 - MOMENT_DECAY) * grad
    second_new = MOMENT_DECAY * second + (1.0 - MOMENT_DECAY) * grad * grad
    update = (
        first_new * (1.0 / CORRECTION) / (jnp.sqrt(second_new * (1.0 / CORRECTION)) + ADAM_EPS)
        + WEIGHT_DECAY * master
    )
    return first_new, second_new, update


def whole_sum(value):
    return jnp.sum(jnp.sum(value, axis=0, keepdims=True), axis=1, keepdims=True)


def spread(parts, width):
    lane = lax.broadcasted_iota(jnp.int32, (1, width), 1)
    return sum(jnp.where(lane == index, part, 0.0) for index, part in enumerate(parts))


def dense_step_kernel(*refs):
    ins, outs = refs[:8], refs[8:]
    parts = []
    for at in range(2):
        grad, master, first, second = (ref[...] for ref in ins[4 * at : 4 * at + 4])
        first_new, second_new, update = lamb_step(grad, master, first, second)
        for ref, value in zip(outs[3 * at : 3 * at + 3], (first_new, second_new, update)):
            ref[...] = value
        parts += [whole_sum(master * master), whole_sum(update * update)]
    outs[6][...] = spread(parts, outs[6].shape[1])


def run_dense_step(in_parts, down_parts):
    shape = jax.ShapeDtypeStruct(in_parts[0].shape, F32)
    width = in_parts[0].shape[1]
    return pl.pallas_call(
        dense_step_kernel,
        out_shape=(shape,) * 6 + (jax.ShapeDtypeStruct((1, width), F32),),
        compiler_params=params(BIG),
    )(*in_parts, *down_parts)


def attn_step_kernel(
    left_ref, right_ref, qm_ref, qf_ref, qs_ref, om_ref, of_ref, os_ref, sums_a_ref, sums_b_ref, squares_ref,
    qg_ref, qf_out, qs_out, qu_ref, og_ref, of_out, os_out, ou_ref, small_ref,
):
    cols = qm_ref.shape[2]
    left, right = left_ref[...], right_ref[...]
    master_square, update_square = 0.0, 0.0
    for index, grad in enumerate((left[:, :cols], left[:, cols:], right[:, :cols])):
        master = qm_ref[index]
        first_new, second_new, update = lamb_step(grad, master, qf_ref[index], qs_ref[index])
        qg_ref[index] = grad
        qf_out[index] = first_new
        qs_out[index] = second_new
        qu_ref[index] = update
        master_square += whole_sum(master * master)
        update_square += whole_sum(update * update)
    grad = right[:, cols:].T
    master = om_ref[...]
    first_new, second_new, update = lamb_step(grad, master, of_ref[...], os_ref[...])
    og_ref[...] = grad
    of_out[...] = first_new
    os_out[...] = second_new
    ou_ref[...] = update
    dense = squares_ref[...]
    parts = [
        master_square, whole_sum(master * master), dense[:, 0:1], dense[:, 2:3],
        update_square, whole_sum(update * update), dense[:, 1:2], dense[:, 3:4],
    ]
    width = small_ref.shape[1]
    small_ref[...] = jnp.concatenate(
        [sums_a_ref[0:2], sums_b_ref[0:4], spread(parts, width), jnp.zeros((1, width), F32)], axis=0
    )


def run_attn_step(left, right, qkv, out, sums_a, sums_b, squares):
    q, o = jax.ShapeDtypeStruct(qkv[0].shape, F32), jax.ShapeDtypeStruct(out[0].shape, F32)
    return pl.pallas_call(
        attn_step_kernel,
        out_shape=(q,) * 4 + (o,) * 4 + (jax.ShapeDtypeStruct(sums_a.shape, F32),),
        compiler_params=params(BIG),
    )(left, right, *qkv, *out, sums_a, sums_b, squares)


def final_kernel(*refs):
    small_ref, vec_ref, vf_ref, vs_ref = refs[:4]
    masters, updates, new = refs[4:8], refs[8:12], refs[12:16]
    vg_out, vf_out, vs_out, v_out, norms_ref = refs[16:]
    norms = jnp.sqrt(small_ref[6:7])
    lane = lax.broadcasted_iota(jnp.int32, norms_ref.shape, 1)
    row = lax.broadcasted_iota(jnp.int32, norms_ref.shape, 0)
    table = jnp.zeros(norms_ref.shape, F32)
    for index in range(4):
        weight, update = norms[:, index : index + 1], norms[:, 4 + index : 5 + index]
        trust = weight / (update + ADAM_EPS)
        new[index][...] = masters[index][...] - LEARN_RATE * trust * updates[index][...]
        for at, value in enumerate((weight, update, trust)):
            table = jnp.where((lane == index) & (row == at), value, table)
    norms_ref[...] = table
    grad = small_ref[0:6]
    first_new = MOMENT_DECAY * vf_ref[...] + (1.0 - MOMENT_DECAY) * grad
    second_new = MOMENT_DECAY * vs_ref[...] + (1.0 - MOMENT_DECAY) * grad * grad
    vg_out[...] = grad
    vf_out[...] = first_new
    vs_out[...] = second_new
    v_out[...] = vec_ref[...] - LEARN_RATE * (first_new * (1.0 / CORRECTION)) / (
        jnp.sqrt(second_new * (1.0 / CORRECTION)) + ADAM_EPS
    )


def run_final(small, vectors, vec_first, vec_second, masters, updates):
    shape = lambda value: jax.ShapeDtypeStruct(value.shape, F32)
    flat = lambda value: value.reshape(-1, value.shape[-1])
    outs = pl.pallas_call(
        final_kernel,
        out_shape=tuple(shape(flat(m)) for m in masters)
        + (shape(vectors),) * 4
        + (jax.ShapeDtypeStruct((3, 4), F32),),
        compiler_params=params(BIG),
    )(small, vectors, vec_first, vec_second, *(flat(m) for m in masters), *(flat(u) for u in updates))
    new = [value.reshape(m.shape) for value, m in zip(outs[:4], masters)]
    return new, outs[4:]


def after(value, *others):
    return lax.optimization_barrier((value,) + others)[0]


def shards(
    rows,
    cotangent,
    group_ids,
    qkv_weight,
    out_weight,
    in_weight,
    down_weight,
    vectors,
    qkv_master,
    qkv_first,
    qkv_second,
    out_master,
    out_first,
    out_second,
    in_master,
    in_first,
    in_second,
    down_master,
    down_first,
    down_second,
    vec_first,
    vec_second,
):
    count = lax.axis_size("dp")
    width = rows.shape[1]
    half = width // 2
    nbits = count.bit_length() - 1
    me = lax.axis_index("dp").astype(jnp.int32)
    rel = jnp.arange(count, dtype=jnp.int32) ^ me
    order1 = tuple(range(nbits))
    order2 = (1, 0) + order1[2:]
    pos, pos2 = (
        sum(((rel >> bit) & 1) << (nbits - 1 - place) for place, bit in enumerate(order))
        for order in (order1, order2)
    )
    low = (me & 1).reshape(1)

    onehot = (group_ids[:, None] == jnp.arange(GROUPS, dtype=jnp.int32)[None, :]).astype(F32)
    counts = jnp.sum(onehot, axis=0)

    attn_w = jnp.concatenate(
        [jnp.swapaxes(qkv_weight, 1, 2).reshape(-1, width), out_weight], axis=0
    )
    pieces = [
        lax.dynamic_slice_in_dim(weight, low[0] * half, half, axis)
        for weight, axis in ((attn_w, 0), (in_weight, 0), (down_weight, 1))
    ]
    counts, pieces[0] = lax.optimization_barrier((counts, pieces[0]))
    attn_far = swap(pieces[0], "mp", 2)
    counts = counts + swap(counts, "mp", 2)
    counts, *pieces = lax.optimization_barrier((counts, *pieces[1:]))
    in_far, down_far = (swap(piece, "mp", 2) for piece in pieces)
    near = [swap(weight, "mp", 1) for weight in (attn_w, in_weight, down_weight)]
    counts, attn_one, in_one, down_one = lax.optimization_barrier((counts, *near))
    counts = counts + swap(counts, "dp", 1)
    x, xt, xt2 = run_start(pos, pos2, rows, vectors, count)
    xt, xt2 = turned_order(xt, pos, count), turned_order(xt2, pos2, count)
    acc, s1, p1, s0, p0 = run_attn_one(x, rows, vectors, attn_one, attn_w)
    attn_far, counts, acc = lax.optimization_barrier((attn_far, counts, acc))
    attn_two = (attn_far, swap(attn_far, "dp", 1))
    counts = counts + swap(counts, "mp", 1)
    for bit in order1[1:]:
        counts = counts + swap(counts, "dp", 1 << bit)
    image_weight = jnp.sqrt(jnp.sum(counts) / (GROUPS * jnp.sum(onehot * counts, axis=1)))
    gout, goutt = run_gout(pos2, image_weight, cotangent, count)
    goutt = turned_order(goutt, pos2, count)
    attn_other, in_far, gout, acc = lax.optimization_barrier((attn_two[1], in_far, gout, acc))
    in_two = (in_far, swap(in_far, "dp", 1))
    attn_two = (attn_far, attn_other)
    attn_three = tuple(swap(piece, "mp", 1) for piece in attn_two)
    first, mid, midt, s3, p3, s2, p2 = run_attn_two(
        pos, low, x, acc, vectors, attn_three, attn_two, count
    )
    midt = turned_order(midt, pos, count)
    y, dm, gi1, gd1 = run_ffn_near(mid, midt, gout, goutt, in_one, down_one)
    gi1, gd1, y, down_far, _ = lax.optimization_barrier((gi1, gd1, y, down_far, in_two[1]))
    down_two = (down_far, swap(down_far, "dp", 1))
    y, dm, gi0, gd0 = run_ffn_near(mid, midt, gout, goutt, in_weight, down_weight, y, dm)
    in_near, down_near = meet(gi0, gi1), meet(gd0, gd1)
    y, down_other, in_sent, down_sent = lax.optimization_barrier(
        (y, down_two[1], upper(in_near), upper(down_near))
    )
    in_near, down_near = fold(in_near, order1[0], in_sent), fold(down_near, order2[0], down_sent)
    down_two = (down_far, down_other)
    in_three, down_three = (
        tuple(swap(piece, "mp", 1) for piece in pieces) for pieces in (in_two, down_two)
    )
    y, dm, gi3, gd3 = run_ffn_far(low, mid, midt, gout, goutt, in_three, down_three, y, dm)
    out_rows, gfirst, gfl, gft, sums_b, gi2, gd2 = run_ffn_last(
        pos2, low, image_weight, mid, midt, gout, goutt, in_two, down_two,
        y, dm, first, cotangent, vectors, count,
    )
    gft = turned_order(gft, pos2, count)
    in_far, down_far = meet(gi2, gi3), meet(gd2, gd3)
    gfl, in_sent, down_sent, _, _ = lax.optimization_barrier(
        (gfl, upper(in_far), upper(down_far), in_near[-1], down_near[-1])
    )
    in_far, down_far = fold(in_far, order1[0], in_sent), fold(down_far, order2[0], down_sent)
    gin, ga3 = run_back_far(low, gfl, xt, xt2, gft, attn_three, (s3, p3))
    gin, ga2 = run_back_far(low, gfl, xt, xt2, gft, attn_two, (s2, p2), gin)
    both = meet(ga2, ga3)
    left_far, right_far = columns(both, slice(0, half)), columns(both, slice(half, None))
    gin, left_sent, right_sent, in_sent, down_sent = lax.optimization_barrier(
        (gin, upper(left_far), upper(right_far), total(in_far).astype(BF16), total(down_far).astype(BF16))
    )
    left_far, right_far = fold(left_far, order1[0], left_sent), fold(right_far, order2[0], right_sent)
    in_grad, down_grad = join(in_near, None, in_sent), join(down_near, None, down_sent)
    gin, ga1 = run_back_near(gfl, xt, xt2, gft, attn_one, (s1, p1), gin)
    ga1, *_ = lax.optimization_barrier((ga1, left_far[-1], right_far[-1]))
    input_grad, sums_a, ga0 = run_back_last(
        gfl, xt, xt2, gft, attn_w, (s0, p0), gin, rows, gfirst, vectors
    )
    both = meet(ga0, ga1)
    left_near, right_near = columns(both, slice(0, half)), columns(both, slice(half, None))
    left_far, right_far = fold(left_far, order1[1]), fold(right_far, order2[1])
    left_near, right_near = fold(left_near, order1[0]), fold(right_near, order2[0])
    near_back, far_back = lax.optimization_barrier(
        ((left_near[-1], right_near[-1]), (left_far[-1], right_far[-1]))
    )
    left_near, right_near = left_near[:-1] + near_back[:1], right_near[:-1] + near_back[1:]
    left_far, right_far = left_far[:-1] + far_back[:1], right_far[:-1] + far_back[1:]
    left_near, right_near = fold(left_near, order1[1]), fold(right_near, order2[1])
    in_grad, down_grad = fold(in_grad, order1[1]), fold(down_grad, order2[1])
    for bit in order1[2:]:
        in_grad, down_grad = fold(in_grad, bit), fold(down_grad, bit)
        left_far, right_far = fold_two(left_far, right_far, bit)
        left_near, right_near = fold_two(left_near, right_near, bit)
    left, right = join_two(left_near, left_far, right_near, right_far)
    in_grad, down_grad, left, right = (total(terms) for terms in (in_grad, down_grad, left, right))

    down_state = (down_master.T, down_first.T, down_second.T)
    in_fn, in_sn, in_up, down_fn, down_sn, down_up, squares = run_dense_step(
        (in_grad, in_master, in_first, in_second), (down_grad,) + down_state
    )
    qkv_grad, qkv_fn, qkv_sn, qkv_up, out_grad, out_fn, out_sn, out_up, small = run_attn_step(
        left, right, (qkv_master, qkv_first, qkv_second), (out_master, out_first, out_second),
        sums_a, sums_b, squares,
    )
    new, vec_outs = run_final(
        all_sum(small), vectors, vec_first, vec_second,
        (qkv_master, out_master, in_master, down_state[0]), (qkv_up, out_up, in_up, down_up),
    )
    return (
        out_rows,
        input_grad,
        qkv_grad,
        out_grad,
        in_grad,
        down_grad.T,
        qkv_fn,
        qkv_sn,
        new[0],
        out_fn,
        out_sn,
        new[1],
        in_fn,
        in_sn,
        new[2],
        down_fn.T,
        down_sn.T,
        new[3].T,
    ) + tuple(vec_outs)


def solution(mesh):
    rows = P(("dp", "mp"), None)
    qkv_state = P(None, "dp", "mp")
    out_state = P("mp", "dp")
    in_state = P("dp", "mp")
    in_specs = (
        (rows, rows, P(("dp", "mp")), P(None, None, "mp"), P("mp", None), P(None, "mp"), P("mp", None), P())
        + (qkv_state,) * 3
        + (out_state,) * 3
        + (in_state,) * 3
        + (out_state,) * 3
        + (P(), P())
    )
    out_specs = (
        (rows, rows, qkv_state, out_state, in_state, out_state)
        + (qkv_state,) * 3
        + (out_state,) * 3
        + (in_state,) * 3
        + (out_state,) * 3
        + (P(),) * 5
    )
    return jax.shard_map(shards, mesh=mesh, in_specs=in_specs, out_specs=out_specs, check_vma=False)
```

```python
import math

import jax
import jax.numpy as jnp
from jax import lax
from jax.experimental import pallas as pl
from jax.experimental.pallas import tpu as pltpu
from jax.sharding import PartitionSpec as P

HEAD_DIM = 64
PATCHES = 256
GROUPS = 8
STEP = 5

NORM_EPS = 1e-06
ADAM_EPS = 1e-06
MOMENT_DECAY = 0.5
LEARN_RATE = 0.5
WEIGHT_DECAY = 0.01
SCALE = HEAD_DIM ** (-0.5)

F32 = jnp.float32
BF16 = jnp.bfloat16
MB = 1024 * 1024
BIG = 16


def mm(left, right):
    return jnp.dot(left, right, preferred_element_type=F32)


def mm_nt(left, right):
    return lax.dot_general(left, right, (((1,), (1,)), ((), ())), preferred_element_type=F32)


def mm_tn(left, right):
    return lax.dot_general(left, right, (((0,), (0,)), ((), ())), preferred_element_type=F32)


def layer_stats(values):
    center = values - jnp.mean(values, axis=-1, keepdims=True)
    inverse = lax.rsqrt(jnp.mean(center * center, axis=-1, keepdims=True) + NORM_EPS)
    return center * inverse, inverse


def norm_back(grad_normed, normed, inverse):
    return inverse * (
        grad_normed
        - jnp.mean(grad_normed, axis=-1, keepdims=True)
        - normed * jnp.mean(grad_normed * normed, axis=-1, keepdims=True)
    )


def gelu_pair(t):
    size = jnp.abs(t) * (2.0**-0.5)
    k = 1.0 / (1.0 + 0.3275911 * size)
    bell = jnp.exp(-size * size)
    poly = k * (
        0.254829592
        + k * (-0.284496736 + k * (1.421413741 + k * (-1.453152027 + k * 1.061405429)))
    )
    tail = 0.5 * poly * bell
    cdf = jnp.where(t < 0, tail, 1.0 - tail)
    return t * cdf, cdf + t * bell * (1.0 / math.sqrt(2.0 * math.pi))


def put_turned(out_ref, value, pos_ref, count, start):
    turned = value.T
    part = turned.shape[0] // count
    width = turned.shape[1]
    here = pl.ds(start, width)
    if len(out_ref.shape) == 2:
        out_ref[:, here] = turned
        return
    for j in range(count):
        out_ref[pos_ref[j], :, here] = turned[j * part : (j + 1) * part]


def turned_shape(width, rows, count):
    part = width // count
    if part % 16 == 0:
        return (count, part, rows)
    return (width, rows)


def turned_order(turned, pos, count):
    width = turned.shape[0] if turned.ndim == 2 else turned.shape[0] * turned.shape[1]
    rows = turned.shape[-1]
    if turned.ndim == 2:
        shaped = turned.reshape(count, width // count, rows)
        turned = jnp.zeros_like(shaped).at[pos].set(shaped)
    return turned.reshape(width, rows)


def params(limit, **more):
    return pltpu.CompilerParams(vmem_limit_bytes=limit * MB, **more)


def full(shape):
    return pl.BlockSpec(shape, lambda *_: (0,) * len(shape), pipeline_mode=pl.Buffered(1))


SMEM = pl.BlockSpec(memory_space=pltpu.SMEM)


def start_kernel(pos_ref, rows_ref, vec_ref, x_ref, xt_ref, *, count):
    width, rows = rows_ref.shape[1], rows_ref.shape[0]
    for start in range(0, rows, PATCHES):
        normed, _ = layer_stats(rows_ref[start : start + PATCHES].astype(F32))
        low = (normed * vec_ref[0:1] + vec_ref[1:2]).astype(BF16)
        x_ref[start : start + PATCHES] = low
        put_turned(xt_ref, low, pos_ref, count, start)


def run_start(pos, rows, vectors, count):
    r, d = rows.shape
    return pl.pallas_call(
        lambda *refs: start_kernel(*refs, count=count),
        out_shape=(
            jax.ShapeDtypeStruct((r, d), BF16),
            jax.ShapeDtypeStruct(turned_shape(d, r, count), BF16),
        ),
        in_specs=[SMEM, pl.BlockSpec(memory_space=pltpu.VMEM), pl.BlockSpec(memory_space=pltpu.VMEM)],
        compiler_params=params(BIG),
    )(pos, rows, vectors)


def gout_kernel(pos_ref, weight_ref, cot_ref, g_ref, gt_ref, *, count):
    rows = cot_ref.shape[0]
    for index in range(rows // PATCHES):
        start = index * PATCHES
        low = (cot_ref[start : start + PATCHES].astype(F32) * weight_ref[index]).astype(BF16)
        g_ref[start : start + PATCHES] = low
        put_turned(gt_ref, low, pos_ref, count, start)


def run_gout(pos, weight, cot, count):
    r, d = cot.shape
    return pl.pallas_call(
        lambda *refs: gout_kernel(*refs, count=count),
        out_shape=(
            jax.ShapeDtypeStruct((r, d), BF16),
            jax.ShapeDtypeStruct(turned_shape(d, r, count), BF16),
        ),
        in_specs=[SMEM, SMEM, pl.BlockSpec(memory_space=pltpu.VMEM)],
        compiler_params=params(BIG),
    )(pos, weight, cot)


def attend_shard(x, w_ref, saved_ref, probs_ref):
    cols = w_ref.shape[0] // 4
    qkv = mm_nt(x, w_ref[: 3 * cols]).astype(BF16)
    saved_ref[:, : 3 * cols] = qkv
    mixed = []
    for h in range(cols // HEAD_DIM):
        at = h * HEAD_DIM
        q = qkv[:, at : at + HEAD_DIM] * SCALE
        k = qkv[:, cols + at : cols + at + HEAD_DIM]
        v = qkv[:, 2 * cols + at : 2 * cols + at + HEAD_DIM]
        scores = mm_nt(k, q)
        expo = jnp.exp(scores - jnp.max(scores, axis=0, keepdims=True))
        probs = (expo * (1.0 / jnp.sum(expo, axis=0, keepdims=True))).astype(BF16)
        probs_ref[h] = probs
        mixed.append(mm_tn(probs, v).astype(BF16))
    mixed = jnp.concatenate(mixed, axis=1)
    saved_ref[:, 3 * cols :] = mixed
    return mm(mixed, w_ref[3 * cols :])


def attn_one_kernel(x_ref, rows_ref, vec_ref, wa_ref, wb_ref, acc_ref, sa_ref, pa_ref, sb_ref, pb_ref):
    x = x_ref[...]
    term = attend_shard(x, wa_ref, sa_ref, pa_ref)
    term += attend_shard(x, wb_ref, sb_ref, pb_ref)
    acc_ref[...] = rows_ref[...].astype(F32) + term + vec_ref[4:5]


def join_halves(low_ref, own_ref, other_ref, whole_ref):
    half = own_ref.shape[0]

    @pl.when(low_ref[0] == 0)
    def _():
        whole_ref[:half] = own_ref[...]
        whole_ref[half:] = other_ref[...]

    @pl.when(low_ref[0] != 0)
    def _():
        whole_ref[:half] = other_ref[...]
        whole_ref[half:] = own_ref[...]


def join_pair(low_ref, halves, wholes):
    @pl.when(pl.program_id(0) == 0)
    def _():
        for (own, other), whole in zip(halves, wholes):
            join_halves(low_ref, own, other, whole)


def attn_two_kernel(
    pos_ref, low_ref, x_ref, acc_ref, vec_ref, ha_ref, ia_ref, hb_ref, ib_ref,
    first_ref, mid_ref, midt_ref, sa_ref, pa_ref, sb_ref, pb_ref, wa_ref, wb_ref, *, count,
):
    join_pair(low_ref, ((ha_ref, ia_ref), (hb_ref, ib_ref)), (wa_ref, wb_ref))
    x = x_ref[...]
    term = attend_shard(x, wa_ref, sa_ref, pa_ref)
    term += attend_shard(x, wb_ref, sb_ref, pb_ref)
    first = acc_ref[...] + term
    first_ref[...] = first
    normed, _ = layer_stats(first)
    low = (normed * vec_ref[2:3] + vec_ref[3:4]).astype(BF16)
    mid_ref[...] = low
    put_turned(midt_ref, low, pos_ref, count, 0)


def image_block(d):
    return pl.BlockSpec((PATCHES, d), lambda i: (i, 0))


def saved_outputs(r, d, heads):
    images = r // PATCHES
    shapes = (
        jax.ShapeDtypeStruct((r, d), BF16),
        jax.ShapeDtypeStruct((images * heads, PATCHES, PATCHES), BF16),
    )
    specs = [image_block(d), pl.BlockSpec((heads, PATCHES, PATCHES), lambda i: (i, 0, 0))]
    return shapes, specs


def cost(micros):
    return pl.CostEstimate(flops=int(micros * 5 * 1e9), bytes_accessed=int(micros * 5 * 3e6), transcendentals=0)


def run_attn_one(x, rows, vectors, wa, wb):
    r, d = x.shape
    heads = d // 4 // HEAD_DIM
    shapes, specs = saved_outputs(r, d, heads)
    return pl.pallas_call(
        attn_one_kernel,
        grid=(r // PATCHES,),
        out_shape=(jax.ShapeDtypeStruct((r, d), F32),) + shapes * 2,
        in_specs=[image_block(d), image_block(d), full(vectors.shape), full((d, d)), full((d, d))],
        out_specs=[image_block(d)] + specs * 2,
        compiler_params=params(BIG),
        cost_estimate=cost(7),
    )(x, rows, vectors, wa, wb)


def run_attn_two(pos, low, x, acc, vectors, wa, wb, count):
    r, d = x.shape
    heads = d // 4 // HEAD_DIM
    shapes, specs = saved_outputs(r, d, heads)
    tshape = turned_shape(d, r, count)
    tspec = pl.BlockSpec(
        tshape[:-1] + (PATCHES,), lambda i: (0,) * (len(tshape) - 1) + (i,)
    )
    return pl.pallas_call(
        lambda *refs: attn_two_kernel(*refs, count=count),
        grid=(r // PATCHES,),
        out_shape=(
            jax.ShapeDtypeStruct((r, d), F32),
            jax.ShapeDtypeStruct((r, d), BF16),
            jax.ShapeDtypeStruct(tshape, BF16),
        )
        + shapes * 2,
        in_specs=[SMEM, SMEM, image_block(d), image_block(d), full(vectors.shape)]
        + [full((d // 2, d))] * 4,
        out_specs=[image_block(d), image_block(d), tspec] + specs * 2,
        scratch_shapes=[pltpu.VMEM((d, d), BF16)] * 2,
        compiler_params=params(BIG),
        cost_estimate=cost(7),
    )(pos, low, x, acc, vectors, *wa, *wb)


TILES = 3


def ffn_tile(mid_ref, midt_ref, g_ref, gt_ref, w_in, w_down, gi_ref, gd_ref, y_ref, dm_ref):
    pre = mm(mid_ref[...], w_in)
    dact = mm_nt(g_ref[...], w_down)
    activ, slope = gelu_pair(pre)
    activ = activ.astype(BF16)
    dpre = (dact * slope).astype(BF16)
    y_ref[...] += mm(activ, w_down)
    dm_ref[...] += mm_nt(dpre, w_in)
    gd_ref[...] = mm(gt_ref[...], activ).astype(BF16)
    gi_ref[...] = mm(midt_ref[...], dpre).astype(BF16)


def joined(low_ref, own_ref, other_ref, axis):
    own, other = own_ref[...], other_ref[...]
    return jnp.where(
        low_ref[0] == 0,
        jnp.concatenate([own, other], axis=axis),
        jnp.concatenate([other, own], axis=axis),
    )


def ffn_near_kernel(mid_ref, midt_ref, g_ref, gt_ref, in_ref, down_ref, *rest):
    *before, y_ref, dm_ref, gi_ref, gd_ref = rest

    @pl.when(pl.program_id(0) == 0)
    def _():
        y_ref[...] = before[0][...] if before else jnp.zeros_like(y_ref)
        dm_ref[...] = before[1][...] if before else jnp.zeros_like(dm_ref)

    ffn_tile(mid_ref, midt_ref, g_ref, gt_ref, in_ref[...], down_ref[...], gi_ref, gd_ref, y_ref, dm_ref)


def ffn_far_kernel(
    low_ref, mid_ref, midt_ref, g_ref, gt_ref, ia_ref, ib_ref, da_ref, db_ref, y_in_ref, dm_in_ref,
    y_ref, dm_ref, gi_ref, gd_ref,
):
    @pl.when(pl.program_id(0) == 0)
    def _():
        y_ref[...] = y_in_ref[...]
        dm_ref[...] = dm_in_ref[...]

    w_in, w_down = joined(low_ref, ia_ref, ib_ref, 0), joined(low_ref, da_ref, db_ref, 1)
    ffn_tile(mid_ref, midt_ref, g_ref, gt_ref, w_in, w_down, gi_ref, gd_ref, y_ref, dm_ref)


def ffn_last_kernel(
    pos_ref, low_ref, weight_ref, mid_ref, midt_ref, g_ref, gt_ref, ia_ref, ib_ref, da_ref, db_ref,
    y_in_ref, dm_in_ref, first_ref, cot_ref, vec_ref,
    out_ref, gf_ref, gfl_ref, gft_ref, sums_ref, gi_ref, gd_ref, y_ref, dm_ref, *, count,
):
    ffn_far_kernel(
        low_ref, mid_ref, midt_ref, g_ref, gt_ref, ia_ref, ib_ref, da_ref, db_ref, y_in_ref, dm_in_ref,
        y_ref, dm_ref, gi_ref, gd_ref,
    )

    @pl.when(pl.program_id(0) == pl.num_programs(0) - 1)
    def _():
        chunk = 128

        def body(index, sums):
            start = pl.multiple_of(index * chunk, chunk)
            here = pl.ds(start, chunk)
            first = first_ref[here, :]
            normed, inverse = layer_stats(first)
            out_ref[here, :] = (first + y_ref[here, :] + vec_ref[5:6]).astype(BF16)
            dmid = dm_ref[here, :]
            gout = cot_ref[here, :].astype(F32) * weight_ref[start // PATCHES]
            gfirst = gout + norm_back(dmid * vec_ref[2:3], normed, inverse)
            gf_ref[here, :] = gfirst
            low = gfirst.astype(BF16)
            gfl_ref[here, :] = low
            put_turned(gft_ref, low, pos_ref, count, start)
            terms = (dmid * normed, dmid, gfirst, gout)
            return tuple(a + jnp.sum(b, axis=0, keepdims=True) for a, b in zip(sums, terms))

        zero = jnp.zeros((1, first_ref.shape[1]), F32)
        sums = lax.fori_loop(0, first_ref.shape[0] // chunk, body, (zero,) * 4)
        sums_ref[...] = jnp.concatenate(sums + sums, axis=0)


def ffn_specs(d, parts):
    tile = d // TILES
    cols = lambda rows: pl.BlockSpec((rows, tile), lambda i: (0, i))
    w_down = pl.BlockSpec((tile, d // parts), lambda i: (i, 0))
    return [cols(d // parts)] * parts + [w_down] * parts, [cols(d)] * 2


def run_ffn_near(mid, midt, g, gt, w_in, w_down, *before):
    r, d = mid.shape
    w_specs, g_specs = ffn_specs(d, 1)
    grad = jax.ShapeDtypeStruct((d, d), BF16)
    return pl.pallas_call(
        ffn_near_kernel,
        grid=(TILES,),
        out_shape=(jax.ShapeDtypeStruct((r, d), F32),) * 2 + (grad,) * 2,
        in_specs=[full((r, d)), full((d, r)), full((r, d)), full((d, r))] + w_specs + [full((r, d))] * len(before),
        out_specs=[full((r, d))] * 2 + g_specs,
        compiler_params=params(BIG),
        cost_estimate=cost(6),
    )(mid, midt, g, gt, w_in, w_down, *before)


def run_ffn_far(low, mid, midt, g, gt, w_in, w_down, y, dm):
    r, d = mid.shape
    w_specs, g_specs = ffn_specs(d, 2)
    grad = jax.ShapeDtypeStruct((d, d), BF16)
    return pl.pallas_call(
        ffn_far_kernel,
        grid=(TILES,),
        out_shape=(jax.ShapeDtypeStruct((r, d), F32),) * 2 + (grad,) * 2,
        in_specs=[SMEM, full((r, d)), full((d, r)), full((r, d)), full((d, r))] + w_specs + [full((r, d))] * 2,
        out_specs=[full((r, d))] * 2 + g_specs,
        compiler_params=params(BIG),
        cost_estimate=cost(6),
    )(low, mid, midt, g, gt, *w_in, *w_down, y, dm)


def run_ffn_last(pos, low, weight, mid, midt, g, gt, w_in, w_down, y, dm, first, cot, vectors, count):
    r, d = mid.shape
    w_specs, g_specs = ffn_specs(d, 2)
    grad = jax.ShapeDtypeStruct((d, d), BF16)
    tshape = turned_shape(d, r, count)
    return pl.pallas_call(
        lambda *refs: ffn_last_kernel(*refs, count=count),
        grid=(TILES,),
        out_shape=(
            jax.ShapeDtypeStruct((r, d), BF16),
            jax.ShapeDtypeStruct((r, d), F32),
            jax.ShapeDtypeStruct((r, d), BF16),
            jax.ShapeDtypeStruct(tshape, BF16),
            jax.ShapeDtypeStruct((8, d), F32),
        )
        + (grad,) * 2,
        in_specs=[SMEM, SMEM, SMEM, full((r, d)), full((d, r)), full((r, d)), full((d, r))]
        + w_specs
        + [full((r, d))] * 4
        + [full(vectors.shape)],
        out_specs=[full((r, d)), full((r, d)), full((r, d)), full(tshape), full((8, d))] + g_specs,
        scratch_shapes=[pltpu.VMEM((r, d), F32)] * 2,
        compiler_params=params(BIG),
        cost_estimate=cost(8),
    )(pos, low, weight, mid, midt, g, gt, *w_in, *w_down, y, dm, first, cot, vectors)


def attend_back_shard(gf, w_ref, saved_ref, probs_ref, keep_ref):
    cols = w_ref.shape[0] // 4
    start = pl.multiple_of(pl.program_id(0) * PATCHES, PATCHES)
    dmix = mm_nt(gf, w_ref[3 * cols :]).astype(BF16)
    dq, dk, dv = [], [], []
    for h in range(cols // HEAD_DIM):
        at = h * HEAD_DIM
        q = saved_ref[:, at : at + HEAD_DIM]
        k = saved_ref[:, cols + at : cols + at + HEAD_DIM]
        v = saved_ref[:, 2 * cols + at : 2 * cols + at + HEAD_DIM]
        do = dmix[:, at : at + HEAD_DIM]
        probs = probs_ref[h]
        dv.append(mm(probs, do).astype(BF16))
        dp = mm_nt(v, do)
        wide = probs.astype(F32)
        ds = (SCALE * wide * (dp - jnp.sum(wide * dp, axis=0, keepdims=True))).astype(BF16)
        dq.append(mm_tn(ds, k).astype(BF16))
        dk.append(mm(ds, q).astype(BF16))
    dqkv = jnp.concatenate(dq + dk + dv, axis=1)
    keep_ref[pl.ds(start, PATCHES), : 3 * cols] = dqkv
    keep_ref[pl.ds(start, PATCHES), 3 * cols :] = saved_ref[:, 3 * cols :]
    return mm(dqkv, w_ref[: 3 * cols])


def attn_grad(xt_ref, gft_ref, keep_ref, g_ref):
    cols = keep_ref.shape[1] // 4
    g_ref[:, : 3 * cols] = mm(xt_ref[...], keep_ref[:, : 3 * cols]).astype(BF16)
    g_ref[:, 3 * cols :] = mm(gft_ref[...], keep_ref[:, 3 * cols :]).astype(BF16)


def back_body(gf_ref, xt_ref, gft_ref, w_ref, saved_ref, probs_ref, g_ref, keep_ref):
    term = attend_back_shard(gf_ref[...], w_ref, saved_ref, probs_ref, keep_ref)

    @pl.when(pl.program_id(0) == pl.num_programs(0) - 1)
    def _():
        attn_grad(xt_ref, gft_ref, keep_ref, g_ref)

    return term


def back_far_kernel(
    low_ref, gf_ref, xt_ref, gft_ref, saved_ref, probs_ref, h_ref, i_ref, *rest
):
    *before, acc_ref, g_ref, keep_ref, w_ref = rest
    join_pair(low_ref, ((h_ref, i_ref),), (w_ref,))
    term = back_body(gf_ref, xt_ref, gft_ref, w_ref, saved_ref, probs_ref, g_ref, keep_ref)
    if before:
        acc_ref[...] = term + before[0][...]
    else:
        acc_ref[...] = jnp.zeros_like(acc_ref)
        acc_ref[...] += term


def back_near_kernel(
    gf_ref, xt_ref, gft_ref, saved_ref, probs_ref, w_ref, before_ref, acc_ref, g_ref, keep_ref
):
    term = back_body(gf_ref, xt_ref, gft_ref, w_ref, saved_ref, probs_ref, g_ref, keep_ref)
    acc_ref[...] = term + before_ref[...]


def back_last_kernel(
    gf_ref, xt_ref, gft_ref, saved_ref, probs_ref, w_ref, before_ref, rows_ref, gfirst_ref, vec_ref,
    ig_ref, sums_ref, g_ref, keep_ref,
):
    term = back_body(gf_ref, xt_ref, gft_ref, w_ref, saved_ref, probs_ref, g_ref, keep_ref)
    grad_in = before_ref[...] + term
    normed, inverse = layer_stats(rows_ref[...].astype(F32))
    ig_ref[...] = gfirst_ref[...] + norm_back(grad_in * vec_ref[0:1], normed, inverse)
    one = jnp.sum(grad_in * normed, axis=0, keepdims=True)
    two = jnp.sum(grad_in, axis=0, keepdims=True)
    sums = jnp.concatenate([one, two] * 4, axis=0)

    @pl.when(pl.program_id(0) == 0)
    def _():
        sums_ref[...] = sums

    @pl.when(pl.program_id(0) > 0)
    def _():
        sums_ref[...] += sums


def back_call(kernel, ops, specs, outs, out_specs, far):
    gfl = ops[1] if far else ops[0]
    r, d = gfl.shape
    heads = d // 4 // HEAD_DIM
    _, saved_specs = saved_outputs(r, d, heads)
    keep, whole = pltpu.VMEM((r, d), BF16), pltpu.VMEM((d, d), BF16)
    return pl.pallas_call(
        kernel,
        grid=(r // PATCHES,),
        out_shape=tuple(outs) + (jax.ShapeDtypeStruct((d, d), BF16),),
        in_specs=([SMEM] if far else []) + [image_block(d)] + [full((d, r))] * 2 + saved_specs + specs,
        out_specs=out_specs + [full((d, d))],
        scratch_shapes=[keep, whole] if far else [keep],
        compiler_params=params(BIG),
        cost_estimate=cost(6),
    )(*ops)


def run_back_far(low, gfl, xt, gft, halves, saved, *acc):
    r, d = gfl.shape
    return back_call(
        back_far_kernel,
        [low, gfl, xt, gft, *saved, *halves, *acc],
        [full((d // 2, d))] * 2 + [image_block(d)] * len(acc),
        [jax.ShapeDtypeStruct((r, d), F32)], [image_block(d)], True,
    )


def run_back_near(gfl, xt, gft, weight, saved, acc):
    r, d = gfl.shape
    return back_call(
        back_near_kernel,
        [gfl, xt, gft, *saved, weight, acc],
        [full((d, d)), image_block(d)],
        [jax.ShapeDtypeStruct((r, d), F32)], [image_block(d)], False,
    )


def run_back_last(gfl, xt, gft, weight, saved, acc, rows, gfirst, vectors):
    r, d = gfl.shape
    return back_call(
        back_last_kernel,
        [gfl, xt, gft, *saved, weight, acc, rows, gfirst, vectors],
        [full((d, d))] + [image_block(d)] * 3 + [full(vectors.shape)],
        [jax.ShapeDtypeStruct((r, d), F32), jax.ShapeDtypeStruct((8, d), F32)],
        [image_block(d), full((8, d))], False,
    )


def swap(value, axis, bit):
    size = lax.axis_size(axis)
    return lax.ppermute(value, axis, [(i, i ^ bit) for i in range(size)])


def all_sum(value):
    for axis in ("mp", "dp"):
        bit = 1
        while bit < lax.axis_size(axis):
            value = value + swap(value, axis, bit)
            bit *= 2
    return value


def total(terms, rows=slice(None)):
    return sum(term[rows].astype(F32) for term in terms)


def columns(terms, cut):
    return tuple(term[:, cut] for term in terms)


def meet(own, partner):
    return own, swap(partner, "mp", 1)


def upper(terms):
    return total(terms, slice(terms[0].shape[0] // 2, None)).astype(BF16)


def fold(terms, bit, sent=None):
    half = terms[0].shape[0] // 2
    back = swap(upper(terms) if sent is None else sent, "dp", 1 << bit)
    return tuple(term[:half] for term in terms) + (back,)


def stacked(move, *sums):
    moved = move(jnp.concatenate(sums, axis=0))
    edges = [0]
    for value in sums:
        edges.append(edges[-1] + value.shape[0])
    return [moved[low:high] for low, high in zip(edges, edges[1:])]


def join(near, far, sent=None):
    return near + (swap(total(far).astype(BF16) if sent is None else sent, "mp", 2),)


def join_two(near_a, far_a, near_b, far_b):
    a, b = stacked(
        lambda value: swap(value, "mp", 2), total(far_a).astype(BF16), total(far_b).astype(BF16)
    )
    return near_a + (a,), near_b + (b,)


def fold_two(terms_a, terms_b, bit):
    half_a, half_b = terms_a[0].shape[0] // 2, terms_b[0].shape[0] // 2
    a, b = stacked(lambda value: swap(value, "dp", 1 << bit), upper(terms_a), upper(terms_b))
    return tuple(term[:half_a] for term in terms_a) + (a,), tuple(term[:half_b] for term in terms_b) + (b,)


CORRECTION = 1.0 - MOMENT_DECAY**STEP


def lamb_step(grad, master, first, second):
    first_new = MOMENT_DECAY * first + (1.0 - MOMENT_DECAY) * grad
    second_new = MOMENT_DECAY * second + (1.0 - MOMENT_DECAY) * grad * grad
    update = (
        first_new * (1.0 / CORRECTION) / (jnp.sqrt(second_new * (1.0 / CORRECTION)) + ADAM_EPS)
        + WEIGHT_DECAY * master
    )
    return first_new, second_new, update


def whole_sum(value):
    return jnp.sum(jnp.sum(value, axis=0, keepdims=True), axis=1, keepdims=True)


def spread(parts, width):
    lane = lax.broadcasted_iota(jnp.int32, (1, width), 1)
    return sum(jnp.where(lane == index, part, 0.0) for index, part in enumerate(parts))


def dense_step_kernel(*refs):
    ins, outs = refs[:8], refs[8:]
    parts = []
    for at in range(2):
        grad, master, first, second = (ref[...] for ref in ins[4 * at : 4 * at + 4])
        first_new, second_new, update = lamb_step(grad, master, first, second)
        for ref, value in zip(outs[3 * at : 3 * at + 3], (first_new, second_new, update)):
            ref[...] = value
        parts += [whole_sum(master * master), whole_sum(update * update)]
    outs[6][...] = spread(parts, outs[6].shape[1])


def run_dense_step(in_parts, down_parts):
    shape = jax.ShapeDtypeStruct(in_parts[0].shape, F32)
    width = in_parts[0].shape[1]
    return pl.pallas_call(
        dense_step_kernel,
        out_shape=(shape,) * 6 + (jax.ShapeDtypeStruct((1, width), F32),),
        compiler_params=params(BIG),
    )(*in_parts, *down_parts)


def attn_step_kernel(
    sum_ref, qm_ref, qf_ref, qs_ref, om_ref, of_ref, os_ref, sums_a_ref, sums_b_ref, squares_ref,
    qg_ref, qf_out, qs_out, qu_ref, og_ref, of_out, os_out, ou_ref, small_ref,
):
    cols = qm_ref.shape[2]
    whole = sum_ref[...]
    master_square, update_square = 0.0, 0.0
    for index, grad in enumerate(whole[:, at * cols : (at + 1) * cols] for at in range(3)):
        master = qm_ref[index]
        first_new, second_new, update = lamb_step(grad, master, qf_ref[index], qs_ref[index])
        qg_ref[index] = grad
        qf_out[index] = first_new
        qs_out[index] = second_new
        qu_ref[index] = update
        master_square += whole_sum(master * master)
        update_square += whole_sum(update * update)
    grad = whole[:, 3 * cols :].T
    master = om_ref[...]
    first_new, second_new, update = lamb_step(grad, master, of_ref[...], os_ref[...])
    og_ref[...] = grad
    of_out[...] = first_new
    os_out[...] = second_new
    ou_ref[...] = update
    dense = squares_ref[...]
    parts = [
        master_square, whole_sum(master * master), dense[:, 0:1], dense[:, 2:3],
        update_square, whole_sum(update * update), dense[:, 1:2], dense[:, 3:4],
    ]
    width = small_ref.shape[1]
    small_ref[...] = jnp.concatenate(
        [sums_a_ref[0:2], sums_b_ref[0:4], spread(parts, width), jnp.zeros((1, width), F32)], axis=0
    )


def run_attn_step(whole, qkv, out, sums_a, sums_b, squares):
    q, o = jax.ShapeDtypeStruct(qkv[0].shape, F32), jax.ShapeDtypeStruct(out[0].shape, F32)
    return pl.pallas_call(
        attn_step_kernel,
        out_shape=(q,) * 4 + (o,) * 4 + (jax.ShapeDtypeStruct(sums_a.shape, F32),),
        compiler_params=params(BIG),
    )(whole, *qkv, *out, sums_a, sums_b, squares)


def final_kernel(*refs):
    small_ref, vec_ref, vf_ref, vs_ref = refs[:4]
    masters, updates, new = refs[4:8], refs[8:12], refs[12:16]
    vg_out, vf_out, vs_out, v_out, norms_ref = refs[16:]
    norms = jnp.sqrt(small_ref[6:7])
    lane = lax.broadcasted_iota(jnp.int32, norms_ref.shape, 1)
    row = lax.broadcasted_iota(jnp.int32, norms_ref.shape, 0)
    table = jnp.zeros(norms_ref.shape, F32)
    for index in range(4):
        weight, update = norms[:, index : index + 1], norms[:, 4 + index : 5 + index]
        trust = weight / (update + ADAM_EPS)
        new[index][...] = masters[index][...] - LEARN_RATE * trust * updates[index][...]
        for at, value in enumerate((weight, update, trust)):
            table = jnp.where((lane == index) & (row == at), value, table)
    norms_ref[...] = table
    grad = small_ref[0:6]
    first_new = MOMENT_DECAY * vf_ref[...] + (1.0 - MOMENT_DECAY) * grad
    second_new = MOMENT_DECAY * vs_ref[...] + (1.0 - MOMENT_DECAY) * grad * grad
    vg_out[...] = grad
    vf_out[...] = first_new
    vs_out[...] = second_new
    v_out[...] = vec_ref[...] - LEARN_RATE * (first_new * (1.0 / CORRECTION)) / (
        jnp.sqrt(second_new * (1.0 / CORRECTION)) + ADAM_EPS
    )


def run_final(small, vectors, vec_first, vec_second, masters, updates):
    shape = lambda value: jax.ShapeDtypeStruct(value.shape, F32)
    flat = lambda value: value.reshape(-1, value.shape[-1])
    outs = pl.pallas_call(
        final_kernel,
        out_shape=tuple(shape(flat(m)) for m in masters)
        + (shape(vectors),) * 4
        + (jax.ShapeDtypeStruct((3, 4), F32),),
        compiler_params=params(BIG),
    )(small, vectors, vec_first, vec_second, *(flat(m) for m in masters), *(flat(u) for u in updates))
    new = [value.reshape(m.shape) for value, m in zip(outs[:4], masters)]
    return new, outs[4:]


def after(value, *others):
    return lax.optimization_barrier((value,) + others)[0]


def shards(
    rows,
    cotangent,
    group_ids,
    qkv_weight,
    out_weight,
    in_weight,
    down_weight,
    vectors,
    qkv_master,
    qkv_first,
    qkv_second,
    out_master,
    out_first,
    out_second,
    in_master,
    in_first,
    in_second,
    down_master,
    down_first,
    down_second,
    vec_first,
    vec_second,
):
    count = lax.axis_size("dp")
    width = rows.shape[1]
    half = width // 2
    nbits = count.bit_length() - 1
    me = lax.axis_index("dp").astype(jnp.int32)
    rel = jnp.arange(count, dtype=jnp.int32) ^ me
    order1 = tuple(range(nbits))
    order2 = (1, 0) + order1[2:]
    pos, pos2 = (
        sum(((rel >> bit) & 1) << (nbits - 1 - place) for place, bit in enumerate(order))
        for order in (order1, order2)
    )
    low = (me & 1).reshape(1)

    onehot = (group_ids[:, None] == jnp.arange(GROUPS, dtype=jnp.int32)[None, :]).astype(F32)
    counts = jnp.sum(onehot, axis=0)

    attn_w = jnp.concatenate(
        [jnp.swapaxes(qkv_weight, 1, 2).reshape(-1, width), out_weight], axis=0
    )
    pieces = [
        lax.dynamic_slice_in_dim(weight, low[0] * half, half, axis)
        for weight, axis in ((attn_w, 0), (in_weight, 0), (down_weight, 1))
    ]
    counts, pieces[0] = lax.optimization_barrier((counts, pieces[0]))
    attn_far = swap(pieces[0], "mp", 2)
    counts = counts + swap(counts, "mp", 2)
    counts, *pieces = lax.optimization_barrier((counts, *pieces[1:]))
    in_far, down_far = (swap(piece, "mp", 2) for piece in pieces)
    near = [swap(weight, "mp", 1) for weight in (attn_w, in_weight, down_weight)]
    counts, attn_one, in_one, down_one = lax.optimization_barrier((counts, *near))
    counts = counts + swap(counts, "dp", 1)
    x, xt = run_start(pos, rows, vectors, count)
    xt = turned_order(xt, pos, count)
    acc, s1, p1, s0, p0 = run_attn_one(x, rows, vectors, attn_one, attn_w)
    attn_far, counts, acc = lax.optimization_barrier((attn_far, counts, acc))
    attn_two = (attn_far, swap(attn_far, "dp", 1))
    counts = counts + swap(counts, "mp", 1)
    for bit in order1[1:]:
        counts = counts + swap(counts, "dp", 1 << bit)
    image_weight = jnp.sqrt(jnp.sum(counts) / (GROUPS * jnp.sum(onehot * counts, axis=1)))
    gout, goutt = run_gout(pos2, image_weight, cotangent, count)
    goutt = turned_order(goutt, pos2, count)
    attn_other, in_far, gout, acc = lax.optimization_barrier((attn_two[1], in_far, gout, acc))
    in_two = (in_far, swap(in_far, "dp", 1))
    attn_two = (attn_far, attn_other)
    attn_three = tuple(swap(piece, "mp", 1) for piece in attn_two)
    first, mid, midt, s3, p3, s2, p2 = run_attn_two(
        pos, low, x, acc, vectors, attn_three, attn_two, count
    )
    midt = turned_order(midt, pos, count)
    y, dm, gi1, gd1 = run_ffn_near(mid, midt, gout, goutt, in_one, down_one)
    gi1, gd1, y, down_far, _ = lax.optimization_barrier((gi1, gd1, y, down_far, in_two[1]))
    down_two = (down_far, swap(down_far, "dp", 1))
    y, dm, gi0, gd0 = run_ffn_near(mid, midt, gout, goutt, in_weight, down_weight, y, dm)
    in_near, down_near = meet(gi0, gi1), meet(gd0, gd1)
    y, down_other, in_sent, down_sent = lax.optimization_barrier(
        (y, down_two[1], upper(in_near), upper(down_near))
    )
    in_near, down_near = fold(in_near, order1[0], in_sent), fold(down_near, order2[0], down_sent)
    down_two = (down_far, down_other)
    in_three, down_three = (
        tuple(swap(piece, "mp", 1) for piece in pieces) for pieces in (in_two, down_two)
    )
    y, dm, gi3, gd3 = run_ffn_far(low, mid, midt, gout, goutt, in_three, down_three, y, dm)
    out_rows, gfirst, gfl, gft, sums_b, gi2, gd2 = run_ffn_last(
        pos, low, image_weight, mid, midt, gout, goutt, in_two, down_two,
        y, dm, first, cotangent, vectors, count,
    )
    gft = turned_order(gft, pos, count)
    in_far, down_far = meet(gi2, gi3), meet(gd2, gd3)
    gfl, in_sent, down_sent, _, _ = lax.optimization_barrier(
        (gfl, upper(in_far), upper(down_far), in_near[-1], down_near[-1])
    )
    in_far, down_far = fold(in_far, order1[0], in_sent), fold(down_far, order2[0], down_sent)
    gin, ga3 = run_back_far(low, gfl, xt, gft, attn_three, (s3, p3))
    gin, ga2 = run_back_far(low, gfl, xt, gft, attn_two, (s2, p2), gin)
    far = meet(ga2, ga3)
    gin, far_sent, in_sent, down_sent = lax.optimization_barrier(
        (gin, upper(far), total(in_far).astype(BF16), total(down_far).astype(BF16))
    )
    far = fold(far, order1[0], far_sent)
    in_grad, down_grad = join(in_near, None, in_sent), join(down_near, None, down_sent)
    gin, ga1 = run_back_near(gfl, xt, gft, attn_one, (s1, p1), gin)
    input_grad, sums_a, ga0 = run_back_last(
        gfl, xt, gft, attn_w, (s0, p0), gin, rows, gfirst, vectors
    )
    near = meet(ga0, ga1)
    near = fold(near, order1[0])
    far = fold(far, order1[1])
    in_grad = fold(in_grad, order1[1])
    near = fold(near, order1[1])
    down_grad = fold(down_grad, order2[1])
    near = near + (swap(total(far).astype(BF16), "mp", 2),)
    for bit in order1[2:]:
        in_grad, down_grad = fold(in_grad, bit), fold(down_grad, bit)
        near = fold(near, bit)
    both = total(near)
    in_grad, down_grad = total(in_grad), total(down_grad)

    down_state = (down_master.T, down_first.T, down_second.T)
    in_fn, in_sn, in_up, down_fn, down_sn, down_up, squares = run_dense_step(
        (in_grad, in_master, in_first, in_second), (down_grad,) + down_state
    )
    qkv_grad, qkv_fn, qkv_sn, qkv_up, out_grad, out_fn, out_sn, out_up, small = run_attn_step(
        both, (qkv_master, qkv_first, qkv_second), (out_master, out_first, out_second),
        sums_a, sums_b, squares,
    )
    new, vec_outs = run_final(
        all_sum(small), vectors, vec_first, vec_second,
        (qkv_master, out_master, in_master, down_state[0]), (qkv_up, out_up, in_up, down_up),
    )
    return (
        out_rows,
        input_grad,
        qkv_grad,
        out_grad,
        in_grad,
        down_grad.T,
        qkv_fn,
        qkv_sn,
        new[0],
        out_fn,
        out_sn,
        new[1],
        in_fn,
        in_sn,
        new[2],
        down_fn.T,
        down_sn.T,
        new[3].T,
    ) + tuple(vec_outs)


def solution(mesh):
    rows = P(("dp", "mp"), None)
    qkv_state = P(None, "dp", "mp")
    out_state = P("mp", "dp")
    in_state = P("dp", "mp")
    in_specs = (
        (rows, rows, P(("dp", "mp")), P(None, None, "mp"), P("mp", None), P(None, "mp"), P("mp", None), P())
        + (qkv_state,) * 3
        + (out_state,) * 3
        + (in_state,) * 3
        + (out_state,) * 3
        + (P(), P())
    )
    out_specs = (
        (rows, rows, qkv_state, out_state, in_state, out_state)
        + (qkv_state,) * 3
        + (out_state,) * 3
        + (in_state,) * 3
        + (out_state,) * 3
        + (P(),) * 5
    )
    return jax.shard_map(shards, mesh=mesh, in_specs=in_specs, out_specs=out_specs, check_vma=False)
```

```python
import math

import jax
import jax.numpy as jnp
from jax import lax
from jax.experimental import pallas as pl
from jax.experimental.pallas import tpu as pltpu
from jax.sharding import PartitionSpec as P

HEAD_DIM = 64
PATCHES = 256
GROUPS = 8
STEP = 5

NORM_EPS = 1e-06
ADAM_EPS = 1e-06
MOMENT_DECAY = 0.5
LEARN_RATE = 0.5
WEIGHT_DECAY = 0.01
SCALE = HEAD_DIM ** (-0.5)

F32 = jnp.float32
BF16 = jnp.bfloat16
MB = 1024 * 1024
BIG = 16


def mm(left, right):
    return jnp.dot(left, right, preferred_element_type=F32)


def mm_nt(left, right):
    return lax.dot_general(left, right, (((1,), (1,)), ((), ())), preferred_element_type=F32)


def mm_tn(left, right):
    return lax.dot_general(left, right, (((0,), (0,)), ((), ())), preferred_element_type=F32)


def layer_stats(values):
    center = values - jnp.mean(values, axis=-1, keepdims=True)
    inverse = lax.rsqrt(jnp.mean(center * center, axis=-1, keepdims=True) + NORM_EPS)
    return center * inverse, inverse


def norm_back(grad_normed, normed, inverse):
    return inverse * (
        grad_normed
        - jnp.mean(grad_normed, axis=-1, keepdims=True)
        - normed * jnp.mean(grad_normed * normed, axis=-1, keepdims=True)
    )


def gelu_pair(t):
    size = jnp.abs(t) * (2.0**-0.5)
    k = 1.0 / (1.0 + 0.3275911 * size)
    bell = jnp.exp(-size * size)
    poly = k * (
        0.254829592
        + k * (-0.284496736 + k * (1.421413741 + k * (-1.453152027 + k * 1.061405429)))
    )
    tail = 0.5 * poly * bell
    cdf = jnp.where(t < 0, tail, 1.0 - tail)
    return t * cdf, cdf + t * bell * (1.0 / math.sqrt(2.0 * math.pi))


def put_turned(out_ref, value, pos_ref, count, start):
    turned = value.T
    part = turned.shape[0] // count
    width = turned.shape[1]
    here = pl.ds(start, width)
    if len(out_ref.shape) == 2:
        out_ref[:, here] = turned
        return
    for j in range(count):
        out_ref[pos_ref[j], :, here] = turned[j * part : (j + 1) * part]


def turned_shape(width, rows, count):
    part = width // count
    if part % 16 == 0:
        return (count, part, rows)
    return (width, rows)


def turned_order(turned, pos, count):
    width = turned.shape[0] if turned.ndim == 2 else turned.shape[0] * turned.shape[1]
    rows = turned.shape[-1]
    if turned.ndim == 2:
        shaped = turned.reshape(count, width // count, rows)
        turned = jnp.zeros_like(shaped).at[pos].set(shaped)
    return turned.reshape(width, rows)


def params(limit, **more):
    return pltpu.CompilerParams(vmem_limit_bytes=limit * MB, **more)


def full(shape):
    return pl.BlockSpec(shape, lambda *_: (0,) * len(shape), pipeline_mode=pl.Buffered(1))


SMEM = pl.BlockSpec(memory_space=pltpu.SMEM)


def start_kernel(pos_ref, rows_ref, vec_ref, x_ref, xt_ref, *, count):
    width, rows = rows_ref.shape[1], rows_ref.shape[0]
    for start in range(0, rows, PATCHES):
        normed, _ = layer_stats(rows_ref[start : start + PATCHES].astype(F32))
        low = (normed * vec_ref[0:1] + vec_ref[1:2]).astype(BF16)
        x_ref[start : start + PATCHES] = low
        put_turned(xt_ref, low, pos_ref, count, start)


def run_start(pos, rows, vectors, count):
    r, d = rows.shape
    return pl.pallas_call(
        lambda *refs: start_kernel(*refs, count=count),
        out_shape=(
            jax.ShapeDtypeStruct((r, d), BF16),
            jax.ShapeDtypeStruct(turned_shape(d, r, count), BF16),
        ),
        in_specs=[SMEM, pl.BlockSpec(memory_space=pltpu.VMEM), pl.BlockSpec(memory_space=pltpu.VMEM)],
        compiler_params=params(6),
    )(pos, rows, vectors)


def gout_kernel(pos_ref, weight_ref, cot_ref, g_ref, gt_ref, *, count):
    rows = cot_ref.shape[0]
    for index in range(rows // PATCHES):
        start = index * PATCHES
        low = (cot_ref[start : start + PATCHES].astype(F32) * weight_ref[index]).astype(BF16)
        g_ref[start : start + PATCHES] = low
        put_turned(gt_ref, low, pos_ref, count, start)


def run_gout(pos, weight, cot, count):
    r, d = cot.shape
    return pl.pallas_call(
        lambda *refs: gout_kernel(*refs, count=count),
        out_shape=(
            jax.ShapeDtypeStruct((r, d), BF16),
            jax.ShapeDtypeStruct(turned_shape(d, r, count), BF16),
        ),
        in_specs=[SMEM, SMEM, pl.BlockSpec(memory_space=pltpu.VMEM)],
        compiler_params=params(4),
    )(pos, weight, cot)


def attend_shard(x, w_ref, saved_ref, probs_ref):
    cols = w_ref.shape[0] // 4
    qkv = mm_nt(x, w_ref[: 3 * cols]).astype(BF16)
    saved_ref[:, : 3 * cols] = qkv
    mixed = []
    for h in range(cols // HEAD_DIM):
        at = h * HEAD_DIM
        q = qkv[:, at : at + HEAD_DIM] * SCALE
        k = qkv[:, cols + at : cols + at + HEAD_DIM]
        v = qkv[:, 2 * cols + at : 2 * cols + at + HEAD_DIM]
        scores = mm_nt(k, q)
        expo = jnp.exp(scores - jnp.max(scores, axis=0, keepdims=True))
        probs = (expo * (1.0 / jnp.sum(expo, axis=0, keepdims=True))).astype(BF16)
        probs_ref[h] = probs
        mixed.append(mm_tn(probs, v).astype(BF16))
    mixed = jnp.concatenate(mixed, axis=1)
    saved_ref[:, 3 * cols :] = mixed
    return mm(mixed, w_ref[3 * cols :])


def attn_one_kernel(x_ref, rows_ref, vec_ref, wa_ref, wb_ref, acc_ref, sa_ref, pa_ref, sb_ref, pb_ref):
    x = x_ref[...]
    term = attend_shard(x, wa_ref, sa_ref, pa_ref)
    term += attend_shard(x, wb_ref, sb_ref, pb_ref)
    acc_ref[...] = rows_ref[...].astype(F32) + term + vec_ref[4:5]


def join_halves(low_ref, own_ref, other_ref, whole_ref):
    half = own_ref.shape[0]

    @pl.when(low_ref[0] == 0)
    def _():
        whole_ref[:half] = own_ref[...]
        whole_ref[half:] = other_ref[...]

    @pl.when(low_ref[0] != 0)
    def _():
        whole_ref[:half] = other_ref[...]
        whole_ref[half:] = own_ref[...]


def join_pair(low_ref, halves, wholes):
    @pl.when(pl.program_id(0) == 0)
    def _():
        for (own, other), whole in zip(halves, wholes):
            join_halves(low_ref, own, other, whole)


def attn_two_kernel(
    pos_ref, low_ref, x_ref, acc_ref, vec_ref, ha_ref, ia_ref, hb_ref, ib_ref,
    first_ref, mid_ref, midt_ref, sa_ref, pa_ref, sb_ref, pb_ref, wa_ref, wb_ref, *, count,
):
    join_pair(low_ref, ((ha_ref, ia_ref), (hb_ref, ib_ref)), (wa_ref, wb_ref))
    x = x_ref[...]
    term = attend_shard(x, wa_ref, sa_ref, pa_ref)
    term += attend_shard(x, wb_ref, sb_ref, pb_ref)
    first = acc_ref[...] + term
    first_ref[...] = first
    normed, _ = layer_stats(first)
    low = (normed * vec_ref[2:3] + vec_ref[3:4]).astype(BF16)
    mid_ref[...] = low
    put_turned(midt_ref, low, pos_ref, count, 0)


def image_block(d):
    return pl.BlockSpec((PATCHES, d), lambda i: (i, 0))


def saved_outputs(r, d, heads):
    images = r // PATCHES
    shapes = (
        jax.ShapeDtypeStruct((r, d), BF16),
        jax.ShapeDtypeStruct((images * heads, PATCHES, PATCHES), BF16),
    )
    specs = [image_block(d), pl.BlockSpec((heads, PATCHES, PATCHES), lambda i: (i, 0, 0))]
    return shapes, specs


def cost(micros):
    return pl.CostEstimate(flops=int(micros * 3 * 1e9), bytes_accessed=int(micros * 3 * 3e6), transcendentals=0)


def run_attn_one(x, rows, vectors, wa, wb):
    r, d = x.shape
    heads = d // 4 // HEAD_DIM
    shapes, specs = saved_outputs(r, d, heads)
    return pl.pallas_call(
        attn_one_kernel,
        grid=(r // PATCHES,),
        out_shape=(jax.ShapeDtypeStruct((r, d), F32),) + shapes * 2,
        in_specs=[image_block(d), image_block(d), full(vectors.shape), full((d, d)), full((d, d))],
        out_specs=[image_block(d)] + specs * 2,
        compiler_params=params(9),
        cost_estimate=cost(7),
    )(x, rows, vectors, wa, wb)


def run_attn_two(pos, low, x, acc, vectors, wa, wb, count):
    r, d = x.shape
    heads = d // 4 // HEAD_DIM
    shapes, specs = saved_outputs(r, d, heads)
    tshape = turned_shape(d, r, count)
    tspec = pl.BlockSpec(
        tshape[:-1] + (PATCHES,), lambda i: (0,) * (len(tshape) - 1) + (i,)
    )
    return pl.pallas_call(
        lambda *refs: attn_two_kernel(*refs, count=count),
        grid=(r // PATCHES,),
        out_shape=(
            jax.ShapeDtypeStruct((r, d), F32),
            jax.ShapeDtypeStruct((r, d), BF16),
            jax.ShapeDtypeStruct(tshape, BF16),
        )
        + shapes * 2,
        in_specs=[SMEM, SMEM, image_block(d), image_block(d), full(vectors.shape)]
        + [full((d // 2, d))] * 4,
        out_specs=[image_block(d), image_block(d), tspec] + specs * 2,
        scratch_shapes=[pltpu.VMEM((d, d), BF16)] * 2,
        compiler_params=params(9),
        cost_estimate=cost(7),
    )(pos, low, x, acc, vectors, *wa, *wb)


TILES = 3


def ffn_tile(mid_ref, midt_ref, g_ref, gt_ref, w_in, w_down, gi_ref, gd_ref, y_ref, dm_ref):
    pre = mm(mid_ref[...], w_in)
    dact = mm_nt(g_ref[...], w_down)
    activ, slope = gelu_pair(pre)
    activ = activ.astype(BF16)
    dpre = (dact * slope).astype(BF16)
    y_ref[...] += mm(activ, w_down)
    dm_ref[...] += mm_nt(dpre, w_in)
    gd_ref[...] = mm(gt_ref[...], activ).astype(BF16)
    gi_ref[...] = mm(midt_ref[...], dpre).astype(BF16)


def joined(low_ref, own_ref, other_ref, axis):
    own, other = own_ref[...], other_ref[...]
    return jnp.where(
        low_ref[0] == 0,
        jnp.concatenate([own, other], axis=axis),
        jnp.concatenate([other, own], axis=axis),
    )


def ffn_near_kernel(mid_ref, midt_ref, g_ref, gt_ref, in_ref, down_ref, *rest):
    *before, y_ref, dm_ref, gi_ref, gd_ref = rest

    @pl.when(pl.program_id(0) == 0)
    def _():
        y_ref[...] = before[0][...] if before else jnp.zeros_like(y_ref)
        dm_ref[...] = before[1][...] if before else jnp.zeros_like(dm_ref)

    ffn_tile(mid_ref, midt_ref, g_ref, gt_ref, in_ref[...], down_ref[...], gi_ref, gd_ref, y_ref, dm_ref)


def ffn_far_kernel(
    low_ref, mid_ref, midt_ref, g_ref, gt_ref, ia_ref, ib_ref, da_ref, db_ref, y_in_ref, dm_in_ref,
    y_ref, dm_ref, gi_ref, gd_ref,
):
    @pl.when(pl.program_id(0) == 0)
    def _():
        y_ref[...] = y_in_ref[...]
        dm_ref[...] = dm_in_ref[...]

    w_in, w_down = joined(low_ref, ia_ref, ib_ref, 0), joined(low_ref, da_ref, db_ref, 1)
    ffn_tile(mid_ref, midt_ref, g_ref, gt_ref, w_in, w_down, gi_ref, gd_ref, y_ref, dm_ref)


def ffn_last_kernel(
    pos_ref, low_ref, weight_ref, mid_ref, midt_ref, g_ref, gt_ref, ia_ref, ib_ref, da_ref, db_ref,
    y_in_ref, dm_in_ref, first_ref, cot_ref, vec_ref,
    out_ref, gf_ref, gfl_ref, gft_ref, sums_ref, gi_ref, gd_ref, y_ref, dm_ref, *, count,
):
    ffn_far_kernel(
        low_ref, mid_ref, midt_ref, g_ref, gt_ref, ia_ref, ib_ref, da_ref, db_ref, y_in_ref, dm_in_ref,
        y_ref, dm_ref, gi_ref, gd_ref,
    )

    @pl.when(pl.program_id(0) == pl.num_programs(0) - 1)
    def _():
        chunk = 256

        def body(index, sums):
            start = pl.multiple_of(index * chunk, chunk)
            here = pl.ds(start, chunk)
            first = first_ref[here, :]
            normed, inverse = layer_stats(first)
            out_ref[here, :] = (first + y_ref[here, :] + vec_ref[5:6]).astype(BF16)
            dmid = dm_ref[here, :]
            gout = cot_ref[here, :].astype(F32) * weight_ref[start // PATCHES]
            gfirst = gout + norm_back(dmid * vec_ref[2:3], normed, inverse)
            gf_ref[here, :] = gfirst
            low = gfirst.astype(BF16)
            gfl_ref[here, :] = low
            put_turned(gft_ref, low, pos_ref, count, start)
            terms = (dmid * normed, dmid, gfirst, gout)
            return tuple(a + jnp.sum(b, axis=0, keepdims=True) for a, b in zip(sums, terms))

        zero = jnp.zeros((1, first_ref.shape[1]), F32)
        sums = lax.fori_loop(0, first_ref.shape[0] // chunk, body, (zero,) * 4)
        sums_ref[...] = jnp.concatenate(sums + sums, axis=0)


def ffn_specs(d, parts):
    tile = d // TILES
    cols = lambda rows: pl.BlockSpec((rows, tile), lambda i: (0, i))
    w_down = pl.BlockSpec((tile, d // parts), lambda i: (i, 0))
    return [cols(d // parts)] * parts + [w_down] * parts, [cols(d)] * 2


def run_ffn_near(mid, midt, g, gt, w_in, w_down, *before):
    r, d = mid.shape
    w_specs, g_specs = ffn_specs(d, 1)
    grad = jax.ShapeDtypeStruct((d, d), BF16)
    return pl.pallas_call(
        ffn_near_kernel,
        grid=(TILES,),
        out_shape=(jax.ShapeDtypeStruct((r, d), F32),) * 2 + (grad,) * 2,
        in_specs=[full((r, d)), full((d, r)), full((r, d)), full((d, r))] + w_specs + [full((r, d))] * len(before),
        out_specs=[full((r, d))] * 2 + g_specs,
        compiler_params=params(10),
        cost_estimate=cost(6),
    )(mid, midt, g, gt, w_in, w_down, *before)


def run_ffn_far(low, mid, midt, g, gt, w_in, w_down, y, dm):
    r, d = mid.shape
    w_specs, g_specs = ffn_specs(d, 2)
    grad = jax.ShapeDtypeStruct((d, d), BF16)
    return pl.pallas_call(
        ffn_far_kernel,
        grid=(TILES,),
        out_shape=(jax.ShapeDtypeStruct((r, d), F32),) * 2 + (grad,) * 2,
        in_specs=[SMEM, full((r, d)), full((d, r)), full((r, d)), full((d, r))] + w_specs + [full((r, d))] * 2,
        out_specs=[full((r, d))] * 2 + g_specs,
        compiler_params=params(12),
        cost_estimate=cost(6),
    )(low, mid, midt, g, gt, *w_in, *w_down, y, dm)


def run_ffn_last(pos, low, weight, mid, midt, g, gt, w_in, w_down, y, dm, first, cot, vectors, count):
    r, d = mid.shape
    w_specs, g_specs = ffn_specs(d, 2)
    grad = jax.ShapeDtypeStruct((d, d), BF16)
    tshape = turned_shape(d, r, count)
    return pl.pallas_call(
        lambda *refs: ffn_last_kernel(*refs, count=count),
        grid=(TILES,),
        out_shape=(
            jax.ShapeDtypeStruct((r, d), BF16),
            jax.ShapeDtypeStruct((r, d), F32),
            jax.ShapeDtypeStruct((r, d), BF16),
            jax.ShapeDtypeStruct(tshape, BF16),
            jax.ShapeDtypeStruct((8, d), F32),
        )
        + (grad,) * 2,
        in_specs=[SMEM, SMEM, SMEM, full((r, d)), full((d, r)), full((r, d)), full((d, r))]
        + w_specs
        + [full((r, d))] * 4
        + [full(vectors.shape)],
        out_specs=[full((r, d)), full((r, d)), full((r, d)), full(tshape), full((8, d))] + g_specs,
        scratch_shapes=[pltpu.VMEM((r, d), F32)] * 2,
        compiler_params=params(14),
        cost_estimate=cost(8),
    )(pos, low, weight, mid, midt, g, gt, *w_in, *w_down, y, dm, first, cot, vectors)


def attend_back_shard(gf, w_ref, saved_ref, probs_ref, keep_ref):
    cols = w_ref.shape[0] // 4
    start = pl.multiple_of(pl.program_id(0) * PATCHES, PATCHES)
    dmix = mm_nt(gf, w_ref[3 * cols :]).astype(BF16)
    dq, dk, dv = [], [], []
    for h in range(cols // HEAD_DIM):
        at = h * HEAD_DIM
        q = saved_ref[:, at : at + HEAD_DIM]
        k = saved_ref[:, cols + at : cols + at + HEAD_DIM]
        v = saved_ref[:, 2 * cols + at : 2 * cols + at + HEAD_DIM]
        do = dmix[:, at : at + HEAD_DIM]
        probs = probs_ref[h]
        dv.append(mm(probs, do).astype(BF16))
        dp = mm_nt(v, do)
        wide = probs.astype(F32)
        ds = (wide * (dp - jnp.sum(wide * dp, axis=0, keepdims=True))).astype(BF16)
        dq.append((SCALE * mm_tn(ds, k)).astype(BF16))
        dk.append((SCALE * mm(ds, q)).astype(BF16))
    dqkv = jnp.concatenate(dq + dk + dv, axis=1)
    keep_ref[pl.ds(start, PATCHES), : 3 * cols] = dqkv
    keep_ref[pl.ds(start, PATCHES), 3 * cols :] = saved_ref[:, 3 * cols :]
    return mm(dqkv, w_ref[: 3 * cols])


def attn_grad(xt_ref, gft_ref, keep_ref, g_ref):
    cols = keep_ref.shape[1] // 4
    g_ref[:, : 3 * cols] = mm(xt_ref[...], keep_ref[:, : 3 * cols]).astype(BF16)
    g_ref[:, 3 * cols :] = mm(gft_ref[...], keep_ref[:, 3 * cols :]).astype(BF16)


def back_body(gf_ref, xt_ref, gft_ref, w_ref, saved_ref, probs_ref, g_ref, keep_ref):
    term = attend_back_shard(gf_ref[...], w_ref, saved_ref, probs_ref, keep_ref)

    @pl.when(pl.program_id(0) == pl.num_programs(0) - 1)
    def _():
        attn_grad(xt_ref, gft_ref, keep_ref, g_ref)

    return term


def back_far_kernel(
    low_ref, gf_ref, xt_ref, gft_ref, saved_ref, probs_ref, h_ref, i_ref, *rest
):
    *before, acc_ref, g_ref, keep_ref, w_ref = rest
    join_pair(low_ref, ((h_ref, i_ref),), (w_ref,))
    term = back_body(gf_ref, xt_ref, gft_ref, w_ref, saved_ref, probs_ref, g_ref, keep_ref)
    if before:
        acc_ref[...] = term + before[0][...]
    else:
        acc_ref[...] = jnp.zeros_like(acc_ref)
        acc_ref[...] += term


def back_near_kernel(
    gf_ref, xt_ref, gft_ref, saved_ref, probs_ref, w_ref, before_ref, acc_ref, g_ref, keep_ref
):
    term = back_body(gf_ref, xt_ref, gft_ref, w_ref, saved_ref, probs_ref, g_ref, keep_ref)
    acc_ref[...] = term + before_ref[...]


def back_last_kernel(
    gf_ref, xt_ref, gft_ref, saved_ref, probs_ref, w_ref, before_ref, rows_ref, gfirst_ref, vec_ref,
    ig_ref, sums_ref, g_ref, keep_ref,
):
    term = back_body(gf_ref, xt_ref, gft_ref, w_ref, saved_ref, probs_ref, g_ref, keep_ref)
    grad_in = before_ref[...] + term
    normed, inverse = layer_stats(rows_ref[...].astype(F32))
    ig_ref[...] = gfirst_ref[...] + norm_back(grad_in * vec_ref[0:1], normed, inverse)
    one = jnp.sum(grad_in * normed, axis=0, keepdims=True)
    two = jnp.sum(grad_in, axis=0, keepdims=True)
    sums = jnp.concatenate([one, two] * 4, axis=0)

    @pl.when(pl.program_id(0) == 0)
    def _():
        sums_ref[...] = sums

    @pl.when(pl.program_id(0) > 0)
    def _():
        sums_ref[...] += sums


def back_call(kernel, ops, specs, outs, out_specs, far):
    gfl = ops[1] if far else ops[0]
    r, d = gfl.shape
    heads = d // 4 // HEAD_DIM
    _, saved_specs = saved_outputs(r, d, heads)
    keep, whole = pltpu.VMEM((r, d), BF16), pltpu.VMEM((d, d), BF16)
    return pl.pallas_call(
        kernel,
        grid=(r // PATCHES,),
        out_shape=tuple(outs) + (jax.ShapeDtypeStruct((d, d), BF16),),
        in_specs=([SMEM] if far else []) + [image_block(d)] + [full((d, r))] * 2 + saved_specs + specs,
        out_specs=out_specs + [full((d, d))],
        scratch_shapes=[keep, whole] if far else [keep],
        compiler_params=params(9),
        cost_estimate=cost(6),
    )(*ops)


def run_back_far(low, gfl, xt, gft, halves, saved, *acc):
    r, d = gfl.shape
    return back_call(
        back_far_kernel,
        [low, gfl, xt, gft, *saved, *halves, *acc],
        [full((d // 2, d))] * 2 + [image_block(d)] * len(acc),
        [jax.ShapeDtypeStruct((r, d), F32)], [image_block(d)], True,
    )


def run_back_near(gfl, xt, gft, weight, saved, acc):
    r, d = gfl.shape
    return back_call(
        back_near_kernel,
        [gfl, xt, gft, *saved, weight, acc],
        [full((d, d)), image_block(d)],
        [jax.ShapeDtypeStruct((r, d), F32)], [image_block(d)], False,
    )


def run_back_last(gfl, xt, gft, weight, saved, acc, rows, gfirst, vectors):
    r, d = gfl.shape
    return back_call(
        back_last_kernel,
        [gfl, xt, gft, *saved, weight, acc, rows, gfirst, vectors],
        [full((d, d))] + [image_block(d)] * 3 + [full(vectors.shape)],
        [jax.ShapeDtypeStruct((r, d), F32), jax.ShapeDtypeStruct((8, d), F32)],
        [image_block(d), full((8, d))], False,
    )


def swap(value, axis, bit):
    size = lax.axis_size(axis)
    return lax.ppermute(value, axis, [(i, i ^ bit) for i in range(size)])


def all_sum(value):
    for axis in ("mp", "dp"):
        bit = 1
        while bit < lax.axis_size(axis):
            value = value + swap(value, axis, bit)
            bit *= 2
    return value


def total(terms, rows=slice(None)):
    return sum(term[rows].astype(F32) for term in terms)


def columns(terms, cut):
    return tuple(term[:, cut] for term in terms)


def meet(own, partner):
    return own, swap(partner, "mp", 1)


def upper(terms):
    return total(terms, slice(terms[0].shape[0] // 2, None)).astype(BF16)


def fold(terms, bit, sent=None):
    half = terms[0].shape[0] // 2
    back = swap(upper(terms) if sent is None else sent, "dp", 1 << bit)
    return tuple(term[:half] for term in terms) + (back,)


def stacked(move, *sums):
    moved = move(jnp.concatenate(sums, axis=0))
    edges = [0]
    for value in sums:
        edges.append(edges[-1] + value.shape[0])
    return [moved[low:high] for low, high in zip(edges, edges[1:])]


def join(near, far, sent=None):
    return near + (swap(total(far).astype(BF16) if sent is None else sent, "mp", 2),)


def join_two(near_a, far_a, near_b, far_b):
    a, b = stacked(
        lambda value: swap(value, "mp", 2), total(far_a).astype(BF16), total(far_b).astype(BF16)
    )
    return near_a + (a,), near_b + (b,)


def fold_two(terms_a, terms_b, bit):
    half_a, half_b = terms_a[0].shape[0] // 2, terms_b[0].shape[0] // 2
    a, b = stacked(lambda value: swap(value, "dp", 1 << bit), upper(terms_a), upper(terms_b))
    return tuple(term[:half_a] for term in terms_a) + (a,), tuple(term[:half_b] for term in terms_b) + (b,)


CORRECTION = 1.0 - MOMENT_DECAY**STEP


def lamb_step(grad, master, first, second):
    first_new = MOMENT_DECAY * first + (1.0 - MOMENT_DECAY) * grad
    second_new = MOMENT_DECAY * second + (1.0 - MOMENT_DECAY) * grad * grad
    update = (
        first_new * (1.0 / CORRECTION) / (jnp.sqrt(second_new * (1.0 / CORRECTION)) + ADAM_EPS)
        + WEIGHT_DECAY * master
    )
    return first_new, second_new, update


def whole_sum(value):
    return jnp.sum(jnp.sum(value, axis=0, keepdims=True), axis=1, keepdims=True)


def spread(parts, width):
    lane = lax.broadcasted_iota(jnp.int32, (1, width), 1)
    return sum(jnp.where(lane == index, part, 0.0) for index, part in enumerate(parts))


def dense_step_kernel(*refs):
    ins, outs = refs[:8], refs[8:]
    parts = []
    for at in range(2):
        grad, master, first, second = (ref[...] for ref in ins[4 * at : 4 * at + 4])
        first_new, second_new, update = lamb_step(grad, master, first, second)
        for ref, value in zip(outs[3 * at : 3 * at + 3], (first_new, second_new, update)):
            ref[...] = value
        parts += [whole_sum(master * master), whole_sum(update * update)]
    outs[6][...] = spread(parts, outs[6].shape[1])


def run_dense_step(in_parts, down_parts):
    shape = jax.ShapeDtypeStruct(in_parts[0].shape, F32)
    width = in_parts[0].shape[1]
    return pl.pallas_call(
        dense_step_kernel,
        out_shape=(shape,) * 6 + (jax.ShapeDtypeStruct((1, width), F32),),
        compiler_params=params(6),
    )(*in_parts, *down_parts)


def attn_step_kernel(
    sum_ref, qm_ref, qf_ref, qs_ref, om_ref, of_ref, os_ref, sums_a_ref, sums_b_ref, squares_ref,
    qg_ref, qf_out, qs_out, qu_ref, og_ref, of_out, os_out, ou_ref, small_ref,
):
    cols = qm_ref.shape[2]
    whole = sum_ref[...]
    master_square, update_square = 0.0, 0.0
    for index, grad in enumerate(whole[:, at * cols : (at + 1) * cols] for at in range(3)):
        master = qm_ref[index]
        first_new, second_new, update = lamb_step(grad, master, qf_ref[index], qs_ref[index])
        qg_ref[index] = grad
        qf_out[index] = first_new
        qs_out[index] = second_new
        qu_ref[index] = update
        master_square += whole_sum(master * master)
        update_square += whole_sum(update * update)
    grad = whole[:, 3 * cols :].T
    master = om_ref[...]
    first_new, second_new, update = lamb_step(grad, master, of_ref[...], os_ref[...])
    og_ref[...] = grad
    of_out[...] = first_new
    os_out[...] = second_new
    ou_ref[...] = update
    dense = squares_ref[...]
    parts = [
        master_square, whole_sum(master * master), dense[:, 0:1], dense[:, 2:3],
        update_square, whole_sum(update * update), dense[:, 1:2], dense[:, 3:4],
    ]
    width = small_ref.shape[1]
    small_ref[...] = jnp.concatenate(
        [sums_a_ref[0:2], sums_b_ref[0:4], spread(parts, width), jnp.zeros((1, width), F32)], axis=0
    )


def run_attn_step(whole, qkv, out, sums_a, sums_b, squares):
    q, o = jax.ShapeDtypeStruct(qkv[0].shape, F32), jax.ShapeDtypeStruct(out[0].shape, F32)
    return pl.pallas_call(
        attn_step_kernel,
        out_shape=(q,) * 4 + (o,) * 4 + (jax.ShapeDtypeStruct(sums_a.shape, F32),),
        compiler_params=params(6),
    )(whole, *qkv, *out, sums_a, sums_b, squares)


def final_kernel(*refs):
    small_ref, vec_ref, vf_ref, vs_ref = refs[:4]
    masters, updates, new = refs[4:8], refs[8:12], refs[12:16]
    vg_out, vf_out, vs_out, v_out, norms_ref = refs[16:]
    norms = jnp.sqrt(small_ref[6:7])
    lane = lax.broadcasted_iota(jnp.int32, norms_ref.shape, 1)
    row = lax.broadcasted_iota(jnp.int32, norms_ref.shape, 0)
    table = jnp.zeros(norms_ref.shape, F32)
    for index in range(4):
        weight, update = norms[:, index : index + 1], norms[:, 4 + index : 5 + index]
        trust = weight / (update + ADAM_EPS)
        new[index][...] = masters[index][...] - LEARN_RATE * trust * updates[index][...]
        for at, value in enumerate((weight, update, trust)):
            table = jnp.where((lane == index) & (row == at), value, table)
    norms_ref[...] = table
    grad = small_ref[0:6]
    first_new = MOMENT_DECAY * vf_ref[...] + (1.0 - MOMENT_DECAY) * grad
    second_new = MOMENT_DECAY * vs_ref[...] + (1.0 - MOMENT_DECAY) * grad * grad
    vg_out[...] = grad
    vf_out[...] = first_new
    vs_out[...] = second_new
    v_out[...] = vec_ref[...] - LEARN_RATE * (first_new * (1.0 / CORRECTION)) / (
        jnp.sqrt(second_new * (1.0 / CORRECTION)) + ADAM_EPS
    )


def run_final(small, vectors, vec_first, vec_second, masters, updates):
    shape = lambda value: jax.ShapeDtypeStruct(value.shape, F32)
    flat = lambda value: value.reshape(-1, value.shape[-1])
    outs = pl.pallas_call(
        final_kernel,
        out_shape=tuple(shape(flat(m)) for m in masters)
        + (shape(vectors),) * 4
        + (jax.ShapeDtypeStruct((3, 4), F32),),
        compiler_params=params(6),
    )(small, vectors, vec_first, vec_second, *(flat(m) for m in masters), *(flat(u) for u in updates))
    new = [value.reshape(m.shape) for value, m in zip(outs[:4], masters)]
    return new, outs[4:]


def after(value, *others):
    return lax.optimization_barrier((value,) + others)[0]


def shards(
    rows,
    cotangent,
    group_ids,
    qkv_weight,
    out_weight,
    in_weight,
    down_weight,
    vectors,
    qkv_master,
    qkv_first,
    qkv_second,
    out_master,
    out_first,
    out_second,
    in_master,
    in_first,
    in_second,
    down_master,
    down_first,
    down_second,
    vec_first,
    vec_second,
):
    count = lax.axis_size("dp")
    width = rows.shape[1]
    half = width // 2
    nbits = count.bit_length() - 1
    me = lax.axis_index("dp").astype(jnp.int32)
    rel = jnp.arange(count, dtype=jnp.int32) ^ me
    order1 = tuple(range(nbits))
    order2 = (1, 0) + order1[2:]
    pos, pos2 = (
        sum(((rel >> bit) & 1) << (nbits - 1 - place) for place, bit in enumerate(order))
        for order in (order1, order2)
    )
    low = (me & 1).reshape(1)

    onehot = (group_ids[:, None] == jnp.arange(GROUPS, dtype=jnp.int32)[None, :]).astype(F32)
    counts = jnp.sum(onehot, axis=0)

    attn_w = jnp.concatenate(
        [jnp.swapaxes(qkv_weight, 1, 2).reshape(-1, width), out_weight], axis=0
    )
    pieces = [
        lax.dynamic_slice_in_dim(weight, low[0] * half, half, axis)
        for weight, axis in ((attn_w, 0), (in_weight, 0), (down_weight, 1))
    ]
    counts, pieces[0] = lax.optimization_barrier((counts, pieces[0]))
    attn_far = swap(pieces[0], "mp", 2)
    counts = counts + swap(counts, "mp", 2)
    counts, *pieces = lax.optimization_barrier((counts, *pieces[1:]))
    in_far, down_far = (swap(piece, "mp", 2) for piece in pieces)
    near = [swap(weight, "mp", 1) for weight in (attn_w, in_weight, down_weight)]
    counts, attn_one, in_one, down_one = lax.optimization_barrier((counts, *near))
    counts = counts + swap(counts, "dp", 1)
    x, xt = run_start(pos, rows, vectors, count)
    xt = turned_order(xt, pos, count)
    acc, s1, p1, s0, p0 = run_attn_one(x, rows, vectors, attn_one, attn_w)
    attn_far, counts, acc = lax.optimization_barrier((attn_far, counts, acc))
    attn_two = (attn_far, swap(attn_far, "dp", 1))
    counts = counts + swap(counts, "mp", 1)
    for bit in order1[1:]:
        counts = counts + swap(counts, "dp", 1 << bit)
    image_weight = jnp.sqrt(jnp.sum(counts) / (GROUPS * jnp.sum(onehot * counts, axis=1)))
    gout, goutt = run_gout(pos2, image_weight, cotangent, count)
    goutt = turned_order(goutt, pos2, count)
    attn_other, in_far, gout, acc = lax.optimization_barrier((attn_two[1], in_far, gout, acc))
    in_two = (in_far, swap(in_far, "dp", 1))
    attn_two = (attn_far, attn_other)
    attn_three = tuple(swap(piece, "mp", 1) for piece in attn_two)
    first, mid, midt, s3, p3, s2, p2 = run_attn_two(
        pos, low, x, acc, vectors, attn_three, attn_two, count
    )
    midt = turned_order(midt, pos, count)
    y, dm, gi1, gd1 = run_ffn_near(mid, midt, gout, goutt, in_one, down_one)
    gi1, gd1, y, down_far, _ = lax.optimization_barrier((gi1, gd1, y, down_far, in_two[1]))
    down_two = (down_far, swap(down_far, "dp", 1))
    y, dm, gi0, gd0 = run_ffn_near(mid, midt, gout, goutt, in_weight, down_weight, y, dm)
    in_near, down_near = meet(gi0, gi1), meet(gd0, gd1)
    y, down_other, in_sent, down_sent = lax.optimization_barrier(
        (y, down_two[1], upper(in_near), upper(down_near))
    )
    in_near, down_near = fold(in_near, order1[0], in_sent), fold(down_near, order2[0], down_sent)
    down_two = (down_far, down_other)
    in_three, down_three = (
        tuple(swap(piece, "mp", 1) for piece in pieces) for pieces in (in_two, down_two)
    )
    y, dm, gi3, gd3 = run_ffn_far(low, mid, midt, gout, goutt, in_three, down_three, y, dm)
    out_rows, gfirst, gfl, gft, sums_b, gi2, gd2 = run_ffn_last(
        pos, low, image_weight, mid, midt, gout, goutt, in_two, down_two,
        y, dm, first, cotangent, vectors, count,
    )
    gft = turned_order(gft, pos, count)
    in_far, down_far = meet(gi2, gi3), meet(gd2, gd3)
    gfl, in_sent, down_sent, _, _ = lax.optimization_barrier(
        (gfl, upper(in_far), upper(down_far), in_near[-1], down_near[-1])
    )
    in_far, down_far = fold(in_far, order1[0], in_sent), fold(down_far, order2[0], down_sent)
    gin, ga3 = run_back_far(low, gfl, xt, gft, attn_three, (s3, p3))
    gin, ga2 = run_back_far(low, gfl, xt, gft, attn_two, (s2, p2), gin)
    far = meet(ga2, ga3)
    gin, far_sent, in_sent, down_sent = lax.optimization_barrier(
        (gin, upper(far), total(in_far).astype(BF16), total(down_far).astype(BF16))
    )
    far = fold(far, order1[0], far_sent)
    in_grad, down_grad = join(in_near, None, in_sent), join(down_near, None, down_sent)
    gin, ga1 = run_back_near(gfl, xt, gft, attn_one, (s1, p1), gin)
    input_grad, sums_a, ga0 = run_back_last(
        gfl, xt, gft, attn_w, (s0, p0), gin, rows, gfirst, vectors
    )
    near = meet(ga0, ga1)
    near = fold(near, order1[0])
    far = fold(far, order1[1])
    in_grad = fold(in_grad, order1[1])
    near = fold(near, order1[1])
    down_grad = fold(down_grad, order2[1])
    near = near + (swap(total(far).astype(BF16), "mp", 2),)
    for bit in order1[2:]:
        in_grad, down_grad = fold(in_grad, bit), fold(down_grad, bit)
        near = fold(near, bit)
    both = total(near)
    in_grad, down_grad = total(in_grad), total(down_grad)

    down_state = (down_master.T, down_first.T, down_second.T)
    in_fn, in_sn, in_up, down_fn, down_sn, down_up, squares = run_dense_step(
        (in_grad, in_master, in_first, in_second), (down_grad,) + down_state
    )
    qkv_grad, qkv_fn, qkv_sn, qkv_up, out_grad, out_fn, out_sn, out_up, small = run_attn_step(
        both, (qkv_master, qkv_first, qkv_second), (out_master, out_first, out_second),
        sums_a, sums_b, squares,
    )
    new, vec_outs = run_final(
        all_sum(small), vectors, vec_first, vec_second,
        (qkv_master, out_master, in_master, down_state[0]), (qkv_up, out_up, in_up, down_up),
    )
    return (
        out_rows,
        input_grad,
        qkv_grad,
        out_grad,
        in_grad,
        down_grad.T,
        qkv_fn,
        qkv_sn,
        new[0],
        out_fn,
        out_sn,
        new[1],
        in_fn,
        in_sn,
        new[2],
        down_fn.T,
        down_sn.T,
        new[3].T,
    ) + tuple(vec_outs)


def solution(mesh):
    rows = P(("dp", "mp"), None)
    qkv_state = P(None, "dp", "mp")
    out_state = P("mp", "dp")
    in_state = P("dp", "mp")
    in_specs = (
        (rows, rows, P(("dp", "mp")), P(None, None, "mp"), P("mp", None), P(None, "mp"), P("mp", None), P())
        + (qkv_state,) * 3
        + (out_state,) * 3
        + (in_state,) * 3
        + (out_state,) * 3
        + (P(), P())
    )
    out_specs = (
        (rows, rows, qkv_state, out_state, in_state, out_state)
        + (qkv_state,) * 3
        + (out_state,) * 3
        + (in_state,) * 3
        + (out_state,) * 3
        + (P(),) * 5
    )
    return jax.shard_map(shards, mesh=mesh, in_specs=in_specs, out_specs=out_specs, check_vma=False)
```
